32 devices in a mesh: groups: 2 (over y), tm: 8 (over z, x), cells: 2 (over core).
Axes of the slice: x: 2, y: 2, z: 4, core: 2. Of those that a mesh axis runs over, the one named last changes fastest.
Arguments:
- propagator: bfloat16 [272, 48, 4, 256], P(('groups', 'tm'), None, None, 'cells'), parts along dimension 0, as said below
- tile_blocks: int32 [272, 2], P(('groups', 'tm')), parts along dimension 0, may hold values from 0 to 15, as said below
- histories: bfloat16 [16, 12, 48], P('tm'), may hold values from -6 to 6
Outputs:
- concentration: float32 [32, 12, 4, 256], P(('groups', 'tm'), None, None, 'cells'), parts along dimension 0
The draws below stay inside these ranges and needn't reach their ends.
There are 2 independent parts, one for each index of `groups`. The reference program is written for one: setup_inputs(seed, part) draws one part's arguments, and reference() takes and returns one part's arrays. A program takes and returns all parts, laid end to end along the dimension named above; an argument that names none is the same for every part. Nothing has to cross between parts.
Inputs may be any that keep to these rules, and one draw needn't show every extreme that they name: `tile_blocks`: rows s * 17 to (s + 1) * 17 - 1 belong to two mirrored source blocks p and 15 - p, where p runs over a permutation of 0 to 7 from one such row group to the next; for each of the two source blocks every arrival block from it up to 15 appears in exactly one row, rows in any order. Tile n holds the propagator from source block tile_blocks[n, 0] to arrival block tile_blocks[n, 1].
All inputs are finite; a program needn't handle non-finite values.
Results may differ from the reference program's by a relative error of at most 0.0003.
Values may be sent and summed in bfloat16 or wider, within the bound.
No kernel may reach another device: no remote copies, remote signals or barrier semaphores. Data moves between devices by JAX's collectives and lax.ppermute only.
A program may use at most 64 MiB of HBM per device.

```python
import jax
import jax.numpy as jnp
from jax import lax

TR = 12
BM = 4
K = 48
NB = 16
CELLS = 256
N_TM = 8


def permute_slots(slot_key):
    return jax.random.permutation(slot_key, NB + 1)


def tile_layout(key):
    pair_count = NB // 2
    slot_count = NB + 1
    order = jax.random.permutation(jax.random.fold_in(key, 11), pair_count)
    index = jnp.arange(slot_count)[None, :]
    early = order[:, None]
    late = NB - 1 - early
    first_part = index < NB - early
    sources = jnp.where(first_part, early, late)
    arrivals = jnp.where(first_part, early + index, late + index - (NB - early))
    shuffle_keys = jax.random.split(jax.random.fold_in(key, 13), pair_count)
    shuffles = jax.vmap(permute_slots)(shuffle_keys)
    sources = jnp.take_along_axis(sources, shuffles, axis=1)
    arrivals = jnp.take_along_axis(arrivals, shuffles, axis=1)
    return (sources.reshape(-1).astype(jnp.int32), arrivals.reshape(-1).astype(jnp.int32))


def draw_tile_blocks(key, part):
    sources, arrivals = tile_layout(key)
    return jnp.stack([sources, arrivals], axis=1).astype(jnp.int32)


def draw_propagator(key, part):
    sources, arrivals = tile_layout(key)
    lag = (arrivals - sources).astype(jnp.float32)
    shape = (NB // 2 * (NB + 1), K, BM, CELLS)
    noise_key = jax.random.fold_in(key, 17)
    noise = jax.random.normal(noise_key, shape, jnp.float32)
    scale = (0.15 + jnp.exp(-lag / 4.0)) / jnp.sqrt(jnp.float32(K))
    return (noise * scale[:, None, None, None]).astype(jnp.bfloat16)


def level_of(key, extent, cuts, smallest, top_value):
    def one(dim, blocks):
        steps = jax.random.uniform(jax.random.fold_in(jax.random.fold_in(key, 6), dim), (blocks,), jnp.float32, smallest / len(cuts), top_value / len(cuts))
        return jnp.repeat(jnp.exp(steps), extent[dim] // blocks).reshape((-1,) + (1,) * (len(extent) - dim - 1))

    level = one(*cuts[0])
    for cut in cuts[1:]:
        level = level * one(*cut)
    return level


def scatter_about(rng, dims, scale, bound, pieces=(), dtype=jnp.bfloat16):
    drawn = scale * jax.random.normal(rng, dims, jnp.float32)
    if pieces:
        drawn = drawn * level_of(rng, dims, pieces, -0.22, 0.18)
    return jnp.clip(drawn, -bound, bound).astype(dtype)


def setup_inputs(seed: int = 0, part: int = 0) -> dict:
    keys = jax.random.split(jax.random.key(seed), 4)
    part_splits = jax.random.split(jax.random.fold_in(keys[3], part), 4)
    return {
        "propagator": draw_propagator(jax.random.fold_in(jax.random.fold_in(keys[3], part), 71), part),
        "tile_blocks": draw_tile_blocks(jax.random.fold_in(jax.random.fold_in(keys[3], part), 71), part),
        "histories": scatter_about(keys[2], (NB, TR, K), 1.0, 6.0, ((0, 8),)),
    }


def reference(propagator, tile_blocks, histories):
    slot_count = NB + 1
    tile_sets = propagator.reshape(N_TM, slot_count, K, BM * CELLS)
    block_sets = tile_blocks.reshape(N_TM, slot_count, 2)

    def accumulate(running, element):
        tile_group, block_pairs = element
        chosen = histories[block_pairs[:, 0]].astype(jnp.float32)
        contribution = jnp.einsum('nrk,nkm->nrm', chosen, tile_group.astype(jnp.float32))
        return running.at[block_pairs[:, 1]].add(contribution), None

    running = jnp.zeros((NB, TR, BM * CELLS), jnp.float32)
    running, unused = lax.scan(accumulate, running, (tile_sets, block_sets))
    return running.reshape(NB, TR, BM, CELLS)
```

```python
import jax
import jax.numpy as jnp
from jax import lax
from jax.sharding import PartitionSpec as P


def shards(propagator, tile_blocks, histories):
    group_count = lax.axis_size("tm")
    own_blocks, tracers, width = histories.shape
    copies = jnp.broadcast_to(histories[None], (group_count, own_blocks, tracers, width))
    all_histories = lax.all_to_all(copies, "tm", 0, 0, tiled=True)
    all_histories = all_histories.reshape(group_count * own_blocks, tracers, width)
    block_count = all_histories.shape[0]
    tracer_count = all_histories.shape[1]
    slot_count, source_width, months, cell_count = propagator.shape
    tile_rows = propagator.reshape(slot_count, source_width, months * cell_count)
    sources = tile_blocks[:, 0]
    arrivals = tile_blocks[:, 1]
    selector = (sources[:, None] == jnp.arange(block_count, dtype=jnp.int32)[None, :]).astype(
        jnp.bfloat16
    )
    chosen = jnp.dot(
        selector,
        all_histories.reshape(block_count, tracer_count * source_width),
        preferred_element_type=jnp.float32,
    )
    chosen = chosen.astype(jnp.bfloat16).reshape(slot_count, tracer_count, source_width)
    contribution = jnp.einsum("nrk,nkm->nrm", chosen, tile_rows, preferred_element_type=jnp.float32)
    partial_sums = (
        jnp.zeros((block_count, tracer_count, months * cell_count), jnp.float32)
        .at[arrivals]
        .add(contribution)
    )
    exchanged = lax.all_to_all(partial_sums, "tm", 0, 0, tiled=True)
    owned = exchanged.reshape(group_count, own_blocks, tracer_count, months * cell_count).sum(0)
    return owned.reshape(owned.shape[0], tracer_count, months, cell_count)


def solution(mesh):
    in_specs = (
        P(("groups", "tm"), None, None, "cells"),
        P(("groups", "tm"), None),
        P("tm", None, None),
    )
    out_specs = P(("groups", "tm"), None, None, "cells")
    return jax.shard_map(shards, mesh=mesh, in_specs=in_specs, out_specs=out_specs, check_vma=False)
```

```python
import jax
import jax.numpy as jnp
from jax import lax
from jax.sharding import PartitionSpec as P


def swap(value, step, size):
    return lax.ppermute(value, "tm", [(i, i ^ step) for i in range(size)])


def shards(propagator, tile_blocks, histories):
    size = lax.axis_size("tm")
    me = lax.axis_index("tm")
    own_blocks, tracer_count, source_width = histories.shape
    block_count = size * own_blocks
    slot_count, source_width, months, cell_count = propagator.shape

    parts = [histories] + [swap(histories, step, size) for step in range(1, size)]
    all_histories = jnp.stack(parts).reshape(block_count, tracer_count * source_width)

    tile_rows = propagator.reshape(slot_count, source_width, months * cell_count)
    owners = tile_blocks // own_blocks
    relative = (owners ^ me) * own_blocks + tile_blocks % own_blocks
    sources = relative[:, 0]
    arrivals = relative[:, 1]
    selector = (sources[:, None] == jnp.arange(block_count, dtype=jnp.int32)[None, :]).astype(
        jnp.bfloat16
    )
    chosen = jnp.dot(selector, all_histories, preferred_element_type=jnp.float32)
    chosen = chosen.astype(jnp.bfloat16).reshape(slot_count, tracer_count, source_width)
    contribution = jnp.einsum("nrk,nkm->nrm", chosen, tile_rows, preferred_element_type=jnp.float32)
    partial_sums = (
        jnp.zeros((block_count, tracer_count, months * cell_count), jnp.float32)
        .at[arrivals]
        .add(contribution)
    )
    pieces = partial_sums.reshape(size, own_blocks, tracer_count, months * cell_count)
    owned = pieces[0]
    for part in [swap(pieces[step], step, size) for step in range(1, size)]:
        owned = owned + part
    return owned.reshape(own_blocks, tracer_count, months, cell_count)


def solution(mesh):
    in_specs = (
        P(("groups", "tm"), None, None, "cells"),
        P(("groups", "tm"), None),
        P("tm", None, None),
    )
    out_specs = P(("groups", "tm"), None, None, "cells")
    return jax.shard_map(shards, mesh=mesh, in_specs=in_specs, out_specs=out_specs, check_vma=False)
```

```python
import jax
import jax.numpy as jnp
from jax import lax
from jax.experimental import pallas as pl
from jax.experimental.pallas import tpu as pltpu
from jax.sharding import PartitionSpec as P


def tile_sums(months, blocks_ref, histories_ref, tiles_ref, sums_ref, wide_ref):
    size, packed_rows, packed_width = histories_ref.shape
    slot_count, tile_height, cell_count = tiles_ref.shape
    block_count, height, cell_count = sums_ref.shape
    own_blocks = block_count // size

    first = blocks_ref[0, 0]
    row_of = lax.broadcasted_iota(jnp.int32, (height, packed_rows), 0) // months * own_blocks
    packed_row = lax.broadcasted_iota(jnp.int32, (height, packed_rows), 1)
    column_of = lax.broadcasted_iota(jnp.int32, (packed_width, tile_height), 1) // months
    packed_column = lax.broadcasted_iota(jnp.int32, (packed_width, tile_height), 0)
    repeat_columns = (column_of == packed_column).astype(jnp.bfloat16)
    month_of_row = lax.broadcasted_iota(jnp.int32, (height, tile_height), 0) % months
    month_of_column = lax.broadcasted_iota(jnp.int32, (height, tile_height), 1) % months
    same_month = month_of_row == month_of_column
    for which, source in enumerate((first, block_count - 1 - first)):
        repeat_rows = (row_of + source % own_blocks == packed_row).astype(jnp.bfloat16)
        tall = jnp.dot(
            repeat_rows, histories_ref[source // own_blocks], preferred_element_type=jnp.float32
        )
        wide = jnp.dot(tall.astype(jnp.bfloat16), repeat_columns, preferred_element_type=jnp.float32)
        wide_ref[which] = jnp.where(same_month, wide, 0.0).astype(jnp.bfloat16)

    sums_ref[...] = jnp.zeros(sums_ref.shape, sums_ref.dtype)

    def add_tile(slot):
        which = (blocks_ref[0, slot] != first).astype(jnp.int32)
        arrival = blocks_ref[1, slot]
        sums_ref[arrival] += jnp.dot(wide_ref[which], tiles_ref[slot], preferred_element_type=jnp.float32)

    unrolled = 17
    rounds = slot_count // unrolled

    def add_round(turn, carry):
        for step in range(unrolled):
            add_tile(turn * unrolled + step)
        return carry

    if rounds == 1:
        add_round(0, 0)
    else:
        lax.fori_loop(0, rounds, add_round, 0)
    for slot in range(rounds * unrolled, slot_count):
        add_tile(slot)


def shards(propagator, tile_blocks, histories):
    size = lax.axis_size("tm")
    own_blocks, tracer_count, source_width = histories.shape
    slot_count, source_width, months, cell_count = propagator.shape
    block_count = size * own_blocks
    height = tracer_count * months

    used_rows = tracer_count * own_blocks
    packed = jnp.pad(
        jnp.swapaxes(histories, 0, 1).reshape(used_rows, source_width),
        ((0, -used_rows % 16), (0, -source_width % 128)),
    )
    copies = jnp.broadcast_to(packed[None], (size,) + packed.shape)
    received = lax.all_to_all(copies, "tm", 0, 0, tiled=True)

    tiles = propagator.reshape(slot_count, source_width * months, cell_count)
    vmem = pl.BlockSpec(memory_space=pltpu.VMEM)
    partial_sums = pl.pallas_call(
        lambda *refs: tile_sums(months, *refs),
        out_shape=jax.ShapeDtypeStruct((block_count, height, cell_count), jnp.float32),
        in_specs=[pl.BlockSpec(memory_space=pltpu.SMEM), vmem, vmem],
        out_specs=vmem,
        scratch_shapes=[pltpu.VMEM((2, height, source_width * months), jnp.bfloat16)],
        compiler_params=pltpu.CompilerParams(vmem_limit_bytes=32 * 1024 * 1024),
        cost_estimate=pl.CostEstimate(
            flops=2 * slot_count * height * source_width * months * cell_count,
            bytes_accessed=propagator.size * 2 + block_count * height * cell_count * 4,
            transcendentals=0,
        ),
    )(tile_blocks.T, received, tiles)

    exchanged = lax.all_to_all(partial_sums, "tm", 0, 0, tiled=True)
    owned = exchanged.reshape(size, own_blocks, height, cell_count).sum(0)
    return owned.reshape(own_blocks, tracer_count, months, cell_count)


def solution(mesh):
    in_specs = (
        P(("groups", "tm"), None, None, "cells"),
        P(("groups", "tm"), None),
        P("tm", None, None),
    )
    out_specs = P(("groups", "tm"), None, None, "cells")
    return jax.shard_map(shards, mesh=mesh, in_specs=in_specs, out_specs=out_specs, check_vma=False)
```

```python
import jax
import jax.numpy as jnp
from jax import lax
from jax.experimental import pallas as pl
from jax.experimental.pallas import tpu as pltpu
from jax.sharding import PartitionSpec as P


def tile_sums(months, me_ref, blocks_ref, histories_ref, tiles_ref, sums_ref, wide_ref):
    size, packed_rows, packed_width = histories_ref.shape
    me = me_ref[0]
    slot_count, tile_height, cell_count = tiles_ref.shape
    block_count, height, cell_count = sums_ref.shape
    own_blocks = block_count // size

    first = blocks_ref[0, 0]
    row_of = lax.broadcasted_iota(jnp.int32, (height, packed_rows), 0) // months * own_blocks
    packed_row = lax.broadcasted_iota(jnp.int32, (height, packed_rows), 1)
    column_of = lax.broadcasted_iota(jnp.int32, (packed_width, tile_height), 1) // months
    packed_column = lax.broadcasted_iota(jnp.int32, (packed_width, tile_height), 0)
    repeat_columns = (column_of == packed_column).astype(jnp.bfloat16)
    month_of_row = lax.broadcasted_iota(jnp.int32, (height, tile_height), 0) % months
    month_of_column = lax.broadcasted_iota(jnp.int32, (height, tile_height), 1) % months
    same_month = month_of_row == month_of_column
    for which, source in enumerate((first, block_count - 1 - first)):
        repeat_rows = (row_of + source % own_blocks == packed_row).astype(jnp.bfloat16)
        tall = jnp.dot(
            repeat_rows, histories_ref[(source // own_blocks) ^ me], preferred_element_type=jnp.float32
        )
        wide = jnp.dot(tall.astype(jnp.bfloat16), repeat_columns, preferred_element_type=jnp.float32)
        wide_ref[which] = jnp.where(same_month, wide, 0.0).astype(jnp.bfloat16)

    sums_ref[...] = jnp.zeros(sums_ref.shape, sums_ref.dtype)

    def add_tile(slot):
        which = (blocks_ref[0, slot] != first).astype(jnp.int32)
        arrival = blocks_ref[1, slot]
        sums_ref[arrival] += jnp.dot(wide_ref[which], tiles_ref[slot], preferred_element_type=jnp.float32)

    unrolled = 17
    rounds = slot_count // unrolled

    def add_round(turn, carry):
        for step in range(unrolled):
            add_tile(turn * unrolled + step)
        return carry

    if rounds == 1:
        add_round(0, 0)
    else:
        lax.fori_loop(0, rounds, add_round, 0)
    for slot in range(rounds * unrolled, slot_count):
        add_tile(slot)


def stage(blocks_in, tiles_in, blocks_out, tiles_out, semaphores):
    copies = [
        pltpu.make_async_copy(blocks_in, blocks_out, semaphores.at[0]),
        pltpu.make_async_copy(tiles_in, tiles_out, semaphores.at[1]),
    ]
    for copy in copies:
        copy.start()
    for copy in copies:
        copy.wait()


def swap(value, step, size):
    return lax.ppermute(value, "tm", [(i, i ^ step) for i in range(size)])


def shards(propagator, tile_blocks, histories):
    size = lax.axis_size("tm")
    own_blocks, tracer_count, source_width = histories.shape
    slot_count, source_width, months, cell_count = propagator.shape
    block_count = size * own_blocks
    height = tracer_count * months

    used_rows = tracer_count * own_blocks
    tail = ((0, 0), (0, -used_rows % 16), (0, -source_width % 128))
    held = jnp.swapaxes(histories, 0, 1).reshape(1, used_rows, source_width)

    step = 1
    while step < size:
        held = jnp.concatenate([held, swap(held, step, size)])
        step *= 2
    received = jnp.pad(held, tail)

    tiles = propagator.reshape(slot_count, source_width * months, cell_count)
    blocks = tile_blocks.T
    vmem = pl.BlockSpec(memory_space=pltpu.VMEM)
    smem = pl.BlockSpec(memory_space=pltpu.SMEM)
    hbm = pl.BlockSpec(memory_space=pltpu.HBM)
    blocks, tiles = pl.pallas_call(
        stage,
        out_shape=[
            jax.ShapeDtypeStruct(blocks.shape, blocks.dtype),
            jax.ShapeDtypeStruct(tiles.shape, tiles.dtype),
        ],
        in_specs=[hbm, hbm],
        out_specs=[vmem, vmem],
        scratch_shapes=[pltpu.SemaphoreType.DMA((2,))],
        compiler_params=pltpu.CompilerParams(vmem_limit_bytes=16 * 1024 * 1024),
        cost_estimate=pl.CostEstimate(flops=0, bytes_accessed=propagator.size * 4, transcendentals=0),
    )(blocks, tiles)
    me = lax.axis_index("tm").astype(jnp.int32)[None]
    partial_sums = pl.pallas_call(
        lambda *refs: tile_sums(months, *refs),
        out_shape=jax.ShapeDtypeStruct((block_count, height, cell_count), jnp.float32),
        in_specs=[smem, smem, vmem, vmem],
        out_specs=vmem,
        scratch_shapes=[pltpu.VMEM((2, height, source_width * months), jnp.bfloat16)],
        compiler_params=pltpu.CompilerParams(vmem_limit_bytes=32 * 1024 * 1024),
        cost_estimate=pl.CostEstimate(
            flops=2 * slot_count * height * source_width * months * cell_count,
            bytes_accessed=propagator.size * 2 + block_count * height * cell_count * 4,
            transcendentals=0,
        ),
    )(me, blocks, received, tiles)

    exchanged = lax.all_to_all(partial_sums, "tm", 0, 0, tiled=True)
    owned = exchanged.reshape(size, own_blocks, height, cell_count).sum(0)
    return owned.reshape(own_blocks, tracer_count, months, cell_count)


def solution(mesh):
    in_specs = (
        P(("groups", "tm"), None, None, "cells"),
        P(("groups", "tm"), None),
        P("tm", None, None),
    )
    out_specs = P(("groups", "tm"), None, None, "cells")
    return jax.shard_map(shards, mesh=mesh, in_specs=in_specs, out_specs=out_specs, check_vma=False)
```

```python
import jax
import jax.numpy as jnp
from jax import lax
from jax.experimental import pallas as pl
from jax.experimental.pallas import tpu as pltpu
from jax.sharding import PartitionSpec as P


def tile_sums(months, blocks_ref, histories_ref, tiles_ref, sums_ref, wide_ref):
    size, packed_rows, packed_width = histories_ref.shape
    slot_count, tile_height, cell_count = tiles_ref.shape
    block_count, height, cell_count = sums_ref.shape
    own_blocks = block_count // size

    first = blocks_ref[0, 0]
    row_of = lax.broadcasted_iota(jnp.int32, (height, packed_rows), 0) // months * own_blocks
    packed_row = lax.broadcasted_iota(jnp.int32, (height, packed_rows), 1)
    column_of = lax.broadcasted_iota(jnp.int32, (packed_width, tile_height), 1) // months
    packed_column = lax.broadcasted_iota(jnp.int32, (packed_width, tile_height), 0)
    repeat_columns = (column_of == packed_column).astype(jnp.bfloat16)
    month_of_row = lax.broadcasted_iota(jnp.int32, (height, tile_height), 0) % months
    month_of_column = lax.broadcasted_iota(jnp.int32, (height, tile_height), 1) % months
    same_month = month_of_row == month_of_column
    for which, source in enumerate((first, block_count - 1 - first)):
        repeat_rows = (row_of + source % own_blocks == packed_row).astype(jnp.bfloat16)
        tall = jnp.dot(
            repeat_rows, histories_ref[source // own_blocks], preferred_element_type=jnp.float32
        )
        wide = jnp.dot(tall.astype(jnp.bfloat16), repeat_columns, preferred_element_type=jnp.float32)
        wide_ref[which] = jnp.where(same_month, wide, 0.0).astype(jnp.bfloat16)

    sums_ref[...] = jnp.zeros(sums_ref.shape, sums_ref.dtype)

    def add_tile(slot):
        which = (blocks_ref[0, slot] != first).astype(jnp.int32)
        arrival = blocks_ref[1, slot]
        sums_ref[arrival] += jnp.dot(wide_ref[which], tiles_ref[slot], preferred_element_type=jnp.float32)

    unrolled = 17
    rounds = slot_count // unrolled

    def add_round(turn, carry):
        for step in range(unrolled):
            add_tile(turn * unrolled + step)
        return carry

    if rounds == 1:
        add_round(0, 0)
    else:
        lax.fori_loop(0, rounds, add_round, 0)
    for slot in range(rounds * unrolled, slot_count):
        add_tile(slot)


def stage(blocks_in, tiles_in, blocks_out, tiles_out, semaphores):
    copies = [
        pltpu.make_async_copy(blocks_in, blocks_out, semaphores.at[0]),
        pltpu.make_async_copy(tiles_in, tiles_out, semaphores.at[1]),
    ]
    for copy in copies:
        copy.start()
    for copy in copies:
        copy.wait()


def shards(propagator, tile_blocks, histories):
    size = lax.axis_size("tm")
    own_blocks, tracer_count, source_width = histories.shape
    slot_count, source_width, months, cell_count = propagator.shape
    block_count = size * own_blocks
    height = tracer_count * months

    used_rows = tracer_count * own_blocks
    packed = jnp.pad(
        jnp.swapaxes(histories, 0, 1).reshape(used_rows, source_width),
        ((0, -used_rows % 16), (0, -source_width % 128)),
    )
    copies = jnp.broadcast_to(packed[None], (size,) + packed.shape)
    received = lax.all_to_all(copies, "tm", 0, 0, tiled=True)

    tiles = propagator.reshape(slot_count, source_width * months, cell_count)
    blocks = tile_blocks.T
    vmem = pl.BlockSpec(memory_space=pltpu.VMEM)
    smem = pl.BlockSpec(memory_space=pltpu.SMEM)
    hbm = pl.BlockSpec(memory_space=pltpu.HBM)
    blocks, tiles = pl.pallas_call(
        stage,
        out_shape=[
            jax.ShapeDtypeStruct(blocks.shape, blocks.dtype),
            jax.ShapeDtypeStruct(tiles.shape, tiles.dtype),
        ],
        in_specs=[hbm, hbm],
        out_specs=[vmem, vmem],
        scratch_shapes=[pltpu.SemaphoreType.DMA((2,))],
        compiler_params=pltpu.CompilerParams(vmem_limit_bytes=16 * 1024 * 1024),
        cost_estimate=pl.CostEstimate(flops=0, bytes_accessed=propagator.size * 4, transcendentals=0),
    )(blocks, tiles)
    partial_sums = pl.pallas_call(
        lambda *refs: tile_sums(months, *refs),
        out_shape=jax.ShapeDtypeStruct((block_count, height, cell_count), jnp.float32),
        in_specs=[smem, vmem, vmem],
        out_specs=vmem,
        scratch_shapes=[pltpu.VMEM((2, height, source_width * months), jnp.bfloat16)],
        compiler_params=pltpu.CompilerParams(vmem_limit_bytes=32 * 1024 * 1024),
        cost_estimate=pl.CostEstimate(
            flops=2 * slot_count * height * source_width * months * cell_count,
            bytes_accessed=propagator.size * 2 + block_count * height * cell_count * 4,
            transcendentals=0,
        ),
    )(blocks, received, tiles)

    exchanged = lax.all_to_all(partial_sums, "tm", 0, 0, tiled=True)
    owned = exchanged.reshape(size, own_blocks, height, cell_count).sum(0)
    return owned.reshape(own_blocks, tracer_count, months, cell_count)


def solution(mesh):
    in_specs = (
        P(("groups", "tm"), None, None, "cells"),
        P(("groups", "tm"), None),
        P("tm", None, None),
    )
    out_specs = P(("groups", "tm"), None, None, "cells")
    return jax.shard_map(shards, mesh=mesh, in_specs=in_specs, out_specs=out_specs, check_vma=False)
```

```python
import jax
import jax.numpy as jnp
from jax import lax
from jax.experimental import pallas as pl
from jax.experimental.pallas import tpu as pltpu
from jax.sharding import PartitionSpec as P


def tile_sums(months, blocks_ref, histories_ref, tiles_ref, sums_ref, wide_ref):
    size, packed_rows, packed_width = histories_ref.shape
    slot_count, tile_height, cell_count = tiles_ref.shape
    block_count, height, cell_count = sums_ref.shape
    own_blocks = block_count // size

    first = blocks_ref[0, 0]
    row_of = lax.broadcasted_iota(jnp.int32, (height, packed_rows), 0) // months * own_blocks
    packed_row = lax.broadcasted_iota(jnp.int32, (height, packed_rows), 1)
    column_of = lax.broadcasted_iota(jnp.int32, (packed_width, tile_height), 1) // months
    packed_column = lax.broadcasted_iota(jnp.int32, (packed_width, tile_height), 0)
    repeat_columns = (column_of == packed_column).astype(jnp.bfloat16)
    month_of_row = lax.broadcasted_iota(jnp.int32, (height, tile_height), 0) % months
    month_of_column = lax.broadcasted_iota(jnp.int32, (height, tile_height), 1) % months
    same_month = month_of_row == month_of_column
    for which, source in enumerate((first, block_count - 1 - first)):
        repeat_rows = (row_of + source % own_blocks == packed_row).astype(jnp.bfloat16)
        tall = jnp.dot(
            repeat_rows, histories_ref[size - 1 - source // own_blocks], preferred_element_type=jnp.float32
        )
        wide = jnp.dot(tall.astype(jnp.bfloat16), repeat_columns, preferred_element_type=jnp.float32)
        wide_ref[which] = jnp.where(same_month, wide, 0.0).astype(jnp.bfloat16)

    sums_ref[...] = jnp.zeros(sums_ref.shape, sums_ref.dtype)

    def add_tile(slot):
        which = (blocks_ref[0, slot] != first).astype(jnp.int32)
        arrival = blocks_ref[1, slot]
        place = (size - 1 - arrival // own_blocks) * own_blocks + arrival % own_blocks
        sums_ref[place] += jnp.dot(wide_ref[which], tiles_ref[slot], preferred_element_type=jnp.float32)

    unrolled = 17
    rounds = slot_count // unrolled

    def add_round(turn, carry):
        for step in range(unrolled):
            add_tile(turn * unrolled + step)
        return carry

    if rounds == 1:
        add_round(0, 0)
    else:
        lax.fori_loop(0, rounds, add_round, 0)
    for slot in range(rounds * unrolled, slot_count):
        add_tile(slot)


def stage(blocks_in, tiles_in, blocks_out, tiles_out, semaphores):
    copies = [
        pltpu.make_async_copy(blocks_in, blocks_out, semaphores.at[0]),
        pltpu.make_async_copy(tiles_in, tiles_out, semaphores.at[1]),
    ]
    for copy in copies:
        copy.start()
    for copy in copies:
        copy.wait()


def exchange(value, size):
    return lax.all_to_all(
        value, "tm", 0, 0, axis_index_groups=[list(range(size - 1, -1, -1))], tiled=True
    )


def shards(propagator, tile_blocks, histories):
    size = lax.axis_size("tm")
    own_blocks, tracer_count, source_width = histories.shape
    slot_count, source_width, months, cell_count = propagator.shape
    block_count = size * own_blocks
    height = tracer_count * months

    used_rows = tracer_count * own_blocks
    rows = jnp.swapaxes(histories, 0, 1).reshape(1, used_rows, source_width)
    copies = jnp.pad(
        jnp.broadcast_to(rows, (size, used_rows, source_width)),
        ((0, 0), (0, -used_rows % 16), (0, -source_width % 128)),
    )
    received = exchange(copies, size)

    tiles = propagator.reshape(slot_count, source_width * months, cell_count)
    blocks = tile_blocks.T
    vmem = pl.BlockSpec(memory_space=pltpu.VMEM)
    smem = pl.BlockSpec(memory_space=pltpu.SMEM)
    hbm = pl.BlockSpec(memory_space=pltpu.HBM)
    blocks, tiles = pl.pallas_call(
        stage,
        out_shape=[
            jax.ShapeDtypeStruct(blocks.shape, blocks.dtype),
            jax.ShapeDtypeStruct(tiles.shape, tiles.dtype),
        ],
        in_specs=[hbm, hbm],
        out_specs=[vmem, vmem],
        scratch_shapes=[pltpu.SemaphoreType.DMA((2,))],
        compiler_params=pltpu.CompilerParams(vmem_limit_bytes=16 * 1024 * 1024),
        cost_estimate=pl.CostEstimate(flops=0, bytes_accessed=propagator.size * 4, transcendentals=0),
    )(blocks, tiles)
    partial_sums = pl.pallas_call(
        lambda *refs: tile_sums(months, *refs),
        out_shape=jax.ShapeDtypeStruct((block_count, height, cell_count), jnp.float32),
        in_specs=[smem, vmem, vmem],
        out_specs=vmem,
        scratch_shapes=[pltpu.VMEM((2, height, source_width * months), jnp.bfloat16)],
        compiler_params=pltpu.CompilerParams(vmem_limit_bytes=32 * 1024 * 1024),
        cost_estimate=pl.CostEstimate(
            flops=2 * slot_count * height * source_width * months * cell_count,
            bytes_accessed=propagator.size * 2 + block_count * height * cell_count * 4,
            transcendentals=0,
        ),
    )(blocks, received, tiles)

    exchanged = exchange(partial_sums, size)
    owned = exchanged.reshape(size, own_blocks, height, cell_count).sum(0)
    return owned.reshape(own_blocks, tracer_count, months, cell_count)


def solution(mesh):
    in_specs = (
        P(("groups", "tm"), None, None, "cells"),
        P(("groups", "tm"), None),
        P("tm", None, None),
    )
    out_specs = P(("groups", "tm"), None, None, "cells")
    return jax.shard_map(shards, mesh=mesh, in_specs=in_specs, out_specs=out_specs, check_vma=False)
```

```python
import jax
import jax.numpy as jnp
from jax import lax
from jax.experimental import pallas as pl
from jax.experimental.pallas import tpu as pltpu
from jax.sharding import PartitionSpec as P


def tile_sums(months, blocks_ref, histories_ref, tiles_ref, sums_ref, wide_ref):
    size, packed_rows, packed_width = histories_ref.shape
    slot_count, tile_height, cell_count = tiles_ref.shape
    block_count, height, cell_count = sums_ref.shape
    own_blocks = block_count // size

    first = blocks_ref[0, 0]
    row_of = lax.broadcasted_iota(jnp.int32, (height, packed_rows), 0) // months * own_blocks
    packed_row = lax.broadcasted_iota(jnp.int32, (height, packed_rows), 1)
    column_of = lax.broadcasted_iota(jnp.int32, (packed_width, tile_height), 1) // months
    packed_column = lax.broadcasted_iota(jnp.int32, (packed_width, tile_height), 0)
    repeat_columns = (column_of == packed_column).astype(jnp.bfloat16)
    month_of_row = lax.broadcasted_iota(jnp.int32, (height, tile_height), 0) % months
    month_of_column = lax.broadcasted_iota(jnp.int32, (height, tile_height), 1) % months
    same_month = month_of_row == month_of_column
    for which, source in enumerate((first, block_count - 1 - first)):
        repeat_rows = (row_of + source % own_blocks == packed_row).astype(jnp.bfloat16)
        tall = jnp.dot(
            repeat_rows, histories_ref[size - 1 - source // own_blocks], preferred_element_type=jnp.float32
        )
        wide = jnp.dot(tall.astype(jnp.bfloat16), repeat_columns, preferred_element_type=jnp.float32)
        wide_ref[which] = jnp.where(same_month, wide, 0.0).astype(jnp.bfloat16)

    sums_ref[...] = jnp.zeros(sums_ref.shape, sums_ref.dtype)

    def add_tile(slot):
        which = (blocks_ref[0, slot] != first).astype(jnp.int32)
        arrival = blocks_ref[1, slot]
        sums_ref[arrival] += jnp.dot(wide_ref[which], tiles_ref[slot], preferred_element_type=jnp.float32)

    unrolled = 17
    rounds = slot_count // unrolled

    def add_round(turn, carry):
        for step in range(unrolled):
            add_tile(turn * unrolled + step)
        return carry

    if rounds == 1:
        add_round(0, 0)
    else:
        lax.fori_loop(0, rounds, add_round, 0)
    for slot in range(rounds * unrolled, slot_count):
        add_tile(slot)


def stage(blocks_in, tiles_in, blocks_out, tiles_out, semaphores):
    copies = [
        pltpu.make_async_copy(blocks_in, blocks_out, semaphores.at[0]),
        pltpu.make_async_copy(tiles_in, tiles_out, semaphores.at[1]),
    ]
    for copy in copies:
        copy.start()
    for copy in copies:
        copy.wait()


def shards(propagator, tile_blocks, histories):
    size = lax.axis_size("tm")
    own_blocks, tracer_count, source_width = histories.shape
    slot_count, source_width, months, cell_count = propagator.shape
    block_count = size * own_blocks
    height = tracer_count * months

    used_rows = tracer_count * own_blocks
    rows = jnp.swapaxes(histories, 0, 1).reshape(1, used_rows, source_width)
    copies = jnp.broadcast_to(rows, (size, used_rows, source_width))
    reverse = [list(range(size - 1, -1, -1))]
    received = lax.all_to_all(copies, "tm", 0, 0, axis_index_groups=reverse, tiled=True)

    tiles = propagator.reshape(slot_count, source_width * months, cell_count)
    blocks = tile_blocks.T
    vmem = pl.BlockSpec(memory_space=pltpu.VMEM)
    smem = pl.BlockSpec(memory_space=pltpu.SMEM)
    hbm = pl.BlockSpec(memory_space=pltpu.HBM)
    blocks, tiles = pl.pallas_call(
        stage,
        out_shape=[
            jax.ShapeDtypeStruct(blocks.shape, blocks.dtype),
            jax.ShapeDtypeStruct(tiles.shape, tiles.dtype),
        ],
        in_specs=[hbm, hbm],
        out_specs=[vmem, vmem],
        scratch_shapes=[pltpu.SemaphoreType.DMA((2,))],
        compiler_params=pltpu.CompilerParams(vmem_limit_bytes=16 * 1024 * 1024),
        cost_estimate=pl.CostEstimate(flops=0, bytes_accessed=propagator.size * 4, transcendentals=0),
    )(blocks, tiles)
    partial_sums = pl.pallas_call(
        lambda *refs: tile_sums(months, *refs),
        out_shape=jax.ShapeDtypeStruct((block_count, height, cell_count), jnp.float32),
        in_specs=[smem, vmem, vmem],
        out_specs=vmem,
        scratch_shapes=[pltpu.VMEM((2, height, source_width * months), jnp.bfloat16)],
        compiler_params=pltpu.CompilerParams(vmem_limit_bytes=32 * 1024 * 1024),
        cost_estimate=pl.CostEstimate(
            flops=2 * slot_count * height * source_width * months * cell_count,
            bytes_accessed=propagator.size * 2 + block_count * height * cell_count * 4,
            transcendentals=0,
        ),
    )(blocks, received, tiles)

    exchanged = lax.all_to_all(partial_sums, "tm", 0, 0, tiled=True)
    owned = exchanged.reshape(size, own_blocks, height, cell_count).sum(0)
    return owned.reshape(own_blocks, tracer_count, months, cell_count)


def solution(mesh):
    in_specs = (
        P(("groups", "tm"), None, None, "cells"),
        P(("groups", "tm"), None),
        P("tm", None, None),
    )
    out_specs = P(("groups", "tm"), None, None, "cells")
    return jax.shard_map(shards, mesh=mesh, in_specs=in_specs, out_specs=out_specs, check_vma=False)
```

```python
import functools

import jax
import jax.numpy as jnp
from jax import lax
from jax.experimental import pallas as pl
from jax.experimental.pallas import tpu as pltpu
from jax.sharding import PartitionSpec as P

STEPS = 32700.0
LEVELS = 128
SMALLEST = 2.0**-126


def tile_sums(months, blocks_ref, histories_ref, tiles_ref, coded_ref, wide_ref, sums_ref):
    packed_rows, packed_width = histories_ref.shape[1:]
    slot_count, tile_height, cell_count = tiles_ref.shape
    block_count, height, cell_count = sums_ref.shape
    size = coded_ref.shape[0]
    own_blocks = block_count // size

    first = blocks_ref[0, 0]
    row_of = lax.broadcasted_iota(jnp.int32, (height, packed_rows), 0) // months * own_blocks
    packed_row = lax.broadcasted_iota(jnp.int32, (height, packed_rows), 1)
    column_of = lax.broadcasted_iota(jnp.int32, (packed_width, tile_height), 1) // months
    packed_column = lax.broadcasted_iota(jnp.int32, (packed_width, tile_height), 0)
    repeat_columns = (column_of == packed_column).astype(jnp.bfloat16)
    month_of_row = lax.broadcasted_iota(jnp.int32, (height, tile_height), 0) % months
    month_of_column = lax.broadcasted_iota(jnp.int32, (height, tile_height), 1) % months
    same_month = month_of_row == month_of_column
    for which, source in enumerate((first, block_count - 1 - first)):
        repeat_rows = (row_of + source % own_blocks == packed_row).astype(jnp.bfloat16)
        tall = jnp.dot(
            repeat_rows, histories_ref[size - 1 - source // own_blocks], preferred_element_type=jnp.float32
        )
        wide = jnp.dot(tall.astype(jnp.bfloat16), repeat_columns, preferred_element_type=jnp.float32)
        wide_ref[which] = jnp.where(same_month, wide, 0.0).astype(jnp.bfloat16)

    sums_ref[...] = jnp.zeros(sums_ref.shape, sums_ref.dtype)

    def add_tile(slot):
        which = (blocks_ref[0, slot] != first).astype(jnp.int32)
        arrival = blocks_ref[1, slot]
        place = (size - 1 - arrival // own_blocks) * own_blocks + arrival % own_blocks
        sums_ref[place] += jnp.dot(wide_ref[which], tiles_ref[slot], preferred_element_type=jnp.float32)

    unrolled = 17
    rounds = slot_count // unrolled

    def add_round(turn, carry):
        for step in range(unrolled):
            add_tile(turn * unrolled + step)
        return carry

    if rounds == 1:
        add_round(0, 0)
    else:
        lax.fori_loop(0, rounds, add_round, 0)
    for slot in range(rounds * unrolled, slot_count):
        add_tile(slot)

    coded_rows = own_blocks * height

    def code(slot, carry):
        blocks = [sums_ref[slot * own_blocks + block] for block in range(own_blocks)]
        top = jnp.max(functools.reduce(jnp.maximum, map(jnp.abs, blocks)), axis=0, keepdims=True)
        level = jnp.ceil(jnp.log2(jnp.maximum(top, SMALLEST)) * LEVELS)
        half = jnp.exp2(level * (-0.5 / LEVELS))
        for block, value in enumerate(blocks):
            steps = jnp.round(value * half * (half * STEPS))
            coded_ref[slot, pl.ds(block * height, height)] = steps.astype(jnp.int32).astype(jnp.int16)
        spread = jnp.broadcast_to(level.astype(jnp.int32), (16, cell_count))
        coded_ref[slot, pl.ds(coded_rows, 16)] = spread.astype(jnp.int16)
        return carry

    lax.fori_loop(0, size, code, 0, unroll=size <= 8)


def add_parts(coded_ref, total_ref):
    size = coded_ref.shape[0]
    own_blocks, height, cell_count = total_ref.shape
    coded_rows = own_blocks * height
    total_ref[...] = jnp.zeros(total_ref.shape, total_ref.dtype)

    def add(slot, carry):
        level = coded_ref[slot, pl.ds(coded_rows, 16)].astype(jnp.int32).astype(jnp.float32)[:1]
        half = jnp.exp2(level * (0.5 / LEVELS))
        for block in range(own_blocks):
            steps = coded_ref[slot, pl.ds(block * height, height)].astype(jnp.int32)
            total_ref[block] += steps.astype(jnp.float32) * (half * (1.0 / STEPS)) * half
        return carry

    lax.fori_loop(0, size, add, 0, unroll=size <= 8)


def stage(blocks_in, tiles_in, blocks_out, tiles_out, semaphores):
    copies = [
        pltpu.make_async_copy(blocks_in, blocks_out, semaphores.at[0]),
        pltpu.make_async_copy(tiles_in, tiles_out, semaphores.at[1]),
    ]
    for copy in copies:
        copy.start()
    for copy in copies:
        copy.wait()


def exchange(value, size):
    return lax.all_to_all(
        value, "tm", 0, 0, axis_index_groups=[list(range(size - 1, -1, -1))], tiled=True
    )


def shards(propagator, tile_blocks, histories):
    size = lax.axis_size("tm")
    own_blocks, tracer_count, source_width = histories.shape
    slot_count, source_width, months, cell_count = propagator.shape
    block_count = size * own_blocks
    height = tracer_count * months

    used_rows = tracer_count * own_blocks
    rows = jnp.swapaxes(histories, 0, 1).reshape(1, used_rows, source_width)
    copies = jnp.pad(
        jnp.broadcast_to(rows, (size, used_rows, source_width)),
        ((0, 0), (0, -used_rows % 16), (0, -source_width % 128)),
    )
    received = exchange(copies, size)

    tiles = propagator.reshape(slot_count, source_width * months, cell_count)
    blocks = tile_blocks.T
    vmem = pl.BlockSpec(memory_space=pltpu.VMEM)
    smem = pl.BlockSpec(memory_space=pltpu.SMEM)
    hbm = pl.BlockSpec(memory_space=pltpu.HBM)
    blocks, tiles = pl.pallas_call(
        stage,
        out_shape=[
            jax.ShapeDtypeStruct(blocks.shape, blocks.dtype),
            jax.ShapeDtypeStruct(tiles.shape, tiles.dtype),
        ],
        in_specs=[hbm, hbm],
        out_specs=[vmem, vmem],
        scratch_shapes=[pltpu.SemaphoreType.DMA((2,))],
        compiler_params=pltpu.CompilerParams(vmem_limit_bytes=16 * 1024 * 1024),
        cost_estimate=pl.CostEstimate(flops=0, bytes_accessed=propagator.size * 4, transcendentals=0),
    )(blocks, tiles)
    coded = pl.pallas_call(
        lambda *refs: tile_sums(months, *refs),
        out_shape=jax.ShapeDtypeStruct((size, own_blocks * height + 16, cell_count), jnp.int16),
        in_specs=[smem, vmem, vmem],
        out_specs=vmem,
        scratch_shapes=[
            pltpu.VMEM((2, height, source_width * months), jnp.bfloat16),
            pltpu.VMEM((block_count, height, cell_count), jnp.float32),
        ],
        compiler_params=pltpu.CompilerParams(vmem_limit_bytes=32 * 1024 * 1024),
        cost_estimate=pl.CostEstimate(
            flops=2 * slot_count * height * source_width * months * cell_count,
            bytes_accessed=propagator.size * 2 + block_count * height * cell_count * 4,
            transcendentals=0,
        ),
    )(blocks, received, tiles)

    owned = pl.pallas_call(
        add_parts,
        out_shape=jax.ShapeDtypeStruct((own_blocks, height, cell_count), jnp.float32),
        in_specs=[vmem],
        out_specs=vmem,
        compiler_params=pltpu.CompilerParams(vmem_limit_bytes=16 * 1024 * 1024),
    )(exchange(coded, size))
    return owned.reshape(own_blocks, tracer_count, months, cell_count)


def solution(mesh):
    in_specs = (
        P(("groups", "tm"), None, None, "cells"),
        P(("groups", "tm"), None),
        P("tm", None, None),
    )
    out_specs = P(("groups", "tm"), None, None, "cells")
    return jax.shard_map(shards, mesh=mesh, in_specs=in_specs, out_specs=out_specs, check_vma=False)
```

```python
import functools

import jax
import jax.numpy as jnp
from jax import lax
from jax.experimental import pallas as pl
from jax.experimental.pallas import tpu as pltpu
from jax.sharding import PartitionSpec as P

STEPS = 32700.0
LEVELS = 128
SMALLEST = 2.0**-126


def tile_sums(months, blocks_ref, histories_ref, tiles_ref, coded_ref, wide_ref, sums_ref):
    packed_rows, packed_width = histories_ref.shape[1:]
    slot_count, tile_height, cell_count = tiles_ref.shape
    block_count, height, cell_count = sums_ref.shape
    size = coded_ref.shape[0]
    own_blocks = block_count // size

    first = blocks_ref[0, 0]
    row_of = lax.broadcasted_iota(jnp.int32, (height, packed_rows), 0) // months * own_blocks
    packed_row = lax.broadcasted_iota(jnp.int32, (height, packed_rows), 1)
    column_of = lax.broadcasted_iota(jnp.int32, (packed_width, tile_height), 1) // months
    packed_column = lax.broadcasted_iota(jnp.int32, (packed_width, tile_height), 0)
    repeat_columns = (column_of == packed_column).astype(jnp.bfloat16)
    month_of_row = lax.broadcasted_iota(jnp.int32, (height, tile_height), 0) % months
    month_of_column = lax.broadcasted_iota(jnp.int32, (height, tile_height), 1) % months
    same_month = month_of_row == month_of_column
    for which, source in enumerate((first, block_count - 1 - first)):
        repeat_rows = (row_of + source % own_blocks == packed_row).astype(jnp.bfloat16)
        tall = jnp.dot(
            repeat_rows, histories_ref[slot_of(source // own_blocks, size)], preferred_element_type=jnp.float32
        )
        wide = jnp.dot(tall.astype(jnp.bfloat16), repeat_columns, preferred_element_type=jnp.float32)
        wide_ref[which] = jnp.where(same_month, wide, 0.0).astype(jnp.bfloat16)

    sums_ref[...] = jnp.zeros(sums_ref.shape, sums_ref.dtype)

    def add_tile(slot):
        which = (blocks_ref[0, slot] != first).astype(jnp.int32)
        arrival = blocks_ref[1, slot]
        place = slot_of(arrival // own_blocks, size) * own_blocks + arrival % own_blocks
        sums_ref[place] += jnp.dot(wide_ref[which], tiles_ref[slot], preferred_element_type=jnp.float32)

    unrolled = 17
    rounds = slot_count // unrolled

    def add_round(turn, carry):
        for step in range(unrolled):
            add_tile(turn * unrolled + step)
        return carry

    if rounds == 1:
        add_round(0, 0)
    else:
        lax.fori_loop(0, rounds, add_round, 0)
    for slot in range(rounds * unrolled, slot_count):
        add_tile(slot)

    coded_rows = own_blocks * height

    def code(slot, carry):
        blocks = [sums_ref[slot * own_blocks + block] for block in range(own_blocks)]
        top = jnp.max(functools.reduce(jnp.maximum, map(jnp.abs, blocks)), axis=0, keepdims=True)
        level = jnp.ceil(jnp.log2(jnp.maximum(top, SMALLEST)) * LEVELS)
        half = jnp.exp2(level * (-0.5 / LEVELS))
        for block, value in enumerate(blocks):
            steps = jnp.round(value * half * (half * STEPS))
            coded_ref[slot, pl.ds(block * height, height)] = steps.astype(jnp.int32).astype(jnp.int16)
        spread = jnp.broadcast_to(level.astype(jnp.int32), (16, cell_count))
        coded_ref[slot, pl.ds(coded_rows, 16)] = spread.astype(jnp.int16)
        return carry

    lax.fori_loop(0, size, code, 0, unroll=size <= 8)


def add_parts(coded_ref, total_ref):
    size = coded_ref.shape[0]
    own_blocks, height, cell_count = total_ref.shape
    coded_rows = own_blocks * height
    total_ref[...] = jnp.zeros(total_ref.shape, total_ref.dtype)

    def add(slot, carry):
        level = coded_ref[slot, pl.ds(coded_rows, 16)].astype(jnp.int32).astype(jnp.float32)[:1]
        half = jnp.exp2(level * (0.5 / LEVELS))
        for block in range(own_blocks):
            steps = coded_ref[slot, pl.ds(block * height, height)].astype(jnp.int32)
            total_ref[block] += steps.astype(jnp.float32) * (half * (1.0 / STEPS)) * half
        return carry

    lax.fori_loop(0, size, add, 0, unroll=size <= 8)


def stage(blocks_in, tiles_in, blocks_out, tiles_out, semaphores):
    copies = [
        pltpu.make_async_copy(blocks_in, blocks_out, semaphores.at[0]),
        pltpu.make_async_copy(tiles_in, tiles_out, semaphores.at[1]),
    ]
    for copy in copies:
        copy.start()
    for copy in copies:
        copy.wait()


def centre(size):
    return size * 5 // 8


def slot_of(device, size):
    return jnp.where(device == centre(size), 0, device + (device < centre(size)).astype(jnp.int32))


def exchange(value, size):
    first = centre(size)
    order = [first] + [device for device in range(size) if device != first]
    return lax.all_to_all(value, "tm", 0, 0, axis_index_groups=[order], tiled=True)


def shards(propagator, tile_blocks, histories):
    size = lax.axis_size("tm")
    own_blocks, tracer_count, source_width = histories.shape
    slot_count, source_width, months, cell_count = propagator.shape
    block_count = size * own_blocks
    height = tracer_count * months

    used_rows = tracer_count * own_blocks
    rows = jnp.swapaxes(histories, 0, 1).reshape(1, used_rows, source_width)
    copies = jnp.pad(
        jnp.broadcast_to(rows, (size, used_rows, source_width)),
        ((0, 0), (0, -used_rows % 16), (0, -source_width % 128)),
    )
    received = exchange(copies, size)

    tiles = propagator.reshape(slot_count, source_width * months, cell_count)
    blocks = tile_blocks.T
    vmem = pl.BlockSpec(memory_space=pltpu.VMEM)
    smem = pl.BlockSpec(memory_space=pltpu.SMEM)
    hbm = pl.BlockSpec(memory_space=pltpu.HBM)
    blocks, tiles = pl.pallas_call(
        stage,
        out_shape=[
            jax.ShapeDtypeStruct(blocks.shape, blocks.dtype),
            jax.ShapeDtypeStruct(tiles.shape, tiles.dtype),
        ],
        in_specs=[hbm, hbm],
        out_specs=[vmem, vmem],
        scratch_shapes=[pltpu.SemaphoreType.DMA((2,))],
        compiler_params=pltpu.CompilerParams(vmem_limit_bytes=16 * 1024 * 1024),
        cost_estimate=pl.CostEstimate(flops=0, bytes_accessed=propagator.size * 4, transcendentals=0),
    )(blocks, tiles)
    coded = pl.pallas_call(
        lambda *refs: tile_sums(months, *refs),
        out_shape=jax.ShapeDtypeStruct((size, own_blocks * height + 16, cell_count), jnp.int16),
        in_specs=[smem, vmem, vmem],
        out_specs=vmem,
        scratch_shapes=[
            pltpu.VMEM((2, height, source_width * months), jnp.bfloat16),
            pltpu.VMEM((block_count, height, cell_count), jnp.float32),
        ],
        compiler_params=pltpu.CompilerParams(vmem_limit_bytes=32 * 1024 * 1024),
        cost_estimate=pl.CostEstimate(
            flops=2 * slot_count * height * source_width * months * cell_count,
            bytes_accessed=propagator.size * 2 + block_count * height * cell_count * 4,
            transcendentals=0,
        ),
    )(blocks, received, tiles)

    owned = pl.pallas_call(
        add_parts,
        out_shape=jax.ShapeDtypeStruct((own_blocks, height, cell_count), jnp.float32),
        in_specs=[vmem],
        out_specs=vmem,
        compiler_params=pltpu.CompilerParams(vmem_limit_bytes=16 * 1024 * 1024),
    )(exchange(coded, size))
    return owned.reshape(own_blocks, tracer_count, months, cell_count)


def solution(mesh):
    in_specs = (
        P(("groups", "tm"), None, None, "cells"),
        P(("groups", "tm"), None),
        P("tm", None, None),
    )
    out_specs = P(("groups", "tm"), None, None, "cells")
    return jax.shard_map(shards, mesh=mesh, in_specs=in_specs, out_specs=out_specs, check_vma=False)
```

```python
import functools

import jax
import jax.numpy as jnp
from jax import lax
from jax.experimental import pallas as pl
from jax.experimental.pallas import tpu as pltpu
from jax.sharding import PartitionSpec as P

STEPS = 32700.0
LEVELS = 128
SMALLEST = 2.0**-126


def tile_sums(months, blocks_ref, histories_ref, tiles_ref, coded_ref, wide_ref, sums_ref):
    packed_rows, packed_width = histories_ref.shape[1:]
    slot_count, tile_height, cell_count = tiles_ref.shape
    block_count, height, cell_count = sums_ref.shape
    size = coded_ref.shape[0]
    own_blocks = block_count // size

    first = blocks_ref[0, 0]
    row_of = lax.broadcasted_iota(jnp.int32, (height, packed_rows), 0) // months * own_blocks
    packed_row = lax.broadcasted_iota(jnp.int32, (height, packed_rows), 1)
    column_of = lax.broadcasted_iota(jnp.int32, (packed_width, tile_height), 1) // months
    packed_column = lax.broadcasted_iota(jnp.int32, (packed_width, tile_height), 0)
    repeat_columns = (column_of == packed_column).astype(jnp.bfloat16)
    month_of_row = lax.broadcasted_iota(jnp.int32, (height, tile_height), 0) % months
    month_of_column = lax.broadcasted_iota(jnp.int32, (height, tile_height), 1) % months
    same_month = month_of_row == month_of_column
    for which, source in enumerate((first, block_count - 1 - first)):
        repeat_rows = (row_of + source % own_blocks == packed_row).astype(jnp.bfloat16)
        tall = jnp.dot(
            repeat_rows, histories_ref[slot_of(source // own_blocks, size)], preferred_element_type=jnp.float32
        )
        wide = jnp.dot(tall.astype(jnp.bfloat16), repeat_columns, preferred_element_type=jnp.float32)
        wide_ref[which] = jnp.where(same_month, wide, 0.0).astype(jnp.bfloat16)

    sums_ref[...] = jnp.zeros(sums_ref.shape, sums_ref.dtype)

    def add_tile(slot):
        which = (blocks_ref[0, slot] != first).astype(jnp.int32)
        arrival = blocks_ref[1, slot]
        place = slot_of(arrival // own_blocks, size) * own_blocks + arrival % own_blocks
        sums_ref[place] += jnp.dot(wide_ref[which], tiles_ref[slot], preferred_element_type=jnp.float32)

    unrolled = 17
    rounds = slot_count // unrolled

    def add_round(turn, carry):
        for step in range(unrolled):
            add_tile(turn * unrolled + step)
        return carry

    if rounds == 1:
        add_round(0, 0)
    else:
        lax.fori_loop(0, rounds, add_round, 0)
    for slot in range(rounds * unrolled, slot_count):
        add_tile(slot)

    coded_rows = own_blocks * height

    def code(slot, carry):
        blocks = [sums_ref[slot * own_blocks + block] for block in range(own_blocks)]
        top = jnp.max(functools.reduce(jnp.maximum, map(jnp.abs, blocks)), axis=0, keepdims=True)
        level = jnp.ceil(jnp.log2(jnp.maximum(top, SMALLEST)) * LEVELS)
        half = jnp.exp2(level * (-0.5 / LEVELS))
        for block, value in enumerate(blocks):
            steps = jnp.round(value * half * (half * STEPS))
            coded_ref[slot, pl.ds(block * height, height)] = steps.astype(jnp.int32).astype(jnp.int16)
        spread = jnp.broadcast_to(level.astype(jnp.int32), (16, cell_count))
        coded_ref[slot, pl.ds(coded_rows, 16)] = spread.astype(jnp.int16)
        return carry

    lax.fori_loop(0, size, code, 0, unroll=size <= 8)


def add_parts(coded_ref, total_ref):
    size = coded_ref.shape[0]
    own_blocks, height, cell_count = total_ref.shape
    coded_rows = own_blocks * height
    total_ref[...] = jnp.zeros(total_ref.shape, total_ref.dtype)

    def add(slot, carry):
        level = coded_ref[slot, pl.ds(coded_rows, 16)].astype(jnp.int32).astype(jnp.float32)[:1]
        half = jnp.exp2(level * (0.5 / LEVELS))
        for block in range(own_blocks):
            steps = coded_ref[slot, pl.ds(block * height, height)].astype(jnp.int32)
            total_ref[block] += steps.astype(jnp.float32) * (half * (1.0 / STEPS)) * half
        return carry

    lax.fori_loop(0, size, add, 0, unroll=size <= 8)


def centre(size):
    return size * 5 // 8


def slot_of(device, size):
    return jnp.where(device == centre(size), 0, device + (device < centre(size)).astype(jnp.int32))


def exchange(value, size):
    first = centre(size)
    order = [first] + [device for device in range(size) if device != first]
    return lax.all_to_all(value, "tm", 0, 0, axis_index_groups=[order], tiled=True)


def shards(propagator, tile_blocks, histories):
    size = lax.axis_size("tm")
    own_blocks, tracer_count, source_width = histories.shape
    slot_count, source_width, months, cell_count = propagator.shape
    block_count = size * own_blocks
    height = tracer_count * months

    used_rows = tracer_count * own_blocks
    rows = jnp.swapaxes(histories, 0, 1).reshape(1, used_rows, source_width)
    copies = jnp.pad(
        jnp.broadcast_to(rows, (size, used_rows, source_width)),
        ((0, 0), (0, -used_rows % 16), (0, -source_width % 128)),
    )
    received = exchange(copies, size)

    tiles = propagator.reshape(slot_count, source_width * months, cell_count)
    blocks = tile_blocks.T
    vmem = pl.BlockSpec(memory_space=pltpu.VMEM)
    smem = pl.BlockSpec(memory_space=pltpu.SMEM)
    hbm = pl.BlockSpec(memory_space=pltpu.HBM)
    tiles = lax.ppermute(tiles, "tm", [(i, i) for i in range(size)])
    blocks = lax.ppermute(blocks, "tm", [(i, i) for i in range(size)])
    coded = pl.pallas_call(
        lambda *refs: tile_sums(months, *refs),
        out_shape=jax.ShapeDtypeStruct((size, own_blocks * height + 16, cell_count), jnp.int16),
        in_specs=[smem, vmem, vmem],
        out_specs=vmem,
        scratch_shapes=[
            pltpu.VMEM((2, height, source_width * months), jnp.bfloat16),
            pltpu.VMEM((block_count, height, cell_count), jnp.float32),
        ],
        compiler_params=pltpu.CompilerParams(vmem_limit_bytes=32 * 1024 * 1024),
        cost_estimate=pl.CostEstimate(
            flops=2 * slot_count * height * source_width * months * cell_count,
            bytes_accessed=propagator.size * 2 + block_count * height * cell_count * 4,
            transcendentals=0,
        ),
    )(blocks, received, tiles)

    owned = pl.pallas_call(
        add_parts,
        out_shape=jax.ShapeDtypeStruct((own_blocks, height, cell_count), jnp.float32),
        in_specs=[vmem],
        out_specs=vmem,
        compiler_params=pltpu.CompilerParams(vmem_limit_bytes=16 * 1024 * 1024),
    )(exchange(coded, size))
    return owned.reshape(own_blocks, tracer_count, months, cell_count)


def solution(mesh):
    in_specs = (
        P(("groups", "tm"), None, None, "cells"),
        P(("groups", "tm"), None),
        P("tm", None, None),
    )
    out_specs = P(("groups", "tm"), None, None, "cells")
    return jax.shard_map(shards, mesh=mesh, in_specs=in_specs, out_specs=out_specs, check_vma=False)
```

```python
import jax
import jax.numpy as jnp
from jax import lax
from jax.experimental import pallas as pl
from jax.experimental.pallas import tpu as pltpu
from jax.sharding import PartitionSpec as P

STEPS = 32700.0
LEVELS = 128
SMALLEST = 2.0**-126


def centre(size):
    return size * 5 // 8


def slot_of(device, size):
    return jnp.where(device == centre(size), 0, device + (device < centre(size)).astype(jnp.int32))


def device_of(slot, size):
    if isinstance(slot, int):
        return centre(size) if slot == 0 else slot - (slot <= centre(size))
    return jnp.where(slot == 0, centre(size), slot - (slot <= centre(size)).astype(jnp.int32))


def exchange(value, size):
    order = [device_of(slot, size) for slot in range(size)]
    return lax.all_to_all(value, "tm", 0, 0, axis_index_groups=[order], tiled=True)


def each(count, body):
    if count <= 17:
        for index in range(count):
            body(index)
    else:
        lax.fori_loop(0, count, lambda index, carry: (body(index), carry)[1], 0)


def stage(size, months, own_blocks, blocks_ref, tiles_ref, sorted_ref, pick_ref, semaphores):
    block_count = sorted_ref.shape[0]
    slot_count = tiles_ref.shape[0]
    height = pick_ref.shape[0] // 2
    packed_rows = pick_ref.shape[1] // size
    first = blocks_ref[0, 0]

    def clear(block):
        sorted_ref[block] = jnp.zeros(sorted_ref.shape[1:], sorted_ref.dtype)

    def load(slot):
        which = (blocks_ref[0, slot] != first).astype(jnp.int32)
        place = sorted_ref.at[blocks_ref[1, slot], which]
        return pltpu.make_async_copy(tiles_ref.at[slot], place, semaphores.at[slot])

    each(block_count, clear)
    each(slot_count, lambda slot: load(slot).start())
    row = lax.broadcasted_iota(jnp.int32, (height, pick_ref.shape[1]), 0)
    column = lax.broadcasted_iota(jnp.int32, (height, pick_ref.shape[1]), 1)
    for which, source in enumerate((first, block_count - 1 - first)):
        start = slot_of(source // own_blocks, size) * packed_rows + source % own_blocks
        picked = column == start + row // months * own_blocks
        pick_ref[pl.ds(which * height, height)] = picked.astype(jnp.bfloat16)
    each(slot_count, lambda slot: load(slot).wait())


def tile_sums(months, histories_ref, pick_ref, sorted_ref, coded_ref):
    size, packed_rows, packed_width = histories_ref.shape
    block_count, sources, tile_height, cell_count = sorted_ref.shape
    own_blocks = block_count // size
    height = pick_ref.shape[0] // sources

    column_of = lax.broadcasted_iota(jnp.int32, (packed_width, tile_height), 1) // months
    packed_column = lax.broadcasted_iota(jnp.int32, (packed_width, tile_height), 0)
    repeat_columns = (column_of == packed_column).astype(jnp.bfloat16)
    month_of_row = lax.broadcasted_iota(jnp.int32, (sources * height, tile_height), 0) % months
    month_of_column = lax.broadcasted_iota(jnp.int32, (sources * height, tile_height), 1) % months
    histories = histories_ref[...].reshape(size * packed_rows, packed_width)
    tall = jnp.dot(pick_ref[...], histories, preferred_element_type=jnp.float32)
    wide = jnp.dot(tall.astype(jnp.bfloat16), repeat_columns, preferred_element_type=jnp.float32)
    wide = jnp.where(month_of_row == month_of_column, wide, 0.0).astype(jnp.bfloat16)

    coded_rows = own_blocks * height

    def code(slot):
        values = []
        for block in range(own_blocks):
            place = device_of(slot, size) * own_blocks + block
            parts = [
                jnp.dot(
                    wide[which * height : (which + 1) * height],
                    sorted_ref[place, which],
                    preferred_element_type=jnp.float32,
                )
                for which in range(sources)
            ]
            values.append(sum(parts[1:], parts[0]))
        top = jnp.abs(values[0])
        for value in values[1:]:
            top = jnp.maximum(top, jnp.abs(value))
        top = jnp.max(top, axis=0, keepdims=True)
        level = jnp.ceil(jnp.log2(jnp.maximum(top, SMALLEST)) * LEVELS)
        half = jnp.exp2(level * (-0.5 / LEVELS))
        for block, value in enumerate(values):
            steps = jnp.round(value * half * (half * STEPS))
            coded_ref[slot, pl.ds(block * height, height)] = steps.astype(jnp.int32).astype(jnp.int16)
        spread = jnp.broadcast_to(level.astype(jnp.int32), (16, cell_count))
        coded_ref[slot, pl.ds(coded_rows, 16)] = spread.astype(jnp.int16)

    each(size, code)


def add_parts(coded_ref, total_ref):
    size = coded_ref.shape[0]
    own_blocks, height, cell_count = total_ref.shape
    coded_rows = own_blocks * height
    total_ref[...] = jnp.zeros(total_ref.shape, total_ref.dtype)

    def add(slot):
        level = coded_ref[slot, pl.ds(coded_rows, 16)].astype(jnp.int32).astype(jnp.float32)[:1]
        half = jnp.exp2(level * (0.5 / LEVELS))
        for block in range(own_blocks):
            steps = coded_ref[slot, pl.ds(block * height, height)].astype(jnp.int32)
            total_ref[block] += steps.astype(jnp.float32) * (half * (1.0 / STEPS)) * half

    each(size, add)


def shards(propagator, tile_blocks, histories):
    size = lax.axis_size("tm")
    own_blocks, tracer_count, source_width = histories.shape
    slot_count, source_width, months, cell_count = propagator.shape
    block_count = size * own_blocks
    height = tracer_count * months
    tile_height = source_width * months

    used_rows = tracer_count * own_blocks
    rows = jnp.swapaxes(histories, 0, 1).reshape(1, used_rows, source_width)
    copies = jnp.pad(
        jnp.broadcast_to(rows, (size, used_rows, source_width)),
        ((0, 0), (0, -used_rows % 16), (0, -source_width % 128)),
    )
    received = exchange(copies, size)

    vmem = pl.BlockSpec(memory_space=pltpu.VMEM)
    smem = pl.BlockSpec(memory_space=pltpu.SMEM)
    anywhere = pl.BlockSpec(memory_space=pl.ANY)
    sorted_tiles, pick = pl.pallas_call(
        lambda *refs: stage(size, months, own_blocks, *refs),
        out_shape=[
            jax.ShapeDtypeStruct((block_count, 2, tile_height, cell_count), propagator.dtype),
            jax.ShapeDtypeStruct((2 * height, size * copies.shape[1]), jnp.bfloat16),
        ],
        in_specs=[smem, anywhere],
        out_specs=[vmem, vmem],
        scratch_shapes=[pltpu.SemaphoreType.DMA((slot_count,))],
        compiler_params=pltpu.CompilerParams(vmem_limit_bytes=20 * 1024 * 1024),
        cost_estimate=pl.CostEstimate(flops=0, bytes_accessed=propagator.size * 4, transcendentals=0),
    )(tile_blocks.T, propagator.reshape(slot_count, tile_height, cell_count))

    coded = pl.pallas_call(
        lambda *refs: tile_sums(months, *refs),
        out_shape=jax.ShapeDtypeStruct((size, own_blocks * height + 16, cell_count), jnp.int16),
        in_specs=[vmem, vmem, vmem],
        out_specs=vmem,
        compiler_params=pltpu.CompilerParams(vmem_limit_bytes=20 * 1024 * 1024),
        cost_estimate=pl.CostEstimate(
            flops=2 * slot_count * height * tile_height * cell_count,
            bytes_accessed=propagator.size * 4,
            transcendentals=0,
        ),
    )(received, pick, sorted_tiles)

    owned = pl.pallas_call(
        add_parts,
        out_shape=jax.ShapeDtypeStruct((own_blocks, height, cell_count), jnp.float32),
        in_specs=[vmem],
        out_specs=vmem,
        compiler_params=pltpu.CompilerParams(vmem_limit_bytes=16 * 1024 * 1024),
    )(exchange(coded, size))
    return owned.reshape(own_blocks, tracer_count, months, cell_count)


def solution(mesh):
    in_specs = (
        P(("groups", "tm"), None, None, "cells"),
        P(("groups", "tm"), None),
        P("tm", None, None),
    )
    out_specs = P(("groups", "tm"), None, None, "cells")
    return jax.shard_map(shards, mesh=mesh, in_specs=in_specs, out_specs=out_specs, check_vma=False)
```

```python
import jax
import jax.numpy as jnp
from jax import lax
from jax.experimental import pallas as pl
from jax.experimental.pallas import tpu as pltpu
from jax.sharding import PartitionSpec as P

STEPS = 32700.0
LEVELS = 128
SMALLEST = 2.0**-126


def centre(size):
    return size * 5 // 8


def slot_of(device, size):
    after = device - (device > centre(size)).astype(jnp.int32)
    return jnp.where(device == centre(size), 0, jnp.where(device == 0, size - 1, after))


def device_of(slot, size):
    if isinstance(slot, int):
        return centre(size) if slot == 0 else 0 if slot == size - 1 else slot + (slot >= centre(size))
    after = slot + (slot >= centre(size)).astype(jnp.int32)
    return jnp.where(slot == 0, centre(size), jnp.where(slot == size - 1, 0, after))


def exchange(value, size):
    order = [device_of(slot, size) for slot in range(size)]
    return lax.all_to_all(value, "tm", 0, 0, axis_index_groups=[order], tiled=True)


def each(count, body):
    if count <= 17:
        for index in range(count):
            body(index)
    else:
        lax.fori_loop(0, count, lambda index, carry: (body(index), carry)[1], 0)


def stage(size, months, own_blocks, blocks_ref, tiles_ref, sorted_ref, pick_ref):
    block_count = sorted_ref.shape[0]
    slot_count = tiles_ref.shape[0]
    height = pick_ref.shape[0] // 2
    packed_rows = pick_ref.shape[1] // size
    first = blocks_ref[0, 0]

    def clear(block):
        sorted_ref[block] = jnp.zeros(sorted_ref.shape[1:], sorted_ref.dtype)

    def place(slot):
        which = (blocks_ref[0, slot] != first).astype(jnp.int32)
        sorted_ref[blocks_ref[1, slot], which] = tiles_ref[slot]

    each(block_count, clear)
    each(slot_count, place)
    row = lax.broadcasted_iota(jnp.int32, (height, pick_ref.shape[1]), 0)
    column = lax.broadcasted_iota(jnp.int32, (height, pick_ref.shape[1]), 1)
    for which, source in enumerate((first, block_count - 1 - first)):
        start = slot_of(source // own_blocks, size) * packed_rows + source % own_blocks
        picked = column == start + row // months * own_blocks
        pick_ref[pl.ds(which * height, height)] = picked.astype(jnp.bfloat16)


def tile_sums(months, histories_ref, pick_ref, sorted_ref, coded_ref):
    size, packed_rows, packed_width = histories_ref.shape
    block_count, sources, tile_height, cell_count = sorted_ref.shape
    own_blocks = block_count // size
    height = pick_ref.shape[0] // sources

    column_of = lax.broadcasted_iota(jnp.int32, (packed_width, tile_height), 1) // months
    packed_column = lax.broadcasted_iota(jnp.int32, (packed_width, tile_height), 0)
    repeat_columns = (column_of == packed_column).astype(jnp.bfloat16)
    month_of_row = lax.broadcasted_iota(jnp.int32, (sources * height, tile_height), 0) % months
    month_of_column = lax.broadcasted_iota(jnp.int32, (sources * height, tile_height), 1) % months
    histories = histories_ref[...].reshape(size * packed_rows, packed_width)
    tall = jnp.dot(pick_ref[...], histories, preferred_element_type=jnp.float32)
    wide = jnp.dot(tall.astype(jnp.bfloat16), repeat_columns, preferred_element_type=jnp.float32)
    wide = jnp.where(month_of_row == month_of_column, wide, 0.0).astype(jnp.bfloat16)

    coded_rows = own_blocks * height

    def code(slot):
        values = []
        for block in range(own_blocks):
            place = device_of(slot, size) * own_blocks + block
            parts = [
                jnp.dot(
                    wide[which * height : (which + 1) * height],
                    sorted_ref[place, which],
                    preferred_element_type=jnp.float32,
                )
                for which in range(sources)
            ]
            values.append(sum(parts[1:], parts[0]))
        top = jnp.abs(values[0])
        for value in values[1:]:
            top = jnp.maximum(top, jnp.abs(value))
        top = jnp.max(top, axis=0, keepdims=True)
        level = jnp.ceil(jnp.log2(jnp.maximum(top, SMALLEST)) * LEVELS)
        half = jnp.exp2(level * (-0.5 / LEVELS))
        for block, value in enumerate(values):
            steps = jnp.round(value * half * (half * STEPS))
            coded_ref[slot, pl.ds(block * height, height)] = steps.astype(jnp.int32).astype(jnp.int16)
        spread = jnp.broadcast_to(level.astype(jnp.int32), (16, cell_count))
        coded_ref[slot, pl.ds(coded_rows, 16)] = spread.astype(jnp.int16)

    each(size, code)


def add_parts(coded_ref, total_ref):
    size = coded_ref.shape[0]
    own_blocks, height, cell_count = total_ref.shape
    coded_rows = own_blocks * height
    total_ref[...] = jnp.zeros(total_ref.shape, total_ref.dtype)

    def add(slot):
        level = coded_ref[slot, pl.ds(coded_rows, 16)].astype(jnp.int32).astype(jnp.float32)[:1]
        half = jnp.exp2(level * (0.5 / LEVELS))
        for block in range(own_blocks):
            steps = coded_ref[slot, pl.ds(block * height, height)].astype(jnp.int32)
            total_ref[block] += steps.astype(jnp.float32) * (half * (1.0 / STEPS)) * half

    each(size, add)


def shards(propagator, tile_blocks, histories):
    size = lax.axis_size("tm")
    own_blocks, tracer_count, source_width = histories.shape
    slot_count, source_width, months, cell_count = propagator.shape
    block_count = size * own_blocks
    height = tracer_count * months
    tile_height = source_width * months

    used_rows = tracer_count * own_blocks
    rows = jnp.swapaxes(histories, 0, 1).reshape(1, used_rows, source_width)
    copies = jnp.pad(
        jnp.broadcast_to(rows, (size, used_rows, source_width)),
        ((0, 0), (0, -used_rows % 16), (0, -source_width % 128)),
    )
    received = exchange(copies, size)

    vmem = pl.BlockSpec(memory_space=pltpu.VMEM)
    smem = pl.BlockSpec(memory_space=pltpu.SMEM)
    sorted_tiles, pick = pl.pallas_call(
        lambda *refs: stage(size, months, own_blocks, *refs),
        out_shape=[
            jax.ShapeDtypeStruct((block_count, 2, tile_height, cell_count), propagator.dtype),
            jax.ShapeDtypeStruct((2 * height, size * copies.shape[1]), jnp.bfloat16),
        ],
        in_specs=[smem, vmem],
        out_specs=[vmem, vmem],
        compiler_params=pltpu.CompilerParams(vmem_limit_bytes=20 * 1024 * 1024),
        cost_estimate=pl.CostEstimate(flops=0, bytes_accessed=propagator.size * 4, transcendentals=0),
    )(tile_blocks.T, propagator.reshape(slot_count, tile_height, cell_count))

    coded = pl.pallas_call(
        lambda *refs: tile_sums(months, *refs),
        out_shape=jax.ShapeDtypeStruct((size, own_blocks * height + 16, cell_count), jnp.int16),
        in_specs=[vmem, vmem, vmem],
        out_specs=vmem,
        compiler_params=pltpu.CompilerParams(vmem_limit_bytes=20 * 1024 * 1024),
        cost_estimate=pl.CostEstimate(
            flops=2 * slot_count * height * tile_height * cell_count,
            bytes_accessed=propagator.size * 4,
            transcendentals=0,
        ),
    )(received, pick, sorted_tiles)

    owned = pl.pallas_call(
        add_parts,
        out_shape=jax.ShapeDtypeStruct((own_blocks, height, cell_count), jnp.float32),
        in_specs=[vmem],
        out_specs=vmem,
        compiler_params=pltpu.CompilerParams(vmem_limit_bytes=16 * 1024 * 1024),
    )(exchange(coded, size))
    return owned.reshape(own_blocks, tracer_count, months, cell_count)


def solution(mesh):
    in_specs = (
        P(("groups", "tm"), None, None, "cells"),
        P(("groups", "tm"), None),
        P("tm", None, None),
    )
    out_specs = P(("groups", "tm"), None, None, "cells")
    return jax.shard_map(shards, mesh=mesh, in_specs=in_specs, out_specs=out_specs, check_vma=False)
```

```python
import jax
import jax.numpy as jnp
from jax import lax
from jax.experimental import pallas as pl
from jax.experimental.pallas import tpu as pltpu
from jax.sharding import PartitionSpec as P

STEPS = 32700.0
LEVELS = 128
SMALLEST = 2.0**-126


def centre(size):
    return size * 5 // 8


def slot_of(device, size):
    after = device - (device > centre(size)).astype(jnp.int32)
    return jnp.where(device == centre(size), 0, jnp.where(device == 0, size - 1, after))


def device_of(slot, size):
    if isinstance(slot, int):
        return centre(size) if slot == 0 else 0 if slot == size - 1 else slot + (slot >= centre(size))
    after = slot + (slot >= centre(size)).astype(jnp.int32)
    return jnp.where(slot == 0, centre(size), jnp.where(slot == size - 1, 0, after))


def exchange(value, size):
    order = [device_of(slot, size) for slot in range(size)]
    return lax.all_to_all(value, "tm", 0, 0, axis_index_groups=[order], tiled=True)


def exchange_across(value, size):
    cells = lax.axis_size("cells")
    order = [device_of(slot, size) for slot in range(size)]
    groups = [
        [device * cells + (cell + (device >= size // 2)) % cells for device in order]
        for cell in range(cells)
    ]
    return lax.all_to_all(value, ("tm", "cells"), 0, 0, axis_index_groups=groups, tiled=True)


def each(count, body):
    if count <= 17:
        for index in range(count):
            body(index)
    else:
        lax.fori_loop(0, count, lambda index, carry: (body(index), carry)[1], 0)


def stage(size, months, own_blocks, blocks_ref, tiles_ref, sorted_ref, pick_ref):
    block_count = sorted_ref.shape[0]
    slot_count = tiles_ref.shape[0]
    height = pick_ref.shape[0] // 2
    packed_rows = pick_ref.shape[1] // size
    first = blocks_ref[0, 0]

    def clear(block):
        sorted_ref[block] = jnp.zeros(sorted_ref.shape[1:], sorted_ref.dtype)

    def place(slot):
        which = (blocks_ref[0, slot] != first).astype(jnp.int32)
        sorted_ref[blocks_ref[1, slot], which] = tiles_ref[slot]

    each(block_count, clear)
    each(slot_count, place)
    row = lax.broadcasted_iota(jnp.int32, (height, pick_ref.shape[1]), 0)
    column = lax.broadcasted_iota(jnp.int32, (height, pick_ref.shape[1]), 1)
    for which, source in enumerate((first, block_count - 1 - first)):
        start = slot_of(source // own_blocks, size) * packed_rows + source % own_blocks
        picked = column == start + row // months * own_blocks
        pick_ref[pl.ds(which * height, height)] = picked.astype(jnp.bfloat16)


def tile_sums(months, histories_ref, pick_ref, sorted_ref, coded_ref):
    size, packed_rows, packed_width = histories_ref.shape
    block_count, sources, tile_height, cell_count = sorted_ref.shape
    own_blocks = block_count // size
    height = pick_ref.shape[0] // sources

    column_of = lax.broadcasted_iota(jnp.int32, (packed_width, tile_height), 1) // months
    packed_column = lax.broadcasted_iota(jnp.int32, (packed_width, tile_height), 0)
    repeat_columns = (column_of == packed_column).astype(jnp.bfloat16)
    month_of_row = lax.broadcasted_iota(jnp.int32, (sources * height, tile_height), 0) % months
    month_of_column = lax.broadcasted_iota(jnp.int32, (sources * height, tile_height), 1) % months
    histories = histories_ref[...].reshape(size * packed_rows, packed_width)
    tall = jnp.dot(pick_ref[...], histories, preferred_element_type=jnp.float32)
    wide = jnp.dot(tall.astype(jnp.bfloat16), repeat_columns, preferred_element_type=jnp.float32)
    wide = jnp.where(month_of_row == month_of_column, wide, 0.0).astype(jnp.bfloat16)

    coded_rows = own_blocks * height

    def code(slot):
        values = []
        for block in range(own_blocks):
            place = device_of(slot, size) * own_blocks + block
            parts = [
                jnp.dot(
                    wide[which * height : (which + 1) * height],
                    sorted_ref[place, which],
                    preferred_element_type=jnp.float32,
                )
                for which in range(sources)
            ]
            values.append(sum(parts[1:], parts[0]))
        top = jnp.abs(values[0])
        for value in values[1:]:
            top = jnp.maximum(top, jnp.abs(value))
        top = jnp.max(top, axis=0, keepdims=True)
        level = jnp.ceil(jnp.log2(jnp.maximum(top, SMALLEST)) * LEVELS)
        half = jnp.exp2(level * (-0.5 / LEVELS))
        for block, value in enumerate(values):
            steps = jnp.round(value * half * (half * STEPS))
            coded_ref[slot, pl.ds(block * height, height)] = steps.astype(jnp.int32).astype(jnp.int16)
        spread = jnp.broadcast_to(level.astype(jnp.int32), (16, cell_count))
        coded_ref[slot, pl.ds(coded_rows, 16)] = spread.astype(jnp.int16)

    each(size, code)


def add_parts(coded_ref, total_ref):
    size = coded_ref.shape[0]
    own_blocks, height, cell_count = total_ref.shape
    coded_rows = own_blocks * height
    total_ref[...] = jnp.zeros(total_ref.shape, total_ref.dtype)

    def add(slot):
        level = coded_ref[slot, pl.ds(coded_rows, 16)].astype(jnp.int32).astype(jnp.float32)[:1]
        half = jnp.exp2(level * (0.5 / LEVELS))
        for block in range(own_blocks):
            steps = coded_ref[slot, pl.ds(block * height, height)].astype(jnp.int32)
            total_ref[block] += steps.astype(jnp.float32) * (half * (1.0 / STEPS)) * half

    each(size, add)


def shards(propagator, tile_blocks, histories):
    size = lax.axis_size("tm")
    own_blocks, tracer_count, source_width = histories.shape
    slot_count, source_width, months, cell_count = propagator.shape
    block_count = size * own_blocks
    height = tracer_count * months
    tile_height = source_width * months

    used_rows = tracer_count * own_blocks
    rows = jnp.swapaxes(histories, 0, 1).reshape(1, used_rows, source_width)
    copies = jnp.pad(
        jnp.broadcast_to(rows, (size, used_rows, source_width)),
        ((0, 0), (0, -used_rows % 16), (0, -source_width % 128)),
    )
    received = exchange_across(copies, size)

    vmem = pl.BlockSpec(memory_space=pltpu.VMEM)
    smem = pl.BlockSpec(memory_space=pltpu.SMEM)
    sorted_tiles, pick = pl.pallas_call(
        lambda *refs: stage(size, months, own_blocks, *refs),
        out_shape=[
            jax.ShapeDtypeStruct((block_count, 2, tile_height, cell_count), propagator.dtype),
            jax.ShapeDtypeStruct((2 * height, size * copies.shape[1]), jnp.bfloat16),
        ],
        in_specs=[smem, vmem],
        out_specs=[vmem, vmem],
        compiler_params=pltpu.CompilerParams(vmem_limit_bytes=20 * 1024 * 1024),
        cost_estimate=pl.CostEstimate(flops=0, bytes_accessed=propagator.size * 4, transcendentals=0),
    )(tile_blocks.T, propagator.reshape(slot_count, tile_height, cell_count))

    coded = pl.pallas_call(
        lambda *refs: tile_sums(months, *refs),
        out_shape=jax.ShapeDtypeStruct((size, own_blocks * height + 16, cell_count), jnp.int16),
        in_specs=[vmem, vmem, vmem],
        out_specs=vmem,
        compiler_params=pltpu.CompilerParams(vmem_limit_bytes=20 * 1024 * 1024),
        cost_estimate=pl.CostEstimate(
            flops=2 * slot_count * height * tile_height * cell_count,
            bytes_accessed=propagator.size * 4,
            transcendentals=0,
        ),
    )(received, pick, sorted_tiles)

    owned = pl.pallas_call(
        add_parts,
        out_shape=jax.ShapeDtypeStruct((own_blocks, height, cell_count), jnp.float32),
        in_specs=[vmem],
        out_specs=vmem,
        compiler_params=pltpu.CompilerParams(vmem_limit_bytes=16 * 1024 * 1024),
    )(exchange(coded, size))
    return owned.reshape(own_blocks, tracer_count, months, cell_count)


def solution(mesh):
    in_specs = (
        P(("groups", "tm"), None, None, "cells"),
        P(("groups", "tm"), None),
        P("tm", None, None),
    )
    out_specs = P(("groups", "tm"), None, None, "cells")
    return jax.shard_map(shards, mesh=mesh, in_specs=in_specs, out_specs=out_specs, check_vma=False)
```

```python
import jax
import jax.numpy as jnp
from jax import lax
from jax.experimental import pallas as pl
from jax.experimental.pallas import tpu as pltpu
from jax.sharding import PartitionSpec as P

STEPS = 32700.0
LEVELS = 128
SMALLEST = 2.0**-126
SCALE_ROWS = 8


def centre(size):
    return size * 5 // 8


def slot_of(device, size):
    after = device - (device > centre(size)).astype(jnp.int32)
    return jnp.where(device == centre(size), 0, jnp.where(device == 0, size - 1, after))


def device_of(slot, size):
    if isinstance(slot, int):
        return centre(size) if slot == 0 else 0 if slot == size - 1 else slot + (slot >= centre(size))
    after = slot + (slot >= centre(size)).astype(jnp.int32)
    return jnp.where(slot == 0, centre(size), jnp.where(slot == size - 1, 0, after))


def exchange(value, size):
    order = [device_of(slot, size) for slot in range(size)]
    return lax.all_to_all(value, "tm", 0, 0, axis_index_groups=[order], tiled=True)


def each(count, body):
    if count <= 17:
        for index in range(count):
            body(index)
    else:
        lax.fori_loop(0, count, lambda index, carry: (body(index), carry)[1], 0)


def stage(size, months, own_blocks, blocks_ref, tiles_ref, sorted_ref, pick_ref):
    block_count = sorted_ref.shape[0] * own_blocks
    slot_count, tile_height, cell_count = tiles_ref.shape
    height = pick_ref.shape[0] // 2
    packed_rows = pick_ref.shape[1] // size
    first = blocks_ref[0, 0]

    def clear(owner):
        sorted_ref[owner] = jnp.zeros(sorted_ref.shape[1:], sorted_ref.dtype)

    def place(slot):
        which = (blocks_ref[0, slot] != first).astype(jnp.int32)
        arrival = blocks_ref[1, slot]
        start = pl.multiple_of(arrival % own_blocks * cell_count, cell_count)
        sorted_ref[arrival // own_blocks, which, :, pl.ds(start, cell_count)] = tiles_ref[slot]

    each(size, clear)
    each(slot_count, place)
    row = lax.broadcasted_iota(jnp.int32, (height, pick_ref.shape[1]), 0)
    column = lax.broadcasted_iota(jnp.int32, (height, pick_ref.shape[1]), 1)
    for which, source in enumerate((first, block_count - 1 - first)):
        start = slot_of(source // own_blocks, size) * packed_rows + source % own_blocks
        picked = column == start + row // months * own_blocks
        pick_ref[pl.ds(which * height, height)] = picked.astype(jnp.bfloat16)


def tile_sums(months, histories_ref, pick_ref, sorted_ref, coded_ref):
    size, packed_rows, packed_width = histories_ref.shape
    sources, tile_height, row_length = sorted_ref.shape[1:]
    cell_count = coded_ref.shape[2]
    own_blocks = row_length // cell_count
    height = pick_ref.shape[0] // sources

    column_of = lax.broadcasted_iota(jnp.int32, (packed_width, tile_height), 1) // months
    packed_column = lax.broadcasted_iota(jnp.int32, (packed_width, tile_height), 0)
    repeat_columns = (column_of == packed_column).astype(jnp.bfloat16)
    month_of_row = lax.broadcasted_iota(jnp.int32, (sources * height, tile_height), 0) % months
    month_of_column = lax.broadcasted_iota(jnp.int32, (sources * height, tile_height), 1) % months
    histories = histories_ref[...].reshape(size * packed_rows, packed_width)
    tall = jnp.dot(pick_ref[...], histories, preferred_element_type=jnp.float32)
    wide = jnp.dot(tall.astype(jnp.bfloat16), repeat_columns, preferred_element_type=jnp.float32)
    wide = jnp.where(month_of_row == month_of_column, wide, 0.0).astype(jnp.bfloat16)

    coded_rows = own_blocks * height

    def code(slot):
        parts = [
            jnp.dot(
                wide[which * height : (which + 1) * height],
                sorted_ref[device_of(slot, size), which],
                preferred_element_type=jnp.float32,
            )
            for which in range(sources)
        ]
        total = sum(parts[1:], parts[0])
        values = [total[:, block * cell_count : (block + 1) * cell_count] for block in range(own_blocks)]
        top = jnp.abs(values[0])
        for value in values[1:]:
            top = jnp.maximum(top, jnp.abs(value))
        top = jnp.max(top, axis=0, keepdims=True)
        level = jnp.ceil(jnp.log2(jnp.maximum(top, SMALLEST)) * LEVELS)
        half = jnp.exp2(level * (-0.5 / LEVELS))
        for block, value in enumerate(values):
            steps = jnp.round(value * half * (half * STEPS))
            coded_ref[slot, pl.ds(block * height, height)] = steps.astype(jnp.int32).astype(jnp.int16)
        spread = jnp.broadcast_to(level.astype(jnp.int32), (SCALE_ROWS, cell_count))
        coded_ref[slot, pl.ds(coded_rows, SCALE_ROWS)] = spread.astype(jnp.int16)

    each(size, code)


def add_parts(coded_ref, total_ref):
    size = coded_ref.shape[0]
    own_blocks, height, cell_count = total_ref.shape
    coded_rows = own_blocks * height
    total_ref[...] = jnp.zeros(total_ref.shape, total_ref.dtype)

    def add(slot):
        level = coded_ref[slot, pl.ds(coded_rows, SCALE_ROWS)].astype(jnp.int32).astype(jnp.float32)[:1]
        half = jnp.exp2(level * (0.5 / LEVELS))
        for block in range(own_blocks):
            steps = coded_ref[slot, pl.ds(block * height, height)].astype(jnp.int32)
            total_ref[block] += steps.astype(jnp.float32) * (half * (1.0 / STEPS)) * half

    each(size, add)


def shards(propagator, tile_blocks, histories):
    size = lax.axis_size("tm")
    own_blocks, tracer_count, source_width = histories.shape
    slot_count, source_width, months, cell_count = propagator.shape
    height = tracer_count * months
    tile_height = source_width * months

    used_rows = tracer_count * own_blocks
    rows = jnp.swapaxes(histories, 0, 1).reshape(1, used_rows, source_width)
    copies = jnp.pad(
        jnp.broadcast_to(rows, (size, used_rows, source_width)),
        ((0, 0), (0, -used_rows % 16), (0, -source_width % 128)),
    )
    received = exchange(copies, size)

    vmem = pl.BlockSpec(memory_space=pltpu.VMEM)
    smem = pl.BlockSpec(memory_space=pltpu.SMEM)
    sorted_tiles, pick = pl.pallas_call(
        lambda *refs: stage(size, months, own_blocks, *refs),
        out_shape=[
            jax.ShapeDtypeStruct((size, 2, tile_height, own_blocks * cell_count), propagator.dtype),
            jax.ShapeDtypeStruct((2 * height, size * copies.shape[1]), jnp.bfloat16),
        ],
        in_specs=[smem, vmem],
        out_specs=[vmem, vmem],
        compiler_params=pltpu.CompilerParams(vmem_limit_bytes=20 * 1024 * 1024),
        cost_estimate=pl.CostEstimate(flops=0, bytes_accessed=propagator.size * 4, transcendentals=0),
    )(tile_blocks.T, propagator.reshape(slot_count, tile_height, cell_count))

    coded = pl.pallas_call(
        lambda *refs: tile_sums(months, *refs),
        out_shape=jax.ShapeDtypeStruct((size, own_blocks * height + SCALE_ROWS, cell_count), jnp.int16),
        in_specs=[vmem, vmem, vmem],
        out_specs=vmem,
        compiler_params=pltpu.CompilerParams(vmem_limit_bytes=20 * 1024 * 1024),
        cost_estimate=pl.CostEstimate(
            flops=2 * slot_count * height * tile_height * cell_count,
            bytes_accessed=propagator.size * 4,
            transcendentals=0,
        ),
    )(received, pick, sorted_tiles)

    owned = pl.pallas_call(
        add_parts,
        out_shape=jax.ShapeDtypeStruct((own_blocks, height, cell_count), jnp.float32),
        in_specs=[vmem],
        out_specs=vmem,
        compiler_params=pltpu.CompilerParams(vmem_limit_bytes=16 * 1024 * 1024),
    )(exchange(coded, size))
    return owned.reshape(own_blocks, tracer_count, months, cell_count)


def solution(mesh):
    in_specs = (
        P(("groups", "tm"), None, None, "cells"),
        P(("groups", "tm"), None),
        P("tm", None, None),
    )
    out_specs = P(("groups", "tm"), None, None, "cells")
    return jax.shard_map(shards, mesh=mesh, in_specs=in_specs, out_specs=out_specs, check_vma=False)
```

```python
import jax
import jax.numpy as jnp
from jax import lax
from jax.experimental import pallas as pl
from jax.experimental.pallas import tpu as pltpu
from jax.sharding import PartitionSpec as P

STEPS = 32700.0
LEVELS = 128
SMALLEST = 2.0**-126
SCALE_ROWS = 8


def centre(size):
    return size * 5 // 8


def slot_of(device, size):
    after = device - (device > centre(size)).astype(jnp.int32)
    return jnp.where(device == centre(size), 0, jnp.where(device == 0, size - 1, after))


def device_of(slot, size):
    if isinstance(slot, int):
        return centre(size) if slot == 0 else 0 if slot == size - 1 else slot + (slot >= centre(size))
    after = slot + (slot >= centre(size)).astype(jnp.int32)
    return jnp.where(slot == 0, centre(size), jnp.where(slot == size - 1, 0, after))


def exchange(value, size):
    order = [device_of(slot, size) for slot in range(size)]
    return lax.all_to_all(value, "tm", 0, 0, axis_index_groups=[order], tiled=True)


def each(count, body):
    if count <= 17:
        for index in range(count):
            body(index)
    else:
        lax.fori_loop(0, count, lambda index, carry: (body(index), carry)[1], 0)


def spread(rows_in, copies_ref, rows_ref, semaphore):
    used_rows, source_width = rows_ref.shape
    load = pltpu.make_async_copy(rows_in, rows_ref, semaphore)
    load.start()
    copies_ref[...] = jnp.zeros(copies_ref.shape, copies_ref.dtype)
    load.wait()
    for slot in range(copies_ref.shape[0]):
        copies_ref[slot, :used_rows, :source_width] = rows_ref[...]


def stage(
    size, months, own_blocks, blocks_in, tiles_in, sorted_ref, pick_ref, blocks_ref, tiles_ref, semaphores
):
    block_count = sorted_ref.shape[0] * own_blocks
    slot_count, tile_height, cell_count = tiles_ref.shape
    height = pick_ref.shape[0] // 2
    packed_rows = pick_ref.shape[1] // size
    load_blocks = pltpu.make_async_copy(blocks_in, blocks_ref, semaphores.at[0])
    load_tiles = pltpu.make_async_copy(tiles_in, tiles_ref, semaphores.at[1])
    load_blocks.start()
    load_tiles.start()

    def clear(owner):
        sorted_ref[owner] = jnp.zeros(sorted_ref.shape[1:], sorted_ref.dtype)

    each(size, clear)
    load_blocks.wait()
    first = blocks_ref[0, 0]

    def place(slot):
        which = (blocks_ref[0, slot] != first).astype(jnp.int32)
        arrival = blocks_ref[1, slot]
        start = pl.multiple_of(arrival % own_blocks * cell_count, cell_count)
        sorted_ref[arrival // own_blocks, which, :, pl.ds(start, cell_count)] = tiles_ref[slot]

    row = lax.broadcasted_iota(jnp.int32, (height, pick_ref.shape[1]), 0)
    column = lax.broadcasted_iota(jnp.int32, (height, pick_ref.shape[1]), 1)
    for which, source in enumerate((first, block_count - 1 - first)):
        start = slot_of(source // own_blocks, size) * packed_rows + source % own_blocks
        picked = column == start + row // months * own_blocks
        pick_ref[pl.ds(which * height, height)] = picked.astype(jnp.bfloat16)
    load_tiles.wait()
    each(slot_count, place)


def tile_sums(months, histories_ref, pick_ref, sorted_ref, coded_ref):
    size, packed_rows, packed_width = histories_ref.shape
    sources, tile_height, row_length = sorted_ref.shape[1:]
    cell_count = coded_ref.shape[2]
    own_blocks = row_length // cell_count
    height = pick_ref.shape[0] // sources

    column_of = lax.broadcasted_iota(jnp.int32, (packed_width, tile_height), 1) // months
    packed_column = lax.broadcasted_iota(jnp.int32, (packed_width, tile_height), 0)
    repeat_columns = (column_of == packed_column).astype(jnp.bfloat16)
    month_of_row = lax.broadcasted_iota(jnp.int32, (sources * height, tile_height), 0) % months
    month_of_column = lax.broadcasted_iota(jnp.int32, (sources * height, tile_height), 1) % months
    histories = histories_ref[...].reshape(size * packed_rows, packed_width)
    tall = jnp.dot(pick_ref[...], histories, preferred_element_type=jnp.float32)
    wide = jnp.dot(tall.astype(jnp.bfloat16), repeat_columns, preferred_element_type=jnp.float32)
    wide = jnp.where(month_of_row == month_of_column, wide, 0.0).astype(jnp.bfloat16)

    coded_rows = own_blocks * height

    def code(slot):
        parts = [
            jnp.dot(
                wide[which * height : (which + 1) * height],
                sorted_ref[device_of(slot, size), which],
                preferred_element_type=jnp.float32,
            )
            for which in range(sources)
        ]
        total = sum(parts[1:], parts[0])
        values = [total[:, block * cell_count : (block + 1) * cell_count] for block in range(own_blocks)]
        top = jnp.abs(values[0])
        for value in values[1:]:
            top = jnp.maximum(top, jnp.abs(value))
        top = jnp.max(top, axis=0, keepdims=True)
        level = jnp.ceil(jnp.log2(jnp.maximum(top, SMALLEST)) * LEVELS)
        half = jnp.exp2(level * (-0.5 / LEVELS))
        for block, value in enumerate(values):
            steps = jnp.round(value * half * (half * STEPS))
            coded_ref[slot, pl.ds(block * height, height)] = steps.astype(jnp.int32).astype(jnp.int16)
        spread = jnp.broadcast_to(level.astype(jnp.int32), (SCALE_ROWS, cell_count))
        coded_ref[slot, pl.ds(coded_rows, SCALE_ROWS)] = spread.astype(jnp.int16)

    each(size, code)


def add_parts(coded_ref, total_ref):
    size = coded_ref.shape[0]
    own_blocks, height, cell_count = total_ref.shape
    coded_rows = own_blocks * height
    total_ref[...] = jnp.zeros(total_ref.shape, total_ref.dtype)

    def add(slot):
        level = coded_ref[slot, pl.ds(coded_rows, SCALE_ROWS)].astype(jnp.int32).astype(jnp.float32)[:1]
        half = jnp.exp2(level * (0.5 / LEVELS))
        for block in range(own_blocks):
            steps = coded_ref[slot, pl.ds(block * height, height)].astype(jnp.int32)
            total_ref[block] += steps.astype(jnp.float32) * (half * (1.0 / STEPS)) * half

    each(size, add)


def shards(propagator, tile_blocks, histories):
    size = lax.axis_size("tm")
    own_blocks, tracer_count, source_width = histories.shape
    slot_count, source_width, months, cell_count = propagator.shape
    height = tracer_count * months
    tile_height = source_width * months

    used_rows = tracer_count * own_blocks
    rows = jnp.swapaxes(histories, 0, 1).reshape(used_rows, source_width)
    packed_shape = (used_rows + -used_rows % 16, source_width + -source_width % 128)
    vmem = pl.BlockSpec(memory_space=pltpu.VMEM)
    hbm = pl.BlockSpec(memory_space=pltpu.HBM)
    copies = pl.pallas_call(
        spread,
        out_shape=pltpu.VMEM((size,) + packed_shape, histories.dtype),
        in_specs=[hbm],
        out_specs=vmem,
        scratch_shapes=[pltpu.VMEM(rows.shape, rows.dtype), pltpu.SemaphoreType.DMA],
        compiler_params=pltpu.CompilerParams(vmem_limit_bytes=4 * 1024 * 1024),
    )(pltpu.with_memory_space_constraint(rows, pltpu.HBM))
    received = exchange(copies, size)

    blocks = tile_blocks.T
    tiles = propagator.reshape(slot_count, tile_height, cell_count)
    sorted_tiles, pick = pl.pallas_call(
        lambda *refs: stage(size, months, own_blocks, *refs),
        out_shape=[
            jax.ShapeDtypeStruct((size, 2, tile_height, own_blocks * cell_count), tiles.dtype),
            jax.ShapeDtypeStruct((2 * height, size * copies.shape[1]), jnp.bfloat16),
        ],
        in_specs=[hbm, hbm],
        out_specs=[vmem, vmem],
        scratch_shapes=[
            pltpu.SMEM(blocks.shape, blocks.dtype),
            pltpu.VMEM(tiles.shape, tiles.dtype),
            pltpu.SemaphoreType.DMA((2,)),
        ],
        compiler_params=pltpu.CompilerParams(vmem_limit_bytes=24 * 1024 * 1024),
        cost_estimate=pl.CostEstimate(flops=0, bytes_accessed=tiles.size * 4, transcendentals=0),
    )(
        pltpu.with_memory_space_constraint(blocks, pltpu.HBM),
        pltpu.with_memory_space_constraint(tiles, pltpu.HBM),
    )

    coded = pl.pallas_call(
        lambda *refs: tile_sums(months, *refs),
        out_shape=jax.ShapeDtypeStruct((size, own_blocks * height + SCALE_ROWS, cell_count), jnp.int16),
        in_specs=[vmem, vmem, vmem],
        out_specs=vmem,
        compiler_params=pltpu.CompilerParams(vmem_limit_bytes=20 * 1024 * 1024),
        cost_estimate=pl.CostEstimate(
            flops=2 * slot_count * height * tile_height * cell_count,
            bytes_accessed=propagator.size * 4,
            transcendentals=0,
        ),
    )(received, pick, sorted_tiles)

    owned = pl.pallas_call(
        add_parts,
        out_shape=jax.ShapeDtypeStruct((own_blocks, height, cell_count), jnp.float32),
        in_specs=[vmem],
        out_specs=vmem,
        compiler_params=pltpu.CompilerParams(vmem_limit_bytes=16 * 1024 * 1024),
    )(exchange(coded, size))
    return owned.reshape(own_blocks, tracer_count, months, cell_count)


def solution(mesh):
    in_specs = (
        P(("groups", "tm"), None, None, "cells"),
        P(("groups", "tm"), None),
        P("tm", None, None),
    )
    out_specs = P(("groups", "tm"), None, None, "cells")
    return jax.shard_map(shards, mesh=mesh, in_specs=in_specs, out_specs=out_specs, check_vma=False)
```

```python
import jax
import jax.numpy as jnp
from jax import lax
from jax.experimental import pallas as pl
from jax.experimental.pallas import tpu as pltpu
from jax.sharding import PartitionSpec as P

STEPS = 32700.0
LEVELS = 128
SMALLEST = 2.0**-126
SCALE_ROWS = 8


def centre(size):
    return size * 5 // 8


def slot_of(device, size):
    after = device - (device > centre(size)).astype(jnp.int32)
    return jnp.where(device == centre(size), 0, jnp.where(device == 0, size - 1, after))


def device_of(slot, size):
    if isinstance(slot, int):
        return centre(size) if slot == 0 else 0 if slot == size - 1 else slot + (slot >= centre(size))
    after = slot + (slot >= centre(size)).astype(jnp.int32)
    return jnp.where(slot == 0, centre(size), jnp.where(slot == size - 1, 0, after))


def exchange(value, size):
    order = [device_of(slot, size) for slot in range(size)]
    return lax.all_to_all(value, "tm", 0, 0, axis_index_groups=[order], tiled=True)


def each(count, body):
    if count <= 17:
        for index in range(count):
            body(index)
    else:
        lax.fori_loop(0, count, lambda index, carry: (body(index), carry)[1], 0)


def prepare(
    months,
    rows_in,
    blocks_in,
    tiles_in,
    copies_ref,
    sorted_ref,
    pick_ref,
    rows_ref,
    blocks_ref,
    tiles_ref,
    semaphores,
):
    size, packed_rows, packed_width = copies_ref.shape
    slot_count, tile_height, cell_count = tiles_ref.shape
    used_rows, source_width = rows_ref.shape
    own_blocks = sorted_ref.shape[3] // cell_count
    height = pick_ref.shape[0] // 2
    loads = [
        pltpu.make_async_copy(source, target, semaphores.at[index])
        for index, (source, target) in enumerate(
            [(tiles_in, tiles_ref), (blocks_in, blocks_ref), (rows_in, rows_ref)]
        )
    ]
    for load in loads:
        load.start()

    def clear(owner):
        sorted_ref[owner] = jnp.zeros(sorted_ref.shape[1:], sorted_ref.dtype)
        copies_ref[owner] = jnp.zeros(copies_ref.shape[1:], copies_ref.dtype)

    each(size, clear)
    loads[1].wait()
    first = blocks_ref[0, 0]
    row = lax.broadcasted_iota(jnp.int32, (height, pick_ref.shape[1]), 0)
    column = lax.broadcasted_iota(jnp.int32, (height, pick_ref.shape[1]), 1)
    for which, source in enumerate((first, size * own_blocks - 1 - first)):
        start = slot_of(source // own_blocks, size) * packed_rows + source % own_blocks
        picked = column == start + row // months * own_blocks
        pick_ref[pl.ds(which * height, height)] = picked.astype(jnp.bfloat16)
    loads[2].wait()

    def copy(owner):
        copies_ref[owner, :used_rows, :source_width] = rows_ref[...]

    def place(slot):
        which = (blocks_ref[0, slot] != first).astype(jnp.int32)
        arrival = blocks_ref[1, slot]
        start = pl.multiple_of(arrival % own_blocks * cell_count, cell_count)
        sorted_ref[arrival // own_blocks, which, :, pl.ds(start, cell_count)] = tiles_ref[slot]

    each(size, copy)
    loads[0].wait()
    each(slot_count, place)


def tile_sums(months, histories_ref, pick_ref, sorted_ref, coded_ref):
    size, packed_rows, packed_width = histories_ref.shape
    sources, tile_height, row_length = sorted_ref.shape[1:]
    cell_count = coded_ref.shape[2]
    own_blocks = row_length // cell_count
    height = pick_ref.shape[0] // sources

    column_of = lax.broadcasted_iota(jnp.int32, (packed_width, tile_height), 1) // months
    packed_column = lax.broadcasted_iota(jnp.int32, (packed_width, tile_height), 0)
    repeat_columns = (column_of == packed_column).astype(jnp.bfloat16)
    month_of_row = lax.broadcasted_iota(jnp.int32, (sources * height, tile_height), 0) % months
    month_of_column = lax.broadcasted_iota(jnp.int32, (sources * height, tile_height), 1) % months
    histories = histories_ref[...].reshape(size * packed_rows, packed_width)
    tall = jnp.dot(pick_ref[...], histories, preferred_element_type=jnp.float32)
    wide = jnp.dot(tall.astype(jnp.bfloat16), repeat_columns, preferred_element_type=jnp.float32)
    wide = jnp.where(month_of_row == month_of_column, wide, 0.0).astype(jnp.bfloat16)

    coded_rows = own_blocks * height

    def code(slot):
        parts = [
            jnp.dot(
                wide[which * height : (which + 1) * height],
                sorted_ref[device_of(slot, size), which],
                preferred_element_type=jnp.float32,
            )
            for which in range(sources)
        ]
        total = sum(parts[1:], parts[0])
        values = [total[:, block * cell_count : (block + 1) * cell_count] for block in range(own_blocks)]
        top = jnp.abs(values[0])
        for value in values[1:]:
            top = jnp.maximum(top, jnp.abs(value))
        top = jnp.max(top, axis=0, keepdims=True)
        level = jnp.ceil(jnp.log2(jnp.maximum(top, SMALLEST)) * LEVELS)
        half = jnp.exp2(level * (-0.5 / LEVELS))
        for block, value in enumerate(values):
            steps = jnp.round(value * half * (half * STEPS))
            coded_ref[slot, pl.ds(block * height, height)] = steps.astype(jnp.int32).astype(jnp.int16)
        spread = jnp.broadcast_to(level.astype(jnp.int32), (SCALE_ROWS, cell_count))
        coded_ref[slot, pl.ds(coded_rows, SCALE_ROWS)] = spread.astype(jnp.int16)

    each(size, code)


def add_parts(coded_ref, total_ref):
    size = coded_ref.shape[0]
    own_blocks, height, cell_count = total_ref.shape
    coded_rows = own_blocks * height
    total_ref[...] = jnp.zeros(total_ref.shape, total_ref.dtype)

    def add(slot):
        level = coded_ref[slot, pl.ds(coded_rows, SCALE_ROWS)].astype(jnp.int32).astype(jnp.float32)[:1]
        half = jnp.exp2(level * (0.5 / LEVELS))
        for block in range(own_blocks):
            steps = coded_ref[slot, pl.ds(block * height, height)].astype(jnp.int32)
            total_ref[block] += steps.astype(jnp.float32) * (half * (1.0 / STEPS)) * half

    each(size, add)


def shards(propagator, tile_blocks, histories):
    size = lax.axis_size("tm")
    own_blocks, tracer_count, source_width = histories.shape
    slot_count, source_width, months, cell_count = propagator.shape
    height = tracer_count * months
    tile_height = source_width * months

    used_rows = tracer_count * own_blocks
    packed_rows = used_rows + -used_rows % 16
    packed_width = source_width + -source_width % 128
    rows = jnp.swapaxes(histories, 0, 1).reshape(used_rows, source_width)
    blocks = tile_blocks.T
    tiles = propagator.reshape(slot_count, tile_height, cell_count)
    vmem = pl.BlockSpec(memory_space=pltpu.VMEM)
    hbm = pl.BlockSpec(memory_space=pltpu.HBM)
    copies, sorted_tiles, pick = pl.pallas_call(
        lambda *refs: prepare(months, *refs),
        out_shape=[
            jax.ShapeDtypeStruct((size, packed_rows, packed_width), rows.dtype),
            jax.ShapeDtypeStruct((size, 2, tile_height, own_blocks * cell_count), tiles.dtype),
            jax.ShapeDtypeStruct((2 * height, size * packed_rows), jnp.bfloat16),
        ],
        in_specs=[hbm, hbm, hbm],
        out_specs=[vmem, vmem, vmem],
        scratch_shapes=[
            pltpu.VMEM(rows.shape, rows.dtype),
            pltpu.SMEM(blocks.shape, blocks.dtype),
            pltpu.VMEM(tiles.shape, tiles.dtype),
            pltpu.SemaphoreType.DMA((3,)),
        ],
        compiler_params=pltpu.CompilerParams(vmem_limit_bytes=24 * 1024 * 1024),
        cost_estimate=pl.CostEstimate(flops=0, bytes_accessed=tiles.size * 4, transcendentals=0),
    )(*(pltpu.with_memory_space_constraint(value, pltpu.HBM) for value in (rows, blocks, tiles)))
    received = exchange(copies, size)

    coded = pl.pallas_call(
        lambda *refs: tile_sums(months, *refs),
        out_shape=jax.ShapeDtypeStruct((size, own_blocks * height + SCALE_ROWS, cell_count), jnp.int16),
        in_specs=[vmem, vmem, vmem],
        out_specs=vmem,
        compiler_params=pltpu.CompilerParams(vmem_limit_bytes=20 * 1024 * 1024),
        cost_estimate=pl.CostEstimate(
            flops=2 * slot_count * height * tile_height * cell_count,
            bytes_accessed=propagator.size * 4,
            transcendentals=0,
        ),
    )(received, pick, sorted_tiles)

    owned = pl.pallas_call(
        add_parts,
        out_shape=jax.ShapeDtypeStruct((own_blocks, height, cell_count), jnp.float32),
        in_specs=[vmem],
        out_specs=vmem,
        compiler_params=pltpu.CompilerParams(vmem_limit_bytes=16 * 1024 * 1024),
    )(exchange(coded, size))
    return owned.reshape(own_blocks, tracer_count, months, cell_count)


def solution(mesh):
    in_specs = (
        P(("groups", "tm"), None, None, "cells"),
        P(("groups", "tm"), None),
        P("tm", None, None),
    )
    out_specs = P(("groups", "tm"), None, None, "cells")
    return jax.shard_map(shards, mesh=mesh, in_specs=in_specs, out_specs=out_specs, check_vma=False)
```

```python
import jax
import jax.numpy as jnp
from jax import lax
from jax.experimental import pallas as pl
from jax.experimental.pallas import tpu as pltpu
from jax.sharding import PartitionSpec as P

STEPS = 32700.0
LEVELS = 128
SMALLEST = 2.0**-126
SCALE_ROWS = 8
PARTS = 6


def centre(size):
    return size * 5 // 8


def slot_of(device, size):
    after = device - (device > centre(size)).astype(jnp.int32)
    return jnp.where(device == centre(size), 0, jnp.where(device == 0, size - 1, after))


def device_of(slot, size):
    if isinstance(slot, int):
        return centre(size) if slot == 0 else 0 if slot == size - 1 else slot + (slot >= centre(size))
    after = slot + (slot >= centre(size)).astype(jnp.int32)
    return jnp.where(slot == 0, centre(size), jnp.where(slot == size - 1, 0, after))


def exchange(value, size):
    order = [device_of(slot, size) for slot in range(size)]
    return lax.all_to_all(value, "tm", 0, 0, axis_index_groups=[order], tiled=True)


def each(count, body):
    if count <= 17:
        for index in range(count):
            body(index)
    else:
        lax.fori_loop(0, count, lambda index, carry: (body(index), carry)[1], 0)


def prepare(
    months,
    rows_in,
    blocks_in,
    tiles_in,
    copies_ref,
    sorted_ref,
    pick_ref,
    rows_ref,
    blocks_ref,
    tiles_ref,
    semaphores,
):
    size, packed_rows, packed_width = copies_ref.shape
    slot_count, tile_height, cell_count = tiles_ref.shape
    used_rows, source_width = rows_ref.shape
    own_blocks = sorted_ref.shape[3] // cell_count
    height = pick_ref.shape[0] // 2
    load_blocks = pltpu.make_async_copy(blocks_in, blocks_ref, semaphores.at[0])
    load_rows = pltpu.make_async_copy(rows_in, rows_ref, semaphores.at[1])
    parts = [range(slot_count * part // PARTS, slot_count * (part + 1) // PARTS) for part in range(PARTS)]
    load_parts = [
        pltpu.make_async_copy(
            tiles_in.at[pl.ds(part.start, len(part))],
            tiles_ref.at[pl.ds(part.start, len(part))],
            semaphores.at[2 + index],
        )
        for index, part in enumerate(parts)
    ]
    load_blocks.start()
    load_rows.start()
    for load in load_parts:
        load.start()

    def clear(owner):
        sorted_ref[owner] = jnp.zeros(sorted_ref.shape[1:], sorted_ref.dtype)
        copies_ref[owner] = jnp.zeros(copies_ref.shape[1:], copies_ref.dtype)

    each(size, clear)
    load_blocks.wait()
    first = blocks_ref[0, 0]
    row = lax.broadcasted_iota(jnp.int32, (height, pick_ref.shape[1]), 0)
    column = lax.broadcasted_iota(jnp.int32, (height, pick_ref.shape[1]), 1)
    for which, source in enumerate((first, size * own_blocks - 1 - first)):
        start = slot_of(source // own_blocks, size) * packed_rows + source % own_blocks
        picked = column == start + row // months * own_blocks
        pick_ref[pl.ds(which * height, height)] = picked.astype(jnp.bfloat16)
    load_rows.wait()

    def copy(owner):
        copies_ref[owner, :used_rows, :source_width] = rows_ref[...]

    def place(slot):
        which = (blocks_ref[0, slot] != first).astype(jnp.int32)
        arrival = blocks_ref[1, slot]
        start = pl.multiple_of(arrival % own_blocks * cell_count, cell_count)
        sorted_ref[arrival // own_blocks, which, :, pl.ds(start, cell_count)] = tiles_ref[slot]

    each(size, copy)
    for load, part in zip(load_parts, parts):
        load.wait()
        each(len(part), lambda slot: place(part.start + slot))


def tile_sums(months, histories_ref, pick_ref, sorted_ref, coded_ref):
    size, packed_rows, packed_width = histories_ref.shape
    sources, tile_height, row_length = sorted_ref.shape[1:]
    cell_count = coded_ref.shape[2]
    own_blocks = row_length // cell_count
    height = pick_ref.shape[0] // sources

    column_of = lax.broadcasted_iota(jnp.int32, (packed_width, tile_height), 1) // months
    packed_column = lax.broadcasted_iota(jnp.int32, (packed_width, tile_height), 0)
    repeat_columns = (column_of == packed_column).astype(jnp.bfloat16)
    month_of_row = lax.broadcasted_iota(jnp.int32, (sources * height, tile_height), 0) % months
    month_of_column = lax.broadcasted_iota(jnp.int32, (sources * height, tile_height), 1) % months
    histories = histories_ref[...].reshape(size * packed_rows, packed_width)
    tall = jnp.dot(pick_ref[...], histories, preferred_element_type=jnp.float32)
    wide = jnp.dot(tall.astype(jnp.bfloat16), repeat_columns, preferred_element_type=jnp.float32)
    wide = jnp.where(month_of_row == month_of_column, wide, 0.0).astype(jnp.bfloat16)

    coded_rows = own_blocks * height

    def code(slot):
        parts = [
            jnp.dot(
                wide[which * height : (which + 1) * height],
                sorted_ref[device_of(slot, size), which],
                preferred_element_type=jnp.float32,
            )
            for which in range(sources)
        ]
        total = sum(parts[1:], parts[0])
        values = [total[:, block * cell_count : (block + 1) * cell_count] for block in range(own_blocks)]
        top = jnp.abs(values[0])
        for value in values[1:]:
            top = jnp.maximum(top, jnp.abs(value))
        top = jnp.max(top, axis=0, keepdims=True)
        level = jnp.ceil(jnp.log2(jnp.maximum(top, SMALLEST)) * LEVELS)
        half = jnp.exp2(level * (-0.5 / LEVELS))
        for block, value in enumerate(values):
            steps = jnp.round(value * half * (half * STEPS))
            coded_ref[slot, pl.ds(block * height, height)] = steps.astype(jnp.int32).astype(jnp.int16)
        spread = jnp.broadcast_to(level.astype(jnp.int32), (SCALE_ROWS, cell_count))
        coded_ref[slot, pl.ds(coded_rows, SCALE_ROWS)] = spread.astype(jnp.int16)

    each(size, code)


def add_parts(coded_ref, total_ref):
    size = coded_ref.shape[0]
    own_blocks, height, cell_count = total_ref.shape
    coded_rows = own_blocks * height
    total_ref[...] = jnp.zeros(total_ref.shape, total_ref.dtype)

    def add(slot):
        level = coded_ref[slot, pl.ds(coded_rows, SCALE_ROWS)].astype(jnp.int32).astype(jnp.float32)[:1]
        half = jnp.exp2(level * (0.5 / LEVELS))
        for block in range(own_blocks):
            steps = coded_ref[slot, pl.ds(block * height, height)].astype(jnp.int32)
            total_ref[block] += steps.astype(jnp.float32) * (half * (1.0 / STEPS)) * half

    each(size, add)


def shards(propagator, tile_blocks, histories):
    size = lax.axis_size("tm")
    own_blocks, tracer_count, source_width = histories.shape
    slot_count, source_width, months, cell_count = propagator.shape
    height = tracer_count * months
    tile_height = source_width * months

    used_rows = tracer_count * own_blocks
    packed_rows = used_rows + -used_rows % 16
    packed_width = source_width + -source_width % 128
    rows = jnp.swapaxes(histories, 0, 1).reshape(used_rows, source_width)
    blocks = tile_blocks.T
    tiles = propagator.reshape(slot_count, tile_height, cell_count)
    vmem = pl.BlockSpec(memory_space=pltpu.VMEM)
    hbm = pl.BlockSpec(memory_space=pltpu.HBM)
    copies, sorted_tiles, pick = pl.pallas_call(
        lambda *refs: prepare(months, *refs),
        out_shape=[
            jax.ShapeDtypeStruct((size, packed_rows, packed_width), rows.dtype),
            jax.ShapeDtypeStruct((size, 2, tile_height, own_blocks * cell_count), tiles.dtype),
            jax.ShapeDtypeStruct((2 * height, size * packed_rows), jnp.bfloat16),
        ],
        in_specs=[hbm, hbm, hbm],
        out_specs=[vmem, vmem, vmem],
        scratch_shapes=[
            pltpu.VMEM(rows.shape, rows.dtype),
            pltpu.SMEM(blocks.shape, blocks.dtype),
            pltpu.VMEM(tiles.shape, tiles.dtype),
            pltpu.SemaphoreType.DMA((2 + PARTS,)),
        ],
        compiler_params=pltpu.CompilerParams(vmem_limit_bytes=24 * 1024 * 1024),
        cost_estimate=pl.CostEstimate(flops=0, bytes_accessed=tiles.size * 4, transcendentals=0),
    )(*(pltpu.with_memory_space_constraint(value, pltpu.HBM) for value in (rows, blocks, tiles)))
    received = exchange(copies, size)

    coded = pl.pallas_call(
        lambda *refs: tile_sums(months, *refs),
        out_shape=jax.ShapeDtypeStruct((size, own_blocks * height + SCALE_ROWS, cell_count), jnp.int16),
        in_specs=[vmem, vmem, vmem],
        out_specs=vmem,
        compiler_params=pltpu.CompilerParams(vmem_limit_bytes=20 * 1024 * 1024),
        cost_estimate=pl.CostEstimate(
            flops=2 * slot_count * height * tile_height * cell_count,
            bytes_accessed=propagator.size * 4,
            transcendentals=0,
        ),
    )(received, pick, sorted_tiles)

    owned = pl.pallas_call(
        add_parts,
        out_shape=jax.ShapeDtypeStruct((own_blocks, height, cell_count), jnp.float32),
        in_specs=[vmem],
        out_specs=vmem,
        compiler_params=pltpu.CompilerParams(vmem_limit_bytes=16 * 1024 * 1024),
    )(exchange(coded, size))
    return owned.reshape(own_blocks, tracer_count, months, cell_count)


def solution(mesh):
    in_specs = (
        P(("groups", "tm"), None, None, "cells"),
        P(("groups", "tm"), None),
        P("tm", None, None),
    )
    out_specs = P(("groups", "tm"), None, None, "cells")
    return jax.shard_map(shards, mesh=mesh, in_specs=in_specs, out_specs=out_specs, check_vma=False)
```

```python
import jax
import jax.numpy as jnp
from jax import lax
from jax.experimental import pallas as pl
from jax.experimental.pallas import tpu as pltpu
from jax.sharding import PartitionSpec as P

STEPS = 32700.0
LEVELS = 128
SMALLEST = 2.0**-126
SCALE_ROWS = 8
PARTS = 6


def centre(size):
    return size * 5 // 8


def history_slot(device, size):
    rest = size + 2 - device - (device < centre(size)).astype(jnp.int32)
    return jnp.where(device == centre(size), 0, jnp.where(device < 2, 2 - device, rest))


def sums_device(slot, size):
    if isinstance(slot, int):
        return centre(size) if slot == 0 else 0 if slot == size - 1 else slot + (slot >= centre(size))
    after = slot + (slot >= centre(size)).astype(jnp.int32)
    return jnp.where(slot == 0, centre(size), jnp.where(slot == size - 1, 0, after))


def exchange(value, order):
    return lax.all_to_all(value, "tm", 0, 0, axis_index_groups=[order], tiled=True)


def each(count, body):
    if count <= 17:
        for index in range(count):
            body(index)
    else:
        lax.fori_loop(0, count, lambda index, carry: (body(index), carry)[1], 0)


def prepare(
    months,
    rows_in,
    blocks_in,
    tiles_in,
    copies_ref,
    sorted_ref,
    pick_ref,
    rows_ref,
    blocks_ref,
    tiles_ref,
    semaphores,
):
    size, packed_rows, packed_width = copies_ref.shape
    slot_count, tile_height, cell_count = tiles_ref.shape
    used_rows, source_width = rows_ref.shape
    own_blocks = sorted_ref.shape[3] // cell_count
    height = pick_ref.shape[0] // 2
    load_blocks = pltpu.make_async_copy(blocks_in, blocks_ref, semaphores.at[0])
    load_rows = pltpu.make_async_copy(rows_in, rows_ref, semaphores.at[1])
    parts = [range(slot_count * part // PARTS, slot_count * (part + 1) // PARTS) for part in range(PARTS)]
    load_parts = [
        pltpu.make_async_copy(
            tiles_in.at[pl.ds(part.start, len(part))],
            tiles_ref.at[pl.ds(part.start, len(part))],
            semaphores.at[2 + index],
        )
        for index, part in enumerate(parts)
    ]
    load_blocks.start()
    load_rows.start()
    for load in load_parts:
        load.start()

    def clear(owner):
        sorted_ref[owner] = jnp.zeros(sorted_ref.shape[1:], sorted_ref.dtype)
        copies_ref[owner] = jnp.zeros(copies_ref.shape[1:], copies_ref.dtype)

    each(size, clear)
    load_blocks.wait()
    first = blocks_ref[0, 0]
    row = lax.broadcasted_iota(jnp.int32, (height, pick_ref.shape[1]), 0)
    column = lax.broadcasted_iota(jnp.int32, (height, pick_ref.shape[1]), 1)
    for which, source in enumerate((first, size * own_blocks - 1 - first)):
        start = history_slot(source // own_blocks, size) * packed_rows + source % own_blocks
        picked = column == start + row // months * own_blocks
        pick_ref[pl.ds(which * height, height)] = picked.astype(jnp.bfloat16)
    load_rows.wait()

    def copy(owner):
        copies_ref[owner, :used_rows, :source_width] = rows_ref[...]

    def place(slot):
        which = (blocks_ref[0, slot] != first).astype(jnp.int32)
        arrival = blocks_ref[1, slot]
        start = pl.multiple_of(arrival % own_blocks * cell_count, cell_count)
        sorted_ref[arrival // own_blocks, which, :, pl.ds(start, cell_count)] = tiles_ref[slot]

    each(size, copy)
    for load, part in zip(load_parts, parts):
        load.wait()
        each(len(part), lambda slot: place(part.start + slot))


def tile_sums(months, histories_ref, pick_ref, sorted_ref, coded_ref):
    size, packed_rows, packed_width = histories_ref.shape
    sources, tile_height, row_length = sorted_ref.shape[1:]
    cell_count = coded_ref.shape[2]
    own_blocks = row_length // cell_count
    height = pick_ref.shape[0] // sources

    column_of = lax.broadcasted_iota(jnp.int32, (packed_width, tile_height), 1) // months
    packed_column = lax.broadcasted_iota(jnp.int32, (packed_width, tile_height), 0)
    repeat_columns = (column_of == packed_column).astype(jnp.bfloat16)
    month_of_row = lax.broadcasted_iota(jnp.int32, (sources * height, tile_height), 0) % months
    month_of_column = lax.broadcasted_iota(jnp.int32, (sources * height, tile_height), 1) % months
    histories = histories_ref[...].reshape(size * packed_rows, packed_width)
    tall = jnp.dot(pick_ref[...], histories, preferred_element_type=jnp.float32)
    wide = jnp.dot(tall.astype(jnp.bfloat16), repeat_columns, preferred_element_type=jnp.float32)
    wide = jnp.where(month_of_row == month_of_column, wide, 0.0).astype(jnp.bfloat16)

    coded_rows = own_blocks * height

    def code(slot):
        parts = [
            jnp.dot(
                wide[which * height : (which + 1) * height],
                sorted_ref[sums_device(slot, size), which],
                preferred_element_type=jnp.float32,
            )
            for which in range(sources)
        ]
        total = sum(parts[1:], parts[0])
        values = [total[:, block * cell_count : (block + 1) * cell_count] for block in range(own_blocks)]
        top = jnp.abs(values[0])
        for value in values[1:]:
            top = jnp.maximum(top, jnp.abs(value))
        top = jnp.max(top, axis=0, keepdims=True)
        level = jnp.ceil(jnp.log2(jnp.maximum(top, SMALLEST)) * LEVELS)
        half = jnp.exp2(level * (-0.5 / LEVELS))
        for block, value in enumerate(values):
            steps = jnp.round(value * half * (half * STEPS))
            coded_ref[slot, pl.ds(block * height, height)] = steps.astype(jnp.int32).astype(jnp.int16)
        spread = jnp.broadcast_to(level.astype(jnp.int32), (SCALE_ROWS, cell_count))
        coded_ref[slot, pl.ds(coded_rows, SCALE_ROWS)] = spread.astype(jnp.int16)

    each(size, code)


def add_parts(coded_ref, total_ref):
    size = coded_ref.shape[0]
    own_blocks, height, cell_count = total_ref.shape
    coded_rows = own_blocks * height
    total_ref[...] = jnp.zeros(total_ref.shape, total_ref.dtype)

    def add(slot):
        level = coded_ref[slot, pl.ds(coded_rows, SCALE_ROWS)].astype(jnp.int32).astype(jnp.float32)[:1]
        half = jnp.exp2(level * (0.5 / LEVELS))
        for block in range(own_blocks):
            steps = coded_ref[slot, pl.ds(block * height, height)].astype(jnp.int32)
            total_ref[block] += steps.astype(jnp.float32) * (half * (1.0 / STEPS)) * half

    each(size, add)


def shards(propagator, tile_blocks, histories):
    size = lax.axis_size("tm")
    own_blocks, tracer_count, source_width = histories.shape
    slot_count, source_width, months, cell_count = propagator.shape
    height = tracer_count * months
    tile_height = source_width * months

    used_rows = tracer_count * own_blocks
    packed_rows = used_rows + -used_rows % 16
    packed_width = source_width + -source_width % 128
    rows = jnp.swapaxes(histories, 0, 1).reshape(used_rows, source_width)
    blocks = tile_blocks.T
    tiles = propagator.reshape(slot_count, tile_height, cell_count)
    vmem = pl.BlockSpec(memory_space=pltpu.VMEM)
    hbm = pl.BlockSpec(memory_space=pltpu.HBM)
    copies, sorted_tiles, pick = pl.pallas_call(
        lambda *refs: prepare(months, *refs),
        out_shape=[
            jax.ShapeDtypeStruct((size, packed_rows, packed_width), rows.dtype),
            jax.ShapeDtypeStruct((size, 2, tile_height, own_blocks * cell_count), tiles.dtype),
            jax.ShapeDtypeStruct((2 * height, size * packed_rows), jnp.bfloat16),
        ],
        in_specs=[hbm, hbm, hbm],
        out_specs=[vmem, vmem, vmem],
        scratch_shapes=[
            pltpu.VMEM(rows.shape, rows.dtype),
            pltpu.SMEM(blocks.shape, blocks.dtype),
            pltpu.VMEM(tiles.shape, tiles.dtype),
            pltpu.SemaphoreType.DMA((2 + PARTS,)),
        ],
        compiler_params=pltpu.CompilerParams(vmem_limit_bytes=24 * 1024 * 1024),
        cost_estimate=pl.CostEstimate(flops=0, bytes_accessed=tiles.size * 4, transcendentals=0),
    )(*(pltpu.with_memory_space_constraint(value, pltpu.HBM) for value in (rows, blocks, tiles)))
    near = [centre(size), 1, 0]
    received = exchange(copies, near + [device for device in range(size - 1, 1, -1) if device not in near])

    coded = pl.pallas_call(
        lambda *refs: tile_sums(months, *refs),
        out_shape=jax.ShapeDtypeStruct((size, own_blocks * height + SCALE_ROWS, cell_count), jnp.int16),
        in_specs=[vmem, vmem, vmem],
        out_specs=vmem,
        compiler_params=pltpu.CompilerParams(vmem_limit_bytes=20 * 1024 * 1024),
        cost_estimate=pl.CostEstimate(
            flops=2 * slot_count * height * tile_height * cell_count,
            bytes_accessed=propagator.size * 4,
            transcendentals=0,
        ),
    )(received, pick, sorted_tiles)

    owned = pl.pallas_call(
        add_parts,
        out_shape=jax.ShapeDtypeStruct((own_blocks, height, cell_count), jnp.float32),
        in_specs=[vmem],
        out_specs=vmem,
        compiler_params=pltpu.CompilerParams(vmem_limit_bytes=16 * 1024 * 1024),
    )(exchange(coded, [sums_device(slot, size) for slot in range(size)]))
    return owned.reshape(own_blocks, tracer_count, months, cell_count)


def solution(mesh):
    in_specs = (
        P(("groups", "tm"), None, None, "cells"),
        P(("groups", "tm"), None),
        P("tm", None, None),
    )
    out_specs = P(("groups", "tm"), None, None, "cells")
    return jax.shard_map(shards, mesh=mesh, in_specs=in_specs, out_specs=out_specs, check_vma=False)
```

```python
import jax
import jax.numpy as jnp
from jax import lax
from jax.experimental import pallas as pl
from jax.experimental.pallas import tpu as pltpu
from jax.sharding import PartitionSpec as P

STEPS = 32700.0
LEVELS = 128
SMALLEST = 2.0**-126
SCALE_ROWS = 8
PARTS = 4


def centre(size):
    return size * 5 // 8


def history_slot(device, size):
    after = device - (device > centre(size)).astype(jnp.int32)
    return jnp.where(device == centre(size), 0, jnp.where(device == 0, size - 1, after))


def sums_device(slot, size):
    if isinstance(slot, int):
        return centre(size) if slot == 0 else size - slot - (size - slot <= centre(size))
    after = size - slot - (size - slot <= centre(size)).astype(jnp.int32)
    return jnp.where(slot == 0, centre(size), after)


def exchange(value, order):
    return lax.all_to_all(value, "tm", 0, 0, axis_index_groups=[order], tiled=True)


def each(count, body):
    if count <= 17:
        for index in range(count):
            body(index)
    else:
        lax.fori_loop(0, count, lambda index, carry: (body(index), carry)[1], 0)


def prepare(
    months,
    rows_in,
    blocks_in,
    tiles_in,
    copies_ref,
    sorted_ref,
    pick_ref,
    rows_ref,
    blocks_ref,
    tiles_ref,
    semaphores,
):
    size, packed_rows, packed_width = copies_ref.shape
    slot_count, tile_height, cell_count = tiles_ref.shape
    used_rows, source_width = rows_ref.shape
    own_blocks = sorted_ref.shape[3] // cell_count
    height = pick_ref.shape[0] // 2
    load_blocks = pltpu.make_async_copy(blocks_in, blocks_ref, semaphores.at[0])
    load_rows = pltpu.make_async_copy(rows_in, rows_ref, semaphores.at[1])
    ends = [slot_count * (part * (part + 1)) // (PARTS * (PARTS + 1)) for part in range(PARTS + 1)]
    parts = [range(start, end) for start, end in zip(ends, ends[1:])]
    load_parts = [
        pltpu.make_async_copy(
            tiles_in.at[pl.ds(part.start, len(part))],
            tiles_ref.at[pl.ds(part.start, len(part))],
            semaphores.at[2 + index],
        )
        for index, part in enumerate(parts)
    ]
    load_blocks.start()
    load_rows.start()
    for load in load_parts:
        load.start()

    def clear(owner):
        sorted_ref[owner] = jnp.zeros(sorted_ref.shape[1:], sorted_ref.dtype)
        copies_ref[owner] = jnp.zeros(copies_ref.shape[1:], copies_ref.dtype)

    each(size, clear)
    load_blocks.wait()
    first = blocks_ref[0, 0]
    row = lax.broadcasted_iota(jnp.int32, (height, pick_ref.shape[1]), 0)
    column = lax.broadcasted_iota(jnp.int32, (height, pick_ref.shape[1]), 1)
    for which, source in enumerate((first, size * own_blocks - 1 - first)):
        start = history_slot(source // own_blocks, size) * packed_rows + source % own_blocks
        picked = column == start + row // months * own_blocks
        pick_ref[pl.ds(which * height, height)] = picked.astype(jnp.bfloat16)
    load_rows.wait()

    def copy(owner):
        copies_ref[owner, :used_rows, :source_width] = rows_ref[...]

    def place(slot):
        which = (blocks_ref[0, slot] != first).astype(jnp.int32)
        arrival = blocks_ref[1, slot]
        start = pl.multiple_of(arrival % own_blocks * cell_count, cell_count)
        sorted_ref[arrival // own_blocks, which, :, pl.ds(start, cell_count)] = tiles_ref[slot]

    each(size, copy)
    for load, part in zip(load_parts, parts):
        load.wait()
        each(len(part), lambda slot: place(part.start + slot))


def tile_sums(months, histories_ref, pick_ref, sorted_ref, coded_ref):
    size, packed_rows, packed_width = histories_ref.shape
    sources, tile_height, row_length = sorted_ref.shape[1:]
    cell_count = coded_ref.shape[2]
    own_blocks = row_length // cell_count
    height = pick_ref.shape[0] // sources

    column_of = lax.broadcasted_iota(jnp.int32, (packed_width, tile_height), 1) // months
    packed_column = lax.broadcasted_iota(jnp.int32, (packed_width, tile_height), 0)
    repeat_columns = (column_of == packed_column).astype(jnp.bfloat16)
    month_of_row = lax.broadcasted_iota(jnp.int32, (sources * height, tile_height), 0) % months
    month_of_column = lax.broadcasted_iota(jnp.int32, (sources * height, tile_height), 1) % months
    histories = histories_ref[...].reshape(size * packed_rows, packed_width)
    tall = jnp.dot(pick_ref[...], histories, preferred_element_type=jnp.float32)
    wide = jnp.dot(tall.astype(jnp.bfloat16), repeat_columns, preferred_element_type=jnp.float32)
    wide = jnp.where(month_of_row == month_of_column, wide, 0.0).astype(jnp.bfloat16)

    coded_rows = own_blocks * height

    def code(slot):
        parts = [
            jnp.dot(
                wide[which * height : (which + 1) * height],
                sorted_ref[sums_device(slot, size), which],
                preferred_element_type=jnp.float32,
            )
            for which in range(sources)
        ]
        total = sum(parts[1:], parts[0])
        values = [total[:, block * cell_count : (block + 1) * cell_count] for block in range(own_blocks)]
        top = jnp.abs(values[0])
        for value in values[1:]:
            top = jnp.maximum(top, jnp.abs(value))
        top = jnp.max(top, axis=0, keepdims=True)
        level = jnp.ceil(jnp.log2(jnp.maximum(top, SMALLEST)) * LEVELS)
        half = jnp.exp2(level * (-0.5 / LEVELS))
        for block, value in enumerate(values):
            steps = jnp.round(value * half * (half * STEPS))
            coded_ref[slot, pl.ds(block * height, height)] = steps.astype(jnp.int32).astype(jnp.int16)
        spread = jnp.broadcast_to(level.astype(jnp.int32), (SCALE_ROWS, cell_count))
        coded_ref[slot, pl.ds(coded_rows, SCALE_ROWS)] = spread.astype(jnp.int16)

    each(size, code)


def add_parts(coded_ref, total_ref):
    size = coded_ref.shape[0]
    own_blocks, height, cell_count = total_ref.shape
    coded_rows = own_blocks * height
    total_ref[...] = jnp.zeros(total_ref.shape, total_ref.dtype)

    def add(slot):
        level = coded_ref[slot, pl.ds(coded_rows, SCALE_ROWS)].astype(jnp.int32).astype(jnp.float32)[:1]
        half = jnp.exp2(level * (0.5 / LEVELS))
        for block in range(own_blocks):
            steps = coded_ref[slot, pl.ds(block * height, height)].astype(jnp.int32)
            total_ref[block] += steps.astype(jnp.float32) * (half * (1.0 / STEPS)) * half

    each(size, add)


def shards(propagator, tile_blocks, histories):
    size = lax.axis_size("tm")
    own_blocks, tracer_count, source_width = histories.shape
    slot_count, source_width, months, cell_count = propagator.shape
    height = tracer_count * months
    tile_height = source_width * months

    used_rows = tracer_count * own_blocks
    packed_rows = used_rows + -used_rows % 16
    packed_width = source_width + -source_width % 128
    rows = jnp.swapaxes(histories, 0, 1).reshape(used_rows, source_width)
    blocks = tile_blocks.T
    tiles = propagator.reshape(slot_count, tile_height, cell_count)
    vmem = pl.BlockSpec(memory_space=pltpu.VMEM)
    hbm = pl.BlockSpec(memory_space=pltpu.HBM)
    copies, sorted_tiles, pick = pl.pallas_call(
        lambda *refs: prepare(months, *refs),
        out_shape=[
            jax.ShapeDtypeStruct((size, packed_rows, packed_width), rows.dtype),
            jax.ShapeDtypeStruct((size, 2, tile_height, own_blocks * cell_count), tiles.dtype),
            jax.ShapeDtypeStruct((2 * height, size * packed_rows), jnp.bfloat16),
        ],
        in_specs=[hbm, hbm, hbm],
        out_specs=[vmem, vmem, vmem],
        scratch_shapes=[
            pltpu.VMEM(rows.shape, rows.dtype),
            pltpu.SMEM(blocks.shape, blocks.dtype),
            pltpu.VMEM(tiles.shape, tiles.dtype),
            pltpu.SemaphoreType.DMA((2 + PARTS,)),
        ],
        compiler_params=pltpu.CompilerParams(vmem_limit_bytes=24 * 1024 * 1024),
        cost_estimate=pl.CostEstimate(flops=0, bytes_accessed=tiles.size * 4, transcendentals=0),
    )(*(pltpu.with_memory_space_constraint(value, pltpu.HBM) for value in (rows, blocks, tiles)))
    inner = [device for device in range(1, size) if device != centre(size)]
    received = exchange(copies, [centre(size)] + inner + [0])

    coded = pl.pallas_call(
        lambda *refs: tile_sums(months, *refs),
        out_shape=jax.ShapeDtypeStruct((size, own_blocks * height + SCALE_ROWS, cell_count), jnp.int16),
        in_specs=[vmem, vmem, vmem],
        out_specs=vmem,
        compiler_params=pltpu.CompilerParams(vmem_limit_bytes=20 * 1024 * 1024),
        cost_estimate=pl.CostEstimate(
            flops=2 * slot_count * height * tile_height * cell_count,
            bytes_accessed=propagator.size * 4,
            transcendentals=0,
        ),
    )(received, pick, sorted_tiles)

    owned = pl.pallas_call(
        add_parts,
        out_shape=jax.ShapeDtypeStruct((own_blocks, height, cell_count), jnp.float32),
        in_specs=[vmem],
        out_specs=vmem,
        compiler_params=pltpu.CompilerParams(vmem_limit_bytes=16 * 1024 * 1024),
    )(exchange(coded, [sums_device(slot, size) for slot in range(size)]))
    return owned.reshape(own_blocks, tracer_count, months, cell_count)


def solution(mesh):
    in_specs = (
        P(("groups", "tm"), None, None, "cells"),
        P(("groups", "tm"), None),
        P("tm", None, None),
    )
    out_specs = P(("groups", "tm"), None, None, "cells")
    return jax.shard_map(shards, mesh=mesh, in_specs=in_specs, out_specs=out_specs, check_vma=False)
```

```python
import jax
import jax.numpy as jnp
from jax import lax
from jax.experimental import pallas as pl
from jax.experimental.pallas import tpu as pltpu
from jax.sharding import PartitionSpec as P

STEPS = 32700.0
LEVELS = 128
SMALLEST = 2.0**-126
SCALE_ROWS = 8
PARTS = 4


def centre(size):
    return size * 5 // 8


def history_slot(device, size):
    after = device - (device > centre(size)).astype(jnp.int32)
    return jnp.where(device == centre(size), 0, jnp.where(device == 0, size - 1, after))


def sums_device(slot, size):
    if isinstance(slot, int):
        return centre(size) if slot == 0 else size - slot - (size - slot <= centre(size))
    after = size - slot - (size - slot <= centre(size)).astype(jnp.int32)
    return jnp.where(slot == 0, centre(size), after)


def exchange(value, order):
    return lax.all_to_all(value, "tm", 0, 0, axis_index_groups=[order], tiled=True)


def each(count, body):
    if count <= 17:
        for index in range(count):
            body(index)
    else:
        lax.fori_loop(0, count, lambda index, carry: (body(index), carry)[1], 0)


def prepare(
    months,
    rows_in,
    blocks_in,
    tiles_in,
    copies_ref,
    sorted_ref,
    pick_ref,
    rows_ref,
    blocks_ref,
    tiles_ref,
    semaphores,
):
    size, packed_rows, packed_width = copies_ref.shape
    slot_count, tile_height, cell_count = tiles_ref.shape
    used_rows, source_width = rows_ref.shape
    own_blocks = sorted_ref.shape[2]
    height = pick_ref.shape[0] // 2
    load_blocks = pltpu.make_async_copy(blocks_in, blocks_ref, semaphores.at[0])
    load_rows = pltpu.make_async_copy(rows_in, rows_ref, semaphores.at[1])
    ends = [slot_count * (part * (part + 1)) // (PARTS * (PARTS + 1)) for part in range(PARTS + 1)]
    parts = [range(start, end) for start, end in zip(ends, ends[1:])]
    load_parts = [
        pltpu.make_async_copy(
            tiles_in.at[pl.ds(part.start, len(part))],
            tiles_ref.at[pl.ds(part.start, len(part))],
            semaphores.at[2 + index],
        )
        for index, part in enumerate(parts)
    ]
    load_blocks.start()
    load_rows.start()
    for load in load_parts:
        load.start()

    def clear(owner):
        sorted_ref[owner] = jnp.zeros(sorted_ref.shape[1:], sorted_ref.dtype)
        copies_ref[owner] = jnp.zeros(copies_ref.shape[1:], copies_ref.dtype)

    each(size, clear)
    load_blocks.wait()
    first = blocks_ref[0, 0]
    row = lax.broadcasted_iota(jnp.int32, (height, pick_ref.shape[1]), 0)
    column = lax.broadcasted_iota(jnp.int32, (height, pick_ref.shape[1]), 1)
    for which, source in enumerate((first, size * own_blocks - 1 - first)):
        start = history_slot(source // own_blocks, size) * packed_rows + source % own_blocks
        picked = column == start + row // months * own_blocks
        pick_ref[pl.ds(which * height, height)] = picked.astype(jnp.bfloat16)
    load_rows.wait()

    def copy(owner):
        copies_ref[owner, :used_rows, :source_width] = rows_ref[...]

    def place(slot):
        which = (blocks_ref[0, slot] != first).astype(jnp.int32)
        arrival = blocks_ref[1, slot]
        sorted_ref[arrival // own_blocks, which, arrival % own_blocks] = tiles_ref[slot]

    each(size, copy)
    for load, part in zip(load_parts, parts):
        load.wait()
        each(len(part), lambda slot: place(part.start + slot))


def tile_sums(months, histories_ref, pick_ref, sorted_ref, coded_ref):
    size, packed_rows, packed_width = histories_ref.shape
    sources, own_blocks, tile_height, cell_count = sorted_ref.shape[1:]
    height = pick_ref.shape[0] // sources

    column_of = lax.broadcasted_iota(jnp.int32, (packed_width, tile_height), 1) // months
    packed_column = lax.broadcasted_iota(jnp.int32, (packed_width, tile_height), 0)
    repeat_columns = (column_of == packed_column).astype(jnp.bfloat16)
    month_of_row = lax.broadcasted_iota(jnp.int32, (sources * height, tile_height), 0) % months
    month_of_column = lax.broadcasted_iota(jnp.int32, (sources * height, tile_height), 1) % months
    histories = histories_ref[...].reshape(size * packed_rows, packed_width)
    tall = jnp.dot(pick_ref[...], histories, preferred_element_type=jnp.float32)
    wide = jnp.dot(tall.astype(jnp.bfloat16), repeat_columns, preferred_element_type=jnp.float32)
    wide = jnp.where(month_of_row == month_of_column, wide, 0.0).astype(jnp.bfloat16)

    coded_rows = own_blocks * height

    def code(slot):
        owner = sums_device(slot, size)
        parts = [
            jnp.dot(
                wide[which * height : (which + 1) * height],
                jnp.concatenate([sorted_ref[owner, which, block] for block in range(own_blocks)], axis=1),
                preferred_element_type=jnp.float32,
            )
            for which in range(sources)
        ]
        total = sum(parts[1:], parts[0])
        values = [total[:, block * cell_count : (block + 1) * cell_count] for block in range(own_blocks)]
        top = jnp.abs(values[0])
        for value in values[1:]:
            top = jnp.maximum(top, jnp.abs(value))
        top = jnp.max(top, axis=0, keepdims=True)
        level = jnp.ceil(jnp.log2(jnp.maximum(top, SMALLEST)) * LEVELS)
        half = jnp.exp2(level * (-0.5 / LEVELS))
        for block, value in enumerate(values):
            steps = jnp.round(value * half * (half * STEPS))
            coded_ref[slot, pl.ds(block * height, height)] = steps.astype(jnp.int32).astype(jnp.int16)
        spread = jnp.broadcast_to(level.astype(jnp.int32), (SCALE_ROWS, cell_count))
        coded_ref[slot, pl.ds(coded_rows, SCALE_ROWS)] = spread.astype(jnp.int16)

    each(size, code)


def add_parts(coded_ref, total_ref):
    size = coded_ref.shape[0]
    own_blocks, height, cell_count = total_ref.shape
    coded_rows = own_blocks * height
    total_ref[...] = jnp.zeros(total_ref.shape, total_ref.dtype)

    def add(slot):
        level = coded_ref[slot, pl.ds(coded_rows, SCALE_ROWS)].astype(jnp.int32).astype(jnp.float32)[:1]
        half = jnp.exp2(level * (0.5 / LEVELS))
        for block in range(own_blocks):
            steps = coded_ref[slot, pl.ds(block * height, height)].astype(jnp.int32)
            total_ref[block] += steps.astype(jnp.float32) * (half * (1.0 / STEPS)) * half

    each(size, add)


def shards(propagator, tile_blocks, histories):
    size = lax.axis_size("tm")
    own_blocks, tracer_count, source_width = histories.shape
    slot_count, source_width, months, cell_count = propagator.shape
    height = tracer_count * months
    tile_height = source_width * months

    used_rows = tracer_count * own_blocks
    packed_rows = used_rows + -used_rows % 16
    packed_width = source_width + -source_width % 128
    rows = jnp.swapaxes(histories, 0, 1).reshape(used_rows, source_width)
    blocks = tile_blocks.T
    tiles = propagator.reshape(slot_count, tile_height, cell_count)
    vmem = pl.BlockSpec(memory_space=pltpu.VMEM)
    hbm = pl.BlockSpec(memory_space=pltpu.HBM)
    copies, sorted_tiles, pick = pl.pallas_call(
        lambda *refs: prepare(months, *refs),
        out_shape=[
            jax.ShapeDtypeStruct((size, packed_rows, packed_width), rows.dtype),
            jax.ShapeDtypeStruct((size, 2, own_blocks, tile_height, cell_count), tiles.dtype),
            jax.ShapeDtypeStruct((2 * height, size * packed_rows), jnp.bfloat16),
        ],
        in_specs=[hbm, hbm, hbm],
        out_specs=[vmem, vmem, vmem],
        scratch_shapes=[
            pltpu.VMEM(rows.shape, rows.dtype),
            pltpu.SMEM(blocks.shape, blocks.dtype),
            pltpu.VMEM(tiles.shape, tiles.dtype),
            pltpu.SemaphoreType.DMA((2 + PARTS,)),
        ],
        compiler_params=pltpu.CompilerParams(vmem_limit_bytes=24 * 1024 * 1024),
        cost_estimate=pl.CostEstimate(flops=0, bytes_accessed=tiles.size * 4, transcendentals=0),
    )(*(pltpu.with_memory_space_constraint(value, pltpu.HBM) for value in (rows, blocks, tiles)))
    inner = [device for device in range(1, size) if device != centre(size)]
    received = exchange(copies, [centre(size)] + inner + [0])

    coded = pl.pallas_call(
        lambda *refs: tile_sums(months, *refs),
        out_shape=jax.ShapeDtypeStruct((size, own_blocks * height + SCALE_ROWS, cell_count), jnp.int16),
        in_specs=[vmem, vmem, vmem],
        out_specs=vmem,
        compiler_params=pltpu.CompilerParams(vmem_limit_bytes=20 * 1024 * 1024),
        cost_estimate=pl.CostEstimate(
            flops=2 * slot_count * height * tile_height * cell_count,
            bytes_accessed=propagator.size * 4,
            transcendentals=0,
        ),
    )(received, pick, sorted_tiles)

    owned = pl.pallas_call(
        add_parts,
        out_shape=jax.ShapeDtypeStruct((own_blocks, height, cell_count), jnp.float32),
        in_specs=[vmem],
        out_specs=vmem,
        compiler_params=pltpu.CompilerParams(vmem_limit_bytes=16 * 1024 * 1024),
    )(exchange(coded, [sums_device(slot, size) for slot in range(size)]))
    return owned.reshape(own_blocks, tracer_count, months, cell_count)


def solution(mesh):
    in_specs = (
        P(("groups", "tm"), None, None, "cells"),
        P(("groups", "tm"), None),
        P("tm", None, None),
    )
    out_specs = P(("groups", "tm"), None, None, "cells")
    return jax.shard_map(shards, mesh=mesh, in_specs=in_specs, out_specs=out_specs, check_vma=False)
```

```python
import jax
import jax.numpy as jnp
from jax import lax
from jax.experimental import pallas as pl
from jax.experimental.pallas import tpu as pltpu
from jax.sharding import PartitionSpec as P

STEPS = 32700.0
LEVELS = 128
SMALLEST = 2.0**-126
SCALE_ROWS = 8
PARTS = 4


def centre(size):
    return size * 5 // 8


def history_slot(device, size):
    after = device - (device > centre(size)).astype(jnp.int32)
    return jnp.where(device == centre(size), 0, jnp.where(device == 0, size - 1, after))


def sums_device(slot, size):
    if isinstance(slot, int):
        return centre(size) if slot == 0 else size - slot - (size - slot <= centre(size))
    after = size - slot - (size - slot <= centre(size)).astype(jnp.int32)
    return jnp.where(slot == 0, centre(size), after)


def exchange(value, order):
    return lax.all_to_all(value, "tm", 0, 0, axis_index_groups=[order], tiled=True)


def each(count, body):
    if count <= 17:
        for index in range(count):
            body(index)
    else:
        lax.fori_loop(0, count, lambda index, carry: (body(index), carry)[1], 0)


def prepare(
    months,
    rows_in,
    blocks_in,
    tiles_in,
    copies_ref,
    sorted_ref,
    pick_ref,
    rows_ref,
    blocks_ref,
    tiles_ref,
    semaphores,
):
    size, packed_rows, packed_width = copies_ref.shape
    slot_count, tile_height, cell_count = tiles_ref.shape
    used_rows, source_width = rows_ref.shape
    own_blocks = sorted_ref.shape[3] // cell_count
    height = pick_ref.shape[0] // 2
    load_blocks = pltpu.make_async_copy(blocks_in, blocks_ref, semaphores.at[0])
    load_rows = pltpu.make_async_copy(rows_in, rows_ref, semaphores.at[1])
    ends = [slot_count * part // PARTS for part in range(PARTS + 1)]
    parts = [range(start, end) for start, end in zip(ends, ends[1:])]
    load_parts = [
        pltpu.make_async_copy(
            tiles_in.at[pl.ds(part.start, len(part))],
            tiles_ref.at[pl.ds(part.start, len(part))],
            semaphores.at[2 + index],
        )
        for index, part in enumerate(parts)
    ]
    load_blocks.start()
    load_rows.start()
    for index, load in enumerate(load_parts):
        load.start(priority=index % 2)

    def clear(owner):
        sorted_ref[owner] = jnp.zeros(sorted_ref.shape[1:], sorted_ref.dtype)
        copies_ref[owner] = jnp.zeros(copies_ref.shape[1:], copies_ref.dtype)

    each(size, clear)
    load_blocks.wait()
    first = blocks_ref[0, 0]
    row = lax.broadcasted_iota(jnp.int32, (height, pick_ref.shape[1]), 0)
    column = lax.broadcasted_iota(jnp.int32, (height, pick_ref.shape[1]), 1)
    for which, source in enumerate((first, size * own_blocks - 1 - first)):
        start = history_slot(source // own_blocks, size) * packed_rows + source % own_blocks
        picked = column == start + row // months * own_blocks
        pick_ref[pl.ds(which * height, height)] = picked.astype(jnp.bfloat16)
    load_rows.wait()

    def copy(owner):
        copies_ref[owner, :used_rows, :source_width] = rows_ref[...]

    def place(slot):
        which = (blocks_ref[0, slot] != first).astype(jnp.int32)
        arrival = blocks_ref[1, slot]
        start = pl.multiple_of(arrival % own_blocks * cell_count, cell_count)
        sorted_ref[arrival // own_blocks, which, :, pl.ds(start, cell_count)] = tiles_ref[slot]

    each(size, copy)
    for load, part in zip(load_parts, parts):
        load.wait()
        each(len(part), lambda slot: place(part.start + slot))


def tile_sums(months, histories_ref, pick_ref, sorted_ref, coded_ref):
    size, packed_rows, packed_width = histories_ref.shape
    sources, tile_height, row_length = sorted_ref.shape[1:]
    cell_count = coded_ref.shape[2]
    own_blocks = row_length // cell_count
    height = pick_ref.shape[0] // sources

    column_of = lax.broadcasted_iota(jnp.int32, (packed_width, tile_height), 1) // months
    packed_column = lax.broadcasted_iota(jnp.int32, (packed_width, tile_height), 0)
    repeat_columns = (column_of == packed_column).astype(jnp.bfloat16)
    month_of_row = lax.broadcasted_iota(jnp.int32, (sources * height, tile_height), 0) % months
    month_of_column = lax.broadcasted_iota(jnp.int32, (sources * height, tile_height), 1) % months
    histories = histories_ref[...].reshape(size * packed_rows, packed_width)
    tall = jnp.dot(pick_ref[...], histories, preferred_element_type=jnp.float32)
    wide = jnp.dot(tall.astype(jnp.bfloat16), repeat_columns, preferred_element_type=jnp.float32)
    wide = jnp.where(month_of_row == month_of_column, wide, 0.0).astype(jnp.bfloat16)

    coded_rows = own_blocks * height

    def code(slot):
        parts = [
            jnp.dot(
                wide[which * height : (which + 1) * height],
                sorted_ref[sums_device(slot, size), which],
                preferred_element_type=jnp.float32,
            )
            for which in range(sources)
        ]
        total = sum(parts[1:], parts[0])
        values = [total[:, block * cell_count : (block + 1) * cell_count] for block in range(own_blocks)]
        top = jnp.abs(values[0])
        for value in values[1:]:
            top = jnp.maximum(top, jnp.abs(value))
        top = jnp.max(top, axis=0, keepdims=True)
        level = jnp.ceil(jnp.log2(jnp.maximum(top, SMALLEST)) * LEVELS)
        half = jnp.exp2(level * (-0.5 / LEVELS))
        for block, value in enumerate(values):
            steps = jnp.round(value * half * (half * STEPS))
            coded_ref[slot, pl.ds(block * height, height)] = steps.astype(jnp.int32).astype(jnp.int16)
        spread = jnp.broadcast_to(level.astype(jnp.int32), (SCALE_ROWS, cell_count))
        coded_ref[slot, pl.ds(coded_rows, SCALE_ROWS)] = spread.astype(jnp.int16)

    each(size, code)


def add_parts(coded_ref, total_ref):
    size = coded_ref.shape[0]
    own_blocks, height, cell_count = total_ref.shape
    coded_rows = own_blocks * height
    total_ref[...] = jnp.zeros(total_ref.shape, total_ref.dtype)

    def add(slot):
        level = coded_ref[slot, pl.ds(coded_rows, SCALE_ROWS)].astype(jnp.int32).astype(jnp.float32)[:1]
        half = jnp.exp2(level * (0.5 / LEVELS))
        for block in range(own_blocks):
            steps = coded_ref[slot, pl.ds(block * height, height)].astype(jnp.int32)
            total_ref[block] += steps.astype(jnp.float32) * (half * (1.0 / STEPS)) * half

    each(size, add)


def shards(propagator, tile_blocks, histories):
    size = lax.axis_size("tm")
    own_blocks, tracer_count, source_width = histories.shape
    slot_count, source_width, months, cell_count = propagator.shape
    height = tracer_count * months
    tile_height = source_width * months

    used_rows = tracer_count * own_blocks
    packed_rows = used_rows + -used_rows % 16
    packed_width = source_width + -source_width % 128
    rows = jnp.swapaxes(histories, 0, 1).reshape(used_rows, source_width)
    blocks = tile_blocks.T
    tiles = propagator.reshape(slot_count, tile_height, cell_count)
    vmem = pl.BlockSpec(memory_space=pltpu.VMEM)
    hbm = pl.BlockSpec(memory_space=pltpu.HBM)
    copies, sorted_tiles, pick = pl.pallas_call(
        lambda *refs: prepare(months, *refs),
        out_shape=[
            jax.ShapeDtypeStruct((size, packed_rows, packed_width), rows.dtype),
            jax.ShapeDtypeStruct((size, 2, tile_height, own_blocks * cell_count), tiles.dtype),
            jax.ShapeDtypeStruct((2 * height, size * packed_rows), jnp.bfloat16),
        ],
        in_specs=[hbm, hbm, hbm],
        out_specs=[vmem, vmem, vmem],
        scratch_shapes=[
            pltpu.VMEM(rows.shape, rows.dtype),
            pltpu.SMEM(blocks.shape, blocks.dtype),
            pltpu.VMEM(tiles.shape, tiles.dtype),
            pltpu.SemaphoreType.DMA((2 + PARTS,)),
        ],
        compiler_params=pltpu.CompilerParams(vmem_limit_bytes=24 * 1024 * 1024),
        cost_estimate=pl.CostEstimate(flops=0, bytes_accessed=tiles.size * 4, transcendentals=0),
    )(*(pltpu.with_memory_space_constraint(value, pltpu.HBM) for value in (rows, blocks, tiles)))
    inner = [device for device in range(1, size) if device != centre(size)]
    received = exchange(copies, [centre(size)] + inner + [0])

    coded = pl.pallas_call(
        lambda *refs: tile_sums(months, *refs),
        out_shape=jax.ShapeDtypeStruct((size, own_blocks * height + SCALE_ROWS, cell_count), jnp.int16),
        in_specs=[vmem, vmem, vmem],
        out_specs=vmem,
        compiler_params=pltpu.CompilerParams(vmem_limit_bytes=20 * 1024 * 1024),
        cost_estimate=pl.CostEstimate(
            flops=2 * slot_count * height * tile_height * cell_count,
            bytes_accessed=propagator.size * 4,
            transcendentals=0,
        ),
    )(received, pick, sorted_tiles)

    owned = pl.pallas_call(
        add_parts,
        out_shape=jax.ShapeDtypeStruct((own_blocks, height, cell_count), jnp.float32),
        in_specs=[vmem],
        out_specs=vmem,
        compiler_params=pltpu.CompilerParams(vmem_limit_bytes=16 * 1024 * 1024),
    )(exchange(coded, [sums_device(slot, size) for slot in range(size)]))
    return owned.reshape(own_blocks, tracer_count, months, cell_count)


def solution(mesh):
    in_specs = (
        P(("groups", "tm"), None, None, "cells"),
        P(("groups", "tm"), None),
        P("tm", None, None),
    )
    out_specs = P(("groups", "tm"), None, None, "cells")
    return jax.shard_map(shards, mesh=mesh, in_specs=in_specs, out_specs=out_specs, check_vma=False)
```

```python
import jax
import jax.numpy as jnp
from jax import lax
from jax.experimental import pallas as pl
from jax.experimental.pallas import tpu as pltpu
from jax.sharding import PartitionSpec as P

STEPS = 32700.0
LEVELS = 128
SMALLEST = 2.0**-126
SCALE_ROWS = 8
PARTS = 4
WRITTEN_OUT = 17


def centre(size):
    return size * 5 // 8


def history_slot(device, size):
    after = device - (device > centre(size)).astype(jnp.int32)
    return jnp.where(device == centre(size), 0, jnp.where(device == 0, size - 1, after))


def sums_device(slot, size):
    if isinstance(slot, int):
        return centre(size) if slot == 0 else size - slot - (size - slot <= centre(size))
    after = size - slot - (size - slot <= centre(size)).astype(jnp.int32)
    return jnp.where(slot == 0, centre(size), after)


def exchange(value, order):
    return lax.all_to_all(value, "tm", 0, 0, axis_index_groups=[order], tiled=True)


def each(count, body):
    if count <= WRITTEN_OUT:
        for index in range(count):
            body(index)
    else:
        lax.fori_loop(0, count, lambda index, carry: (body(index), carry)[1], 0)


def prepare(
    months,
    rows_in,
    blocks_in,
    tiles_in,
    copies_ref,
    sorted_ref,
    pick_ref,
    rows_ref,
    blocks_ref,
    tiles_ref,
    semaphores,
):
    size, packed_rows, packed_width = copies_ref.shape
    slot_count, tile_height, cell_count = tiles_ref.shape
    used_rows, source_width = rows_ref.shape
    own_blocks = sorted_ref.shape[3] // cell_count
    height = pick_ref.shape[0] // 2
    load_blocks = pltpu.make_async_copy(blocks_in, blocks_ref, semaphores.at[0])
    load_rows = pltpu.make_async_copy(rows_in, rows_ref, semaphores.at[1])
    ends = [slot_count * part // PARTS for part in range(PARTS + 1)]
    parts = [range(start, end) for start, end in zip(ends, ends[1:])]
    load_parts = [
        pltpu.make_async_copy(
            tiles_in.at[pl.ds(part.start, len(part))],
            tiles_ref.at[pl.ds(part.start, len(part))],
            semaphores.at[2 + index],
        )
        for index, part in enumerate(parts)
    ]
    load_blocks.start()
    load_rows.start()
    for index, load in enumerate(load_parts):
        load.start(priority=index % 2)

    def clear(owner):
        sorted_ref[owner] = jnp.zeros(sorted_ref.shape[1:], sorted_ref.dtype)
        copies_ref[owner] = jnp.zeros(copies_ref.shape[1:], copies_ref.dtype)

    each(size, clear)
    load_blocks.wait()
    blocks = blocks_ref[...] if slot_count <= WRITTEN_OUT else blocks_ref
    first = blocks[0, 0]
    row = lax.broadcasted_iota(jnp.int32, (height, pick_ref.shape[1]), 0)
    column = lax.broadcasted_iota(jnp.int32, (height, pick_ref.shape[1]), 1)
    for which, source in enumerate((first, size * own_blocks - 1 - first)):
        start = history_slot(source // own_blocks, size) * packed_rows + source % own_blocks
        picked = column == start + row // months * own_blocks
        pick_ref[pl.ds(which * height, height)] = picked.astype(jnp.bfloat16)
    load_rows.wait()

    def copy(owner):
        copies_ref[owner, :used_rows, :source_width] = rows_ref[...]

    def place(slot):
        which = (blocks[0, slot] != first).astype(jnp.int32)
        arrival = blocks[1, slot]
        start = pl.multiple_of(arrival % own_blocks * cell_count, cell_count)
        sorted_ref[arrival // own_blocks, which, :, pl.ds(start, cell_count)] = tiles_ref[slot]

    each(size, copy)
    for load, part in zip(load_parts, parts):
        load.wait()
        each(len(part), lambda slot: place(part.start + slot))


def tile_sums(months, histories_ref, pick_ref, sorted_ref, coded_ref):
    size, packed_rows, packed_width = histories_ref.shape
    sources, tile_height, row_length = sorted_ref.shape[1:]
    cell_count = coded_ref.shape[2]
    own_blocks = row_length // cell_count
    height = pick_ref.shape[0] // sources

    column_of = lax.broadcasted_iota(jnp.int32, (packed_width, tile_height), 1) // months
    packed_column = lax.broadcasted_iota(jnp.int32, (packed_width, tile_height), 0)
    repeat_columns = (column_of == packed_column).astype(jnp.bfloat16)
    month_of_row = lax.broadcasted_iota(jnp.int32, (sources * height, tile_height), 0) % months
    month_of_column = lax.broadcasted_iota(jnp.int32, (sources * height, tile_height), 1) % months
    histories = histories_ref[...].reshape(size * packed_rows, packed_width)
    tall = jnp.dot(pick_ref[...], histories, preferred_element_type=jnp.float32)
    wide = jnp.dot(tall.astype(jnp.bfloat16), repeat_columns, preferred_element_type=jnp.float32)
    wide = jnp.where(month_of_row == month_of_column, wide, 0.0).astype(jnp.bfloat16)

    coded_rows = own_blocks * height

    def code(slot):
        parts = [
            jnp.dot(
                wide[which * height : (which + 1) * height],
                sorted_ref[sums_device(slot, size), which],
                preferred_element_type=jnp.float32,
            )
            for which in range(sources)
        ]
        total = sum(parts[1:], parts[0])
        values = [total[:, block * cell_count : (block + 1) * cell_count] for block in range(own_blocks)]
        top = jnp.abs(values[0])
        for value in values[1:]:
            top = jnp.maximum(top, jnp.abs(value))
        top = jnp.max(top, axis=0, keepdims=True)
        level = jnp.ceil(jnp.log2(jnp.maximum(top, SMALLEST)) * LEVELS)
        half = jnp.exp2(level * (-0.5 / LEVELS))
        for block, value in enumerate(values):
            steps = jnp.round(value * half * (half * STEPS))
            coded_ref[slot, pl.ds(block * height, height)] = steps.astype(jnp.int32).astype(jnp.int16)
        spread = jnp.broadcast_to(level.astype(jnp.int32), (SCALE_ROWS, cell_count))
        coded_ref[slot, pl.ds(coded_rows, SCALE_ROWS)] = spread.astype(jnp.int16)

    each(size, code)


def add_parts(coded_ref, total_ref):
    size = coded_ref.shape[0]
    own_blocks, height, cell_count = total_ref.shape
    coded_rows = own_blocks * height
    total_ref[...] = jnp.zeros(total_ref.shape, total_ref.dtype)

    def add(slot):
        level = coded_ref[slot, pl.ds(coded_rows, SCALE_ROWS)].astype(jnp.int32).astype(jnp.float32)[:1]
        half = jnp.exp2(level * (0.5 / LEVELS))
        for block in range(own_blocks):
            steps = coded_ref[slot, pl.ds(block * height, height)].astype(jnp.int32)
            total_ref[block] += steps.astype(jnp.float32) * (half * (1.0 / STEPS)) * half

    each(size, add)


def shards(propagator, tile_blocks, histories):
    size = lax.axis_size("tm")
    own_blocks, tracer_count, source_width = histories.shape
    slot_count, source_width, months, cell_count = propagator.shape
    height = tracer_count * months
    tile_height = source_width * months

    used_rows = tracer_count * own_blocks
    packed_rows = used_rows + -used_rows % 16
    packed_width = source_width + -source_width % 128
    rows = jnp.swapaxes(histories, 0, 1).reshape(used_rows, source_width)
    blocks = tile_blocks.T
    tiles = propagator.reshape(slot_count, tile_height, cell_count)
    vmem = pl.BlockSpec(memory_space=pltpu.VMEM)
    hbm = pl.BlockSpec(memory_space=pltpu.HBM)
    copies, sorted_tiles, pick = pl.pallas_call(
        lambda *refs: prepare(months, *refs),
        out_shape=[
            jax.ShapeDtypeStruct((size, packed_rows, packed_width), rows.dtype),
            jax.ShapeDtypeStruct((size, 2, tile_height, own_blocks * cell_count), tiles.dtype),
            jax.ShapeDtypeStruct((2 * height, size * packed_rows), jnp.bfloat16),
        ],
        in_specs=[hbm, hbm, hbm],
        out_specs=[vmem, vmem, vmem],
        scratch_shapes=[
            pltpu.VMEM(rows.shape, rows.dtype),
            (pltpu.VMEM if slot_count <= WRITTEN_OUT else pltpu.SMEM)(blocks.shape, blocks.dtype),
            pltpu.VMEM(tiles.shape, tiles.dtype),
            pltpu.SemaphoreType.DMA((2 + PARTS,)),
        ],
        compiler_params=pltpu.CompilerParams(vmem_limit_bytes=24 * 1024 * 1024),
        cost_estimate=pl.CostEstimate(flops=0, bytes_accessed=tiles.size * 4, transcendentals=0),
    )(*(pltpu.with_memory_space_constraint(value, pltpu.HBM) for value in (rows, blocks, tiles)))
    inner = [device for device in range(1, size) if device != centre(size)]
    received = exchange(copies, [centre(size)] + inner + [0])

    coded = pl.pallas_call(
        lambda *refs: tile_sums(months, *refs),
        out_shape=jax.ShapeDtypeStruct((size, own_blocks * height + SCALE_ROWS, cell_count), jnp.int16),
        in_specs=[vmem, vmem, vmem],
        out_specs=vmem,
        compiler_params=pltpu.CompilerParams(vmem_limit_bytes=20 * 1024 * 1024),
        cost_estimate=pl.CostEstimate(
            flops=2 * slot_count * height * tile_height * cell_count,
            bytes_accessed=propagator.size * 4,
            transcendentals=0,
        ),
    )(received, pick, sorted_tiles)

    owned = pl.pallas_call(
        add_parts,
        out_shape=jax.ShapeDtypeStruct((own_blocks, height, cell_count), jnp.float32),
        in_specs=[vmem],
        out_specs=vmem,
        compiler_params=pltpu.CompilerParams(vmem_limit_bytes=16 * 1024 * 1024),
    )(exchange(coded, [sums_device(slot, size) for slot in range(size)]))
    return owned.reshape(own_blocks, tracer_count, months, cell_count)


def solution(mesh):
    in_specs = (
        P(("groups", "tm"), None, None, "cells"),
        P(("groups", "tm"), None),
        P("tm", None, None),
    )
    out_specs = P(("groups", "tm"), None, None, "cells")
    return jax.shard_map(shards, mesh=mesh, in_specs=in_specs, out_specs=out_specs, check_vma=False)
```

```python
import jax
import jax.numpy as jnp
from jax import lax
from jax.experimental import pallas as pl
from jax.experimental.pallas import tpu as pltpu
from jax.sharding import PartitionSpec as P

STEPS = 32700.0
LEVELS = 128
SMALLEST = 2.0**-126
SCALE_ROWS = 8
PARTS = 4
WRITTEN_OUT = 17
SOURCES = 2


def centre(size):
    return size * 5 // 8


def history_slot(device, size):
    after = device - (device > centre(size)).astype(jnp.int32)
    return jnp.where(device == centre(size), 0, jnp.where(device == 0, size - 1, after))


def sums_device(slot, size):
    if isinstance(slot, int):
        return centre(size) if slot == 0 else size - slot - (size - slot <= centre(size))
    after = size - slot - (size - slot <= centre(size)).astype(jnp.int32)
    return jnp.where(slot == 0, centre(size), after)


def exchange(value, order):
    return lax.all_to_all(value, "tm", 0, 0, axis_index_groups=[order], tiled=True)


def split(value, divisor):
    if divisor & (divisor - 1):
        return lax.div(value, jnp.full_like(value, divisor)), lax.rem(value, jnp.full_like(value, divisor))
    return value >> (divisor.bit_length() - 1), value & (divisor - 1)


def each(count, body):
    if count <= WRITTEN_OUT:
        for index in range(count):
            body(index)
    else:
        lax.fori_loop(0, count, lambda index, carry: (body(index), carry)[1], 0)


def prepare(
    months,
    rows_in,
    blocks_in,
    tiles_in,
    copies_ref,
    sorted_ref,
    pick_ref,
    columns_ref,
    same_ref,
    rows_ref,
    blocks_ref,
    tiles_ref,
    semaphores,
):
    size, packed_rows, packed_width = copies_ref.shape
    slot_count, tile_height, cell_count = tiles_ref.shape
    used_rows, source_width = rows_ref.shape
    block_count = sorted_ref.shape[0] // SOURCES
    own_blocks = block_count // size
    height = pick_ref.shape[0] // SOURCES
    ends = [slot_count * part // PARTS for part in range(PARTS + 1)]
    parts = [range(start, end) for start, end in zip(ends, ends[1:])]
    load_blocks = pltpu.make_async_copy(blocks_in, blocks_ref, semaphores.at[0])
    load_rows = pltpu.make_async_copy(rows_in, rows_ref, semaphores.at[1])
    load_parts = [
        pltpu.make_async_copy(
            tiles_in.at[pl.ds(part.start, len(part))],
            tiles_ref.at[pl.ds(part.start, len(part))],
            semaphores.at[2 + index],
        )
        for index, part in enumerate(parts)
    ]
    load_blocks.start()
    load_rows.start()
    for load in load_parts:
        load.start()

    def clear(owner):
        rows = pl.ds(owner * SOURCES * own_blocks, SOURCES * own_blocks)
        sorted_ref[rows] = jnp.zeros((SOURCES * own_blocks, tile_height, cell_count), sorted_ref.dtype)
        copies_ref[owner] = jnp.zeros(copies_ref.shape[1:], copies_ref.dtype)

    each(size, clear)
    packed_column = lax.broadcasted_iota(jnp.int32, columns_ref.shape, 0)
    column_of = split(lax.broadcasted_iota(jnp.int32, columns_ref.shape, 1), months)[0]
    columns_ref[...] = (column_of == packed_column).astype(columns_ref.dtype)
    month_of_row = split(lax.broadcasted_iota(jnp.int32, same_ref.shape, 0), months)[1]
    month_of_column = split(lax.broadcasted_iota(jnp.int32, same_ref.shape, 1), months)[1]
    same_ref[...] = (month_of_row == month_of_column).astype(same_ref.dtype)
    tracer = split(lax.broadcasted_iota(jnp.int32, (height, pick_ref.shape[1]), 0), months)[0]
    offset = lax.broadcasted_iota(jnp.int32, (height, pick_ref.shape[1]), 1) - tracer * own_blocks

    load_blocks.wait()
    first = blocks_ref[0, 0]

    def place_of(slot):
        which = (blocks_ref[0, slot] != first).astype(jnp.int32)
        return which * block_count + blocks_ref[1, slot]

    places = [place_of(slot) for slot in range(slot_count)] if slot_count <= WRITTEN_OUT else None
    for which, source in enumerate((first, block_count - 1 - first)):
        owner, block = split(source, own_blocks)
        picked = offset == history_slot(owner, size) * packed_rows + block
        pick_ref[pl.ds(which * height, height)] = picked.astype(pick_ref.dtype)
    load_rows.wait()

    def copy(owner):
        copies_ref[owner, :used_rows, :source_width] = rows_ref[...]

    each(size, copy)
    for load, part in zip(load_parts, parts):
        load.wait()
        if places:
            for slot in part:
                sorted_ref[places[slot]] = tiles_ref[slot]
    if not places:

        def place(slot):
            sorted_ref[place_of(slot)] = tiles_ref[slot]

        each(slot_count, place)


def tile_sums(histories_ref, pick_ref, columns_ref, same_ref, sorted_ref, coded_ref):
    size, packed_rows, packed_width = histories_ref.shape
    block_count = sorted_ref.shape[0] // SOURCES
    own_blocks = block_count // size
    height = pick_ref.shape[0] // SOURCES
    cell_count = coded_ref.shape[2]
    coded_rows = own_blocks * height

    histories = histories_ref[...].reshape(size * packed_rows, packed_width)
    tall = jnp.dot(pick_ref[...], histories, preferred_element_type=jnp.float32)
    wide = jnp.dot(tall.astype(jnp.bfloat16), columns_ref[...], preferred_element_type=jnp.float32)
    wide = (wide * same_ref[...]).astype(jnp.bfloat16)

    def code(slot):
        total = None
        for which in range(SOURCES):
            start = which * block_count + sums_device(slot, size) * own_blocks
            tiles = jnp.concatenate([sorted_ref[start + block] for block in range(own_blocks)], axis=1)
            rows = wide[which * height : (which + 1) * height]
            part = jnp.dot(rows, tiles, preferred_element_type=jnp.float32)
            total = part if total is None else total + part
        values = [total[:, block * cell_count : (block + 1) * cell_count] for block in range(own_blocks)]
        top = jnp.abs(values[0])
        for value in values[1:]:
            top = jnp.maximum(top, jnp.abs(value))
        top = jnp.max(top, axis=0, keepdims=True)
        level = jnp.ceil(jnp.log2(jnp.maximum(top, SMALLEST)) * LEVELS)
        half = jnp.exp2(level * (-0.5 / LEVELS))
        for block, value in enumerate(values):
            steps = jnp.round(value * half * (half * STEPS))
            coded_ref[slot, pl.ds(block * height, height)] = steps.astype(jnp.int32).astype(jnp.int16)
        spread = jnp.broadcast_to(level.astype(jnp.int32), (SCALE_ROWS, cell_count))
        coded_ref[slot, pl.ds(coded_rows, SCALE_ROWS)] = spread.astype(jnp.int16)

    each(size, code)


def add_parts(coded_ref, total_ref):
    size = coded_ref.shape[0]
    own_blocks, height, cell_count = total_ref.shape
    coded_rows = own_blocks * height
    total_ref[...] = jnp.zeros(total_ref.shape, total_ref.dtype)

    def add(slot):
        level = coded_ref[slot, pl.ds(coded_rows, SCALE_ROWS)].astype(jnp.int32).astype(jnp.float32)[:1]
        half = jnp.exp2(level * (0.5 / LEVELS))
        for block in range(own_blocks):
            steps = coded_ref[slot, pl.ds(block * height, height)].astype(jnp.int32)
            total_ref[block] += steps.astype(jnp.float32) * (half * (1.0 / STEPS)) * half

    each(size, add)


def shards(propagator, tile_blocks, histories):
    size = lax.axis_size("tm")
    own_blocks, tracer_count, source_width = histories.shape
    slot_count, source_width, months, cell_count = propagator.shape
    block_count = size * own_blocks
    height = tracer_count * months
    tile_height = source_width * months

    used_rows = tracer_count * own_blocks
    packed_rows = used_rows + -used_rows % 16
    packed_width = source_width + -source_width % 128
    rows = jnp.swapaxes(histories, 0, 1).reshape(used_rows, source_width)
    blocks = tile_blocks.T
    tiles = propagator.reshape(slot_count, tile_height, cell_count)
    vmem = pl.BlockSpec(memory_space=pltpu.VMEM)
    hbm = pl.BlockSpec(memory_space=pltpu.HBM)
    copies, sorted_tiles, pick, columns, same = pl.pallas_call(
        lambda *refs: prepare(months, *refs),
        out_shape=[
            jax.ShapeDtypeStruct((size, packed_rows, packed_width), rows.dtype),
            jax.ShapeDtypeStruct((SOURCES * block_count, tile_height, cell_count), tiles.dtype),
            jax.ShapeDtypeStruct((SOURCES * height, size * packed_rows), jnp.bfloat16),
            jax.ShapeDtypeStruct((packed_width, tile_height), jnp.bfloat16),
            jax.ShapeDtypeStruct((SOURCES * height, tile_height), jnp.float32),
        ],
        in_specs=[hbm] * 3,
        out_specs=[vmem] * 5,
        scratch_shapes=[
            pltpu.VMEM(rows.shape, rows.dtype),
            pltpu.SMEM(blocks.shape, blocks.dtype),
            pltpu.VMEM(tiles.shape, tiles.dtype),
            pltpu.SemaphoreType.DMA((2 + PARTS,)),
        ],
        compiler_params=pltpu.CompilerParams(vmem_limit_bytes=24 * 1024 * 1024),
        cost_estimate=pl.CostEstimate(flops=0, bytes_accessed=tiles.size * 4, transcendentals=0),
    )(*(pltpu.with_memory_space_constraint(value, pltpu.HBM) for value in (rows, blocks, tiles)))

    inner = [device for device in range(1, size) if device != centre(size)]
    received = exchange(copies, [centre(size)] + inner + [0])

    coded = pl.pallas_call(
        tile_sums,
        out_shape=jax.ShapeDtypeStruct((size, own_blocks * height + SCALE_ROWS, cell_count), jnp.int16),
        in_specs=[vmem] * 5,
        out_specs=vmem,
        compiler_params=pltpu.CompilerParams(vmem_limit_bytes=20 * 1024 * 1024),
        cost_estimate=pl.CostEstimate(
            flops=2 * slot_count * height * tile_height * cell_count,
            bytes_accessed=propagator.size * 4,
            transcendentals=0,
        ),
    )(received, pick, columns, same, sorted_tiles)

    owned = pl.pallas_call(
        add_parts,
        out_shape=jax.ShapeDtypeStruct((own_blocks, height, cell_count), jnp.float32),
        in_specs=[vmem],
        out_specs=vmem,
        compiler_params=pltpu.CompilerParams(vmem_limit_bytes=16 * 1024 * 1024),
    )(exchange(coded, [sums_device(slot, size) for slot in range(size)]))
    return owned.reshape(own_blocks, tracer_count, months, cell_count)


def solution(mesh):
    in_specs = (
        P(("groups", "tm"), None, None, "cells"),
        P(("groups", "tm"), None),
        P("tm", None, None),
    )
    out_specs = P(("groups", "tm"), None, None, "cells")
    return jax.shard_map(shards, mesh=mesh, in_specs=in_specs, out_specs=out_specs, check_vma=False)
```

```python
import jax
import jax.numpy as jnp
from jax import lax
from jax.experimental import pallas as pl
from jax.experimental.pallas import tpu as pltpu
from jax.sharding import PartitionSpec as P

STEPS = 32700.0
LEVELS = 128
SMALLEST = 2.0**-126
SCALE_ROWS = 8
WRITTEN_OUT = 17
SOURCES = 2


def centre(size):
    return size * 5 // 8


def history_slot(device, size):
    after = device - (device > centre(size)).astype(jnp.int32)
    return jnp.where(device == centre(size), 0, jnp.where(device == 0, size - 1, after))


def sums_device(slot, size):
    return size - 1 - slot


def starts_late(size):
    return lax.axis_index("tm") >= size * 3 // 4


def exchange(value, order):
    return lax.all_to_all(value, "tm", 0, 0, axis_index_groups=[order], tiled=True)


def split(value, divisor):
    if divisor & (divisor - 1):
        return lax.div(value, jnp.full_like(value, divisor)), lax.rem(value, jnp.full_like(value, divisor))
    return value >> (divisor.bit_length() - 1), value & (divisor - 1)


def each(count, body):
    if count <= WRITTEN_OUT:
        for index in range(count):
            body(index)
    else:
        lax.fori_loop(0, count, lambda index, carry: (body(index), carry)[1], 0)


def tile_loads(blocks_in, tiles_in, blocks_ref, tiles_ref, semaphores):
    return [
        pltpu.make_async_copy(blocks_in, blocks_ref, semaphores.at[0]),
        pltpu.make_async_copy(tiles_in, tiles_ref, semaphores.at[1]),
    ]


def arrange(size, months, loads, blocks_ref, tiles_ref, sorted_ref, pick_ref):
    slot_count, tile_height, cell_count = tiles_ref.shape
    block_count = sorted_ref.shape[0] // SOURCES
    own_blocks = block_count // size
    height = pick_ref.shape[0] // SOURCES
    packed_rows = pick_ref.shape[1] // size

    def clear(owner):
        rows = pl.ds(owner * SOURCES * own_blocks, SOURCES * own_blocks)
        sorted_ref[rows] = jnp.zeros((SOURCES * own_blocks, tile_height, cell_count), sorted_ref.dtype)

    each(size, clear)
    tracer = split(lax.broadcasted_iota(jnp.int32, (height, pick_ref.shape[1]), 0), months)[0]
    offset = lax.broadcasted_iota(jnp.int32, (height, pick_ref.shape[1]), 1) - tracer * own_blocks
    loads[0].wait()
    first = blocks_ref[0, 0]

    def place_of(slot):
        which = (blocks_ref[0, slot] != first).astype(jnp.int32)
        return which * block_count + blocks_ref[1, slot]

    places = [place_of(slot) for slot in range(slot_count)] if slot_count <= WRITTEN_OUT else None
    for which, source in enumerate((first, block_count - 1 - first)):
        owner, block = split(source, own_blocks)
        picked = offset == history_slot(owner, size) * packed_rows + block
        pick_ref[pl.ds(which * height, height)] = picked.astype(pick_ref.dtype)
    loads[1].wait()

    def place(slot):
        sorted_ref[places[slot] if places else place_of(slot)] = tiles_ref[slot]

    each(slot_count, place)


def prepare(
    months,
    rows_in,
    blocks_in,
    tiles_in,
    copies_ref,
    sorted_ref,
    pick_ref,
    columns_ref,
    same_ref,
    rows_ref,
    blocks_ref,
    tiles_ref,
    semaphores,
):
    size = copies_ref.shape[0]
    used_rows, source_width = rows_ref.shape
    early = jnp.logical_not(starts_late(size))
    load_rows = pltpu.make_async_copy(rows_in, rows_ref, semaphores.at[2])
    loads = tile_loads(blocks_in, tiles_in, blocks_ref, tiles_ref, semaphores)
    load_rows.start()

    @pl.when(early)
    def _():
        for load in loads:
            load.start()

    packed_column = lax.broadcasted_iota(jnp.int32, columns_ref.shape, 0)
    column_of = split(lax.broadcasted_iota(jnp.int32, columns_ref.shape, 1), months)[0]
    columns_ref[...] = (column_of == packed_column).astype(columns_ref.dtype)
    month_of_row = split(lax.broadcasted_iota(jnp.int32, same_ref.shape, 0), months)[1]
    month_of_column = split(lax.broadcasted_iota(jnp.int32, same_ref.shape, 1), months)[1]
    same_ref[...] = (month_of_row == month_of_column).astype(same_ref.dtype)
    copies_ref[...] = jnp.zeros(copies_ref.shape, copies_ref.dtype)
    load_rows.wait()

    def copy(owner):
        copies_ref[owner, :used_rows, :source_width] = rows_ref[...]

    each(size, copy)

    @pl.when(early)
    def _():
        arrange(size, months, loads, blocks_ref, tiles_ref, sorted_ref, pick_ref)


def tile_sums(
    months,
    histories_ref,
    pick_ref,
    columns_ref,
    same_ref,
    sorted_ref,
    blocks_in,
    tiles_in,
    coded_ref,
    late_pick_ref,
    late_sorted_ref,
    blocks_ref,
    tiles_ref,
    semaphores,
):
    size = histories_ref.shape[0]
    late = starts_late(size)

    @pl.when(late)
    def _():
        loads = tile_loads(blocks_in, tiles_in, blocks_ref, tiles_ref, semaphores)
        for load in loads:
            load.start()
        arrange(size, months, loads, blocks_ref, tiles_ref, late_sorted_ref, late_pick_ref)
        code_sums(histories_ref, late_pick_ref, columns_ref, same_ref, late_sorted_ref, coded_ref)

    @pl.when(jnp.logical_not(late))
    def _():
        code_sums(histories_ref, pick_ref, columns_ref, same_ref, sorted_ref, coded_ref)


def code_sums(histories_ref, pick_ref, columns_ref, same_ref, sorted_ref, coded_ref):
    size, packed_rows, packed_width = histories_ref.shape
    block_count = sorted_ref.shape[0] // SOURCES
    own_blocks = block_count // size
    height = pick_ref.shape[0] // SOURCES
    cell_count = coded_ref.shape[2]
    coded_rows = own_blocks * height

    histories = histories_ref[...].reshape(size * packed_rows, packed_width)
    tall = jnp.dot(pick_ref[...], histories, preferred_element_type=jnp.float32)
    wide = jnp.dot(tall.astype(jnp.bfloat16), columns_ref[...], preferred_element_type=jnp.float32)
    wide = (wide * same_ref[...]).astype(jnp.bfloat16)

    def code(slot):
        total = None
        for which in range(SOURCES):
            start = which * block_count + sums_device(slot, size) * own_blocks
            tiles = jnp.concatenate([sorted_ref[start + block] for block in range(own_blocks)], axis=1)
            rows = wide[which * height : (which + 1) * height]
            part = jnp.dot(rows, tiles, preferred_element_type=jnp.float32)
            total = part if total is None else total + part
        values = [total[:, block * cell_count : (block + 1) * cell_count] for block in range(own_blocks)]
        top = jnp.abs(values[0])
        for value in values[1:]:
            top = jnp.maximum(top, jnp.abs(value))
        top = jnp.max(top, axis=0, keepdims=True)
        level = jnp.ceil(jnp.log2(jnp.maximum(top, SMALLEST)) * LEVELS)
        half = jnp.exp2(level * (-0.5 / LEVELS))
        for block, value in enumerate(values):
            steps = jnp.round(value * half * (half * STEPS))
            coded_ref[slot, pl.ds(block * height, height)] = steps.astype(jnp.int32).astype(jnp.int16)
        spread = jnp.broadcast_to(level.astype(jnp.int32), (SCALE_ROWS, cell_count))
        coded_ref[slot, pl.ds(coded_rows, SCALE_ROWS)] = spread.astype(jnp.int16)

    each(size, code)


def add_parts(coded_ref, total_ref):
    size = coded_ref.shape[0]
    own_blocks, height, cell_count = total_ref.shape
    coded_rows = own_blocks * height
    total_ref[...] = jnp.zeros(total_ref.shape, total_ref.dtype)

    def add(slot):
        level = coded_ref[slot, pl.ds(coded_rows, SCALE_ROWS)].astype(jnp.int32).astype(jnp.float32)[:1]
        half = jnp.exp2(level * (0.5 / LEVELS))
        for block in range(own_blocks):
            steps = coded_ref[slot, pl.ds(block * height, height)].astype(jnp.int32)
            total_ref[block] += steps.astype(jnp.float32) * (half * (1.0 / STEPS)) * half

    each(size, add)


def shards(propagator, tile_blocks, histories):
    size = lax.axis_size("tm")
    own_blocks, tracer_count, source_width = histories.shape
    slot_count, source_width, months, cell_count = propagator.shape
    block_count = size * own_blocks
    height = tracer_count * months
    tile_height = source_width * months

    used_rows = tracer_count * own_blocks
    packed_rows = used_rows + -used_rows % 16
    packed_width = source_width + -source_width % 128
    rows, blocks, tiles = (
        pltpu.with_memory_space_constraint(value, pltpu.HBM)
        for value in (
            jnp.swapaxes(histories, 0, 1).reshape(used_rows, source_width),
            tile_blocks.T,
            propagator.reshape(slot_count, tile_height, cell_count),
        )
    )
    vmem = pl.BlockSpec(memory_space=pltpu.VMEM)
    hbm = pl.BlockSpec(memory_space=pltpu.HBM)
    copies, sorted_tiles, pick, columns, same = pl.pallas_call(
        lambda *refs: prepare(months, *refs),
        out_shape=[
            jax.ShapeDtypeStruct((size, packed_rows, packed_width), rows.dtype),
            jax.ShapeDtypeStruct((SOURCES * block_count, tile_height, cell_count), tiles.dtype),
            jax.ShapeDtypeStruct((SOURCES * height, size * packed_rows), jnp.bfloat16),
            jax.ShapeDtypeStruct((packed_width, tile_height), jnp.bfloat16),
            jax.ShapeDtypeStruct((SOURCES * height, tile_height), jnp.float32),
        ],
        in_specs=[hbm] * 3,
        out_specs=[vmem] * 5,
        scratch_shapes=[
            pltpu.VMEM(rows.shape, rows.dtype),
            pltpu.SMEM(blocks.shape, blocks.dtype),
            pltpu.VMEM(tiles.shape, tiles.dtype),
            pltpu.SemaphoreType.DMA((3,)),
        ],
        compiler_params=pltpu.CompilerParams(vmem_limit_bytes=24 * 1024 * 1024),
        cost_estimate=pl.CostEstimate(flops=0, bytes_accessed=tiles.size * 4, transcendentals=0),
    )(rows, blocks, tiles)

    inner = [device for device in range(1, size) if device != centre(size)]
    received = exchange(copies, [centre(size)] + inner + [0])

    coded = pl.pallas_call(
        lambda *refs: tile_sums(months, *refs),
        out_shape=jax.ShapeDtypeStruct((size, own_blocks * height + SCALE_ROWS, cell_count), jnp.int16),
        in_specs=[vmem] * 5 + [hbm] * 2,
        out_specs=vmem,
        scratch_shapes=[
            pltpu.VMEM(pick.shape, pick.dtype),
            pltpu.VMEM(sorted_tiles.shape, sorted_tiles.dtype),
            pltpu.SMEM(blocks.shape, blocks.dtype),
            pltpu.VMEM(tiles.shape, tiles.dtype),
            pltpu.SemaphoreType.DMA((2,)),
        ],
        compiler_params=pltpu.CompilerParams(vmem_limit_bytes=28 * 1024 * 1024),
        cost_estimate=pl.CostEstimate(
            flops=2 * slot_count * height * tile_height * cell_count,
            bytes_accessed=propagator.size * 4,
            transcendentals=0,
        ),
    )(received, pick, columns, same, sorted_tiles, blocks, tiles)

    owned = pl.pallas_call(
        add_parts,
        out_shape=jax.ShapeDtypeStruct((own_blocks, height, cell_count), jnp.float32),
        in_specs=[vmem],
        out_specs=vmem,
        compiler_params=pltpu.CompilerParams(vmem_limit_bytes=16 * 1024 * 1024),
    )(exchange(coded, [sums_device(slot, size) for slot in range(size)]))
    return owned.reshape(own_blocks, tracer_count, months, cell_count)


def solution(mesh):
    in_specs = (
        P(("groups", "tm"), None, None, "cells"),
        P(("groups", "tm"), None),
        P("tm", None, None),
    )
    out_specs = P(("groups", "tm"), None, None, "cells")
    return jax.shard_map(shards, mesh=mesh, in_specs=in_specs, out_specs=out_specs, check_vma=False)
```

```python
import jax
import jax.numpy as jnp
from jax import lax
from jax.experimental import pallas as pl
from jax.experimental.pallas import tpu as pltpu
from jax.sharding import PartitionSpec as P

STEPS = 32700.0
LEVELS = 128
SMALLEST = 2.0**-126
SCALE_ROWS = 8
WRITTEN_OUT = 17
SOURCES = 2


def centre(size):
    return size * 5 // 8


def history_slot(device, size):
    after = device - (device > centre(size)).astype(jnp.int32)
    return jnp.where(device == centre(size), 0, jnp.where(device == 0, size - 1, after))


def sums_device(slot, size):
    if isinstance(slot, int):
        return centre(size) if slot == 0 else size - slot - (size - slot <= centre(size))
    after = size - slot - (size - slot <= centre(size)).astype(jnp.int32)
    return jnp.where(slot == 0, centre(size), after)


def exchange(value, order):
    return lax.all_to_all(value, "tm", 0, 0, axis_index_groups=[order], tiled=True)


def split(value, divisor):
    if divisor & (divisor - 1):
        return lax.div(value, jnp.full_like(value, divisor)), lax.rem(value, jnp.full_like(value, divisor))
    return value >> (divisor.bit_length() - 1), value & (divisor - 1)


def each(count, body):
    if count <= WRITTEN_OUT:
        for index in range(count):
            body(index)
    else:
        lax.fori_loop(0, count, lambda index, carry: (body(index), carry)[1], 0)


def arrange(size, months, load_blocks, load_tiles, blocks_ref, tiles_ref, sorted_ref, pick_ref):
    slot_count, tile_height, cell_count = tiles_ref.shape
    block_count = sorted_ref.shape[0] // SOURCES
    own_blocks = block_count // size
    height = pick_ref.shape[0] // SOURCES
    packed_rows = pick_ref.shape[1] // size

    def clear(owner):
        rows = pl.ds(owner * SOURCES * own_blocks, SOURCES * own_blocks)
        sorted_ref[rows] = jnp.zeros((SOURCES * own_blocks, tile_height, cell_count), sorted_ref.dtype)

    each(size, clear)
    tracer = split(lax.broadcasted_iota(jnp.int32, (height, pick_ref.shape[1]), 0), months)[0]
    offset = lax.broadcasted_iota(jnp.int32, (height, pick_ref.shape[1]), 1) - tracer * own_blocks
    load_blocks.wait()
    first = blocks_ref[0, 0]

    def place_of(slot):
        which = (blocks_ref[0, slot] != first).astype(jnp.int32)
        return which * block_count + blocks_ref[1, slot]

    places = [place_of(slot) for slot in range(slot_count)] if slot_count <= WRITTEN_OUT else None
    for which, source in enumerate((first, block_count - 1 - first)):
        owner, block = split(source, own_blocks)
        picked = offset == history_slot(owner, size) * packed_rows + block
        pick_ref[pl.ds(which * height, height)] = picked.astype(pick_ref.dtype)
    load_tiles.wait()

    def place(slot):
        sorted_ref[places[slot] if places else place_of(slot)] = tiles_ref[slot]

    each(slot_count, place)


def prepare(
    months,
    rows_in,
    blocks_in,
    tiles_in,
    copies_ref,
    sorted_ref,
    pick_ref,
    columns_ref,
    same_ref,
    rows_ref,
    blocks_ref,
    tiles_ref,
    semaphores,
):
    size = copies_ref.shape[0]
    used_rows, source_width = rows_ref.shape
    load_rows = pltpu.make_async_copy(rows_in, rows_ref, semaphores.at[0])
    load_blocks = pltpu.make_async_copy(blocks_in, blocks_ref, semaphores.at[1])
    load_tiles = pltpu.make_async_copy(tiles_in, tiles_ref, semaphores.at[2])
    for load in (load_rows, load_blocks, load_tiles):
        load.start()
    packed_column = lax.broadcasted_iota(jnp.int32, columns_ref.shape, 0)
    column_of = split(lax.broadcasted_iota(jnp.int32, columns_ref.shape, 1), months)[0]
    columns_ref[...] = (column_of == packed_column).astype(columns_ref.dtype)
    month_of_row = split(lax.broadcasted_iota(jnp.int32, same_ref.shape, 0), months)[1]
    month_of_column = split(lax.broadcasted_iota(jnp.int32, same_ref.shape, 1), months)[1]
    same_ref[...] = (month_of_row == month_of_column).astype(same_ref.dtype)
    copies_ref[...] = jnp.zeros(copies_ref.shape, copies_ref.dtype)
    load_rows.wait()

    def copy(owner):
        copies_ref[owner, :used_rows, :source_width] = rows_ref[...]

    each(size, copy)
    arrange(size, months, load_blocks, load_tiles, blocks_ref, tiles_ref, sorted_ref, pick_ref)


def tile_sums(histories_ref, pick_ref, columns_ref, same_ref, sorted_ref, coded_ref):
    size, packed_rows, packed_width = histories_ref.shape
    block_count = sorted_ref.shape[0] // SOURCES
    own_blocks = block_count // size
    height = pick_ref.shape[0] // SOURCES
    cell_count = coded_ref.shape[2]
    coded_rows = own_blocks * height

    histories = histories_ref[...].reshape(size * packed_rows, packed_width)
    tall = jnp.dot(pick_ref[...], histories, preferred_element_type=jnp.float32)
    wide = jnp.dot(tall.astype(jnp.bfloat16), columns_ref[...], preferred_element_type=jnp.float32)
    wide = (wide * same_ref[...]).astype(jnp.bfloat16)

    def code(slot):
        total = None
        for which in range(SOURCES):
            start = which * block_count + sums_device(slot, size) * own_blocks
            tiles = jnp.concatenate([sorted_ref[start + block] for block in range(own_blocks)], axis=1)
            rows = wide[which * height : (which + 1) * height]
            part = jnp.dot(rows, tiles, preferred_element_type=jnp.float32)
            total = part if total is None else total + part
        values = [total[:, block * cell_count : (block + 1) * cell_count] for block in range(own_blocks)]
        top = jnp.abs(values[0])
        for value in values[1:]:
            top = jnp.maximum(top, jnp.abs(value))
        top = jnp.max(top, axis=0, keepdims=True)
        level = jnp.ceil(jnp.log2(jnp.maximum(top, SMALLEST)) * LEVELS)
        half = jnp.exp2(level * (-0.5 / LEVELS))
        for block, value in enumerate(values):
            steps = jnp.round(value * half * (half * STEPS))
            coded_ref[slot, pl.ds(block * height, height)] = steps.astype(jnp.int32).astype(jnp.int16)
        spread = jnp.broadcast_to(level.astype(jnp.int32), (SCALE_ROWS, cell_count))
        coded_ref[slot, pl.ds(coded_rows, SCALE_ROWS)] = spread.astype(jnp.int16)

    each(size, code)


def add_parts(coded_ref, total_ref):
    size = coded_ref.shape[0]
    own_blocks, height, cell_count = total_ref.shape
    coded_rows = own_blocks * height
    total_ref[...] = jnp.zeros(total_ref.shape, total_ref.dtype)

    def add(slot):
        level = coded_ref[slot, pl.ds(coded_rows, SCALE_ROWS)].astype(jnp.int32).astype(jnp.float32)[:1]
        half = jnp.exp2(level * (0.5 / LEVELS))
        for block in range(own_blocks):
            steps = coded_ref[slot, pl.ds(block * height, height)].astype(jnp.int32)
            total_ref[block] += steps.astype(jnp.float32) * (half * (1.0 / STEPS)) * half

    each(size, add)


def shards(propagator, tile_blocks, histories):
    size = lax.axis_size("tm")
    own_blocks, tracer_count, source_width = histories.shape
    slot_count, source_width, months, cell_count = propagator.shape
    block_count = size * own_blocks
    height = tracer_count * months
    tile_height = source_width * months

    used_rows = tracer_count * own_blocks
    packed_rows = used_rows + -used_rows % 16
    packed_width = source_width + -source_width % 128
    rows, blocks, tiles = (
        pltpu.with_memory_space_constraint(value, pltpu.HBM)
        for value in (
            jnp.swapaxes(histories, 0, 1).reshape(used_rows, source_width),
            tile_blocks.T,
            propagator.reshape(slot_count, tile_height, cell_count),
        )
    )
    vmem = pl.BlockSpec(memory_space=pltpu.VMEM)
    hbm = pl.BlockSpec(memory_space=pltpu.HBM)
    copies, sorted_tiles, pick, columns, same = pl.pallas_call(
        lambda *refs: prepare(months, *refs),
        out_shape=[
            jax.ShapeDtypeStruct((size, packed_rows, packed_width), rows.dtype),
            jax.ShapeDtypeStruct((SOURCES * block_count, tile_height, cell_count), tiles.dtype),
            jax.ShapeDtypeStruct((SOURCES * height, size * packed_rows), jnp.bfloat16),
            jax.ShapeDtypeStruct((packed_width, tile_height), jnp.bfloat16),
            jax.ShapeDtypeStruct((SOURCES * height, tile_height), jnp.float32),
        ],
        in_specs=[hbm] * 3,
        out_specs=[vmem] * 5,
        scratch_shapes=[
            pltpu.VMEM(rows.shape, rows.dtype),
            pltpu.SMEM(blocks.shape, blocks.dtype),
            pltpu.VMEM(tiles.shape, tiles.dtype),
            pltpu.SemaphoreType.DMA((3,)),
        ],
        compiler_params=pltpu.CompilerParams(vmem_limit_bytes=24 * 1024 * 1024),
        cost_estimate=pl.CostEstimate(flops=0, bytes_accessed=tiles.size * 4, transcendentals=0),
    )(rows, blocks, tiles)

    inner = [device for device in range(1, size) if device != centre(size)]
    received = exchange(copies, [centre(size)] + inner + [0])

    coded = pl.pallas_call(
        tile_sums,
        out_shape=jax.ShapeDtypeStruct((size, own_blocks * height + SCALE_ROWS, cell_count), jnp.int16),
        in_specs=[vmem] * 5,
        out_specs=vmem,
        compiler_params=pltpu.CompilerParams(vmem_limit_bytes=20 * 1024 * 1024),
        cost_estimate=pl.CostEstimate(
            flops=2 * slot_count * height * tile_height * cell_count,
            bytes_accessed=propagator.size * 4,
            transcendentals=0,
        ),
    )(received, pick, columns, same, sorted_tiles)

    owned = pl.pallas_call(
        add_parts,
        out_shape=jax.ShapeDtypeStruct((own_blocks, height, cell_count), jnp.float32),
        in_specs=[vmem],
        out_specs=vmem,
        compiler_params=pltpu.CompilerParams(vmem_limit_bytes=16 * 1024 * 1024),
    )(exchange(coded, [sums_device(slot, size) for slot in range(size)]))
    return owned.reshape(own_blocks, tracer_count, months, cell_count)


def solution(mesh):
    in_specs = (
        P(("groups", "tm"), None, None, "cells"),
        P(("groups", "tm"), None),
        P("tm", None, None),
    )
    out_specs = P(("groups", "tm"), None, None, "cells")
    return jax.shard_map(shards, mesh=mesh, in_specs=in_specs, out_specs=out_specs, check_vma=False)
```

```python
import jax
import jax.numpy as jnp
from jax import lax
from jax.experimental import pallas as pl
from jax.experimental.pallas import tpu as pltpu
from jax.sharding import PartitionSpec as P

STEPS = 32700.0
LEVELS = 128
SMALLEST = 2.0**-126
SCALE_ROWS = 8
WRITTEN_OUT = 17
SOURCES = 2


def centre(size):
    return size * 5 // 8


def history_slot(device, size):
    after = device - (device > centre(size)).astype(jnp.int32)
    return jnp.where(device == centre(size), 0, jnp.where(device == 0, size - 1, after))


def sums_device(slot, size):
    if isinstance(slot, int):
        return centre(size) if slot == 0 else size - slot - (size - slot <= centre(size))
    after = size - slot - (size - slot <= centre(size)).astype(jnp.int32)
    return jnp.where(slot == 0, centre(size), after)


def exchange(value, order):
    return lax.all_to_all(value, "tm", 0, 0, axis_index_groups=[order], tiled=True)


def split(value, divisor):
    if divisor & (divisor - 1):
        return lax.div(value, jnp.full_like(value, divisor)), lax.rem(value, jnp.full_like(value, divisor))
    return value >> (divisor.bit_length() - 1), value & (divisor - 1)


def each(count, body):
    if count <= WRITTEN_OUT:
        for index in range(count):
            body(index)
    else:
        lax.fori_loop(0, count, lambda index, carry: (body(index), carry)[1], 0)


def arrange(size, months, load_blocks, load_tiles, blocks_ref, tiles_ref, sorted_ref, pick_ref):
    slot_count = tiles_ref.shape[0]
    half_count = sorted_ref.shape[0] // 3
    block_count = half_count * 2
    own_blocks = block_count // size
    height = pick_ref.shape[0] // SOURCES
    packed_rows = pick_ref.shape[1] // size
    group = sorted_ref.shape[0] // size

    def clear(index):
        sorted_ref[pl.ds(index * group, group)] = jnp.zeros((group,) + tiles_ref.shape[1:], sorted_ref.dtype)

    each(size, clear)
    tracer = split(lax.broadcasted_iota(jnp.int32, (height, pick_ref.shape[1]), 0), months)[0]
    offset = lax.broadcasted_iota(jnp.int32, (height, pick_ref.shape[1]), 1) - tracer * own_blocks
    load_blocks.wait()
    lower = jnp.minimum(blocks_ref[0, 0], block_count - 1 - blocks_ref[0, 0])

    def place_of(slot):
        return blocks_ref[1, slot] + jnp.where(blocks_ref[0, slot] == lower, 0, half_count)

    places = [place_of(slot) for slot in range(slot_count)] if slot_count <= WRITTEN_OUT else None
    for which, source in enumerate((lower, block_count - 1 - lower)):
        owner, block = split(source, own_blocks)
        picked = offset == history_slot(owner, size) * packed_rows + block
        pick_ref[pl.ds(which * height, height)] = picked.astype(pick_ref.dtype)
    load_tiles.wait()

    def place(slot):
        sorted_ref[places[slot] if places else place_of(slot)] = tiles_ref[slot]

    each(slot_count, place)


def prepare(
    months,
    rows_in,
    blocks_in,
    tiles_in,
    copies_ref,
    sorted_ref,
    pick_ref,
    columns_ref,
    same_ref,
    rows_ref,
    blocks_ref,
    tiles_ref,
    semaphores,
):
    size = copies_ref.shape[0]
    used_rows, source_width = rows_ref.shape
    load_rows = pltpu.make_async_copy(rows_in, rows_ref, semaphores.at[0])
    load_blocks = pltpu.make_async_copy(blocks_in, blocks_ref, semaphores.at[1])
    load_tiles = pltpu.make_async_copy(tiles_in, tiles_ref, semaphores.at[2])
    for load in (load_rows, load_blocks, load_tiles):
        load.start()
    packed_column = lax.broadcasted_iota(jnp.int32, columns_ref.shape, 0)
    column_of = split(lax.broadcasted_iota(jnp.int32, columns_ref.shape, 1), months)[0]
    columns_ref[...] = (column_of == packed_column).astype(columns_ref.dtype)
    month_of_row = split(lax.broadcasted_iota(jnp.int32, same_ref.shape, 0), months)[1]
    month_of_column = split(lax.broadcasted_iota(jnp.int32, same_ref.shape, 1), months)[1]
    same_ref[...] = (month_of_row == month_of_column).astype(same_ref.dtype)
    copies_ref[...] = jnp.zeros(copies_ref.shape, copies_ref.dtype)
    load_rows.wait()

    def copy(owner):
        copies_ref[owner, :used_rows, :source_width] = rows_ref[...]

    each(size, copy)
    arrange(size, months, load_blocks, load_tiles, blocks_ref, tiles_ref, sorted_ref, pick_ref)


def tile_sums(histories_ref, pick_ref, columns_ref, same_ref, sorted_ref, coded_ref):
    size, packed_rows, packed_width = histories_ref.shape
    half_count = sorted_ref.shape[0] // 3
    own_blocks = half_count * 2 // size
    height = pick_ref.shape[0] // SOURCES
    cell_count = coded_ref.shape[2]
    coded_rows = own_blocks * height

    histories = histories_ref[...].reshape(size * packed_rows, packed_width)
    tall = jnp.dot(pick_ref[...], histories, preferred_element_type=jnp.float32)
    wide = jnp.dot(tall.astype(jnp.bfloat16), columns_ref[...], preferred_element_type=jnp.float32)
    wide = (wide * same_ref[...]).astype(jnp.bfloat16)

    def product(which, start):
        tiles = jnp.concatenate([sorted_ref[start + block] for block in range(own_blocks)], axis=1)
        rows = wide[which * height : (which + 1) * height]
        return jnp.dot(rows, tiles, preferred_element_type=jnp.float32)

    def code(slot):
        owner = sums_device(slot, size)
        start = owner * own_blocks
        total = product(0, start)
        if isinstance(slot, int):
            if owner >= size // 2:
                total += product(1, half_count + start)
        else:
            upper = product(1, half_count + jnp.maximum(start, half_count))
            total += jnp.where(owner >= size // 2, upper, 0.0)
        values = [total[:, block * cell_count : (block + 1) * cell_count] for block in range(own_blocks)]
        top = jnp.abs(values[0])
        for value in values[1:]:
            top = jnp.maximum(top, jnp.abs(value))
        top = jnp.max(top, axis=0, keepdims=True)
        level = jnp.ceil(jnp.log2(jnp.maximum(top, SMALLEST)) * LEVELS)
        half = jnp.exp2(level * (-0.5 / LEVELS))
        for block, value in enumerate(values):
            steps = jnp.round(value * half * (half * STEPS))
            coded_ref[slot, pl.ds(block * height, height)] = steps.astype(jnp.int32).astype(jnp.int16)
        spread = jnp.broadcast_to(level.astype(jnp.int32), (SCALE_ROWS, cell_count))
        coded_ref[slot, pl.ds(coded_rows, SCALE_ROWS)] = spread.astype(jnp.int16)

    each(size, code)


def add_parts(coded_ref, total_ref):
    size = coded_ref.shape[0]
    own_blocks, height, cell_count = total_ref.shape
    coded_rows = own_blocks * height
    total_ref[...] = jnp.zeros(total_ref.shape, total_ref.dtype)

    def add(slot):
        level = coded_ref[slot, pl.ds(coded_rows, SCALE_ROWS)].astype(jnp.int32).astype(jnp.float32)[:1]
        half = jnp.exp2(level * (0.5 / LEVELS))
        for block in range(own_blocks):
            steps = coded_ref[slot, pl.ds(block * height, height)].astype(jnp.int32)
            total_ref[block] += steps.astype(jnp.float32) * (half * (1.0 / STEPS)) * half

    each(size, add)


def shards(propagator, tile_blocks, histories):
    size = lax.axis_size("tm")
    own_blocks, tracer_count, source_width = histories.shape
    slot_count, source_width, months, cell_count = propagator.shape
    block_count = size * own_blocks
    height = tracer_count * months
    tile_height = source_width * months

    used_rows = tracer_count * own_blocks
    packed_rows = used_rows + -used_rows % 16
    packed_width = source_width + -source_width % 128
    rows, blocks, tiles = (
        pltpu.with_memory_space_constraint(value, pltpu.HBM)
        for value in (
            jnp.swapaxes(histories, 0, 1).reshape(used_rows, source_width),
            tile_blocks.T,
            propagator.reshape(slot_count, tile_height, cell_count),
        )
    )
    vmem = pl.BlockSpec(memory_space=pltpu.VMEM)
    hbm = pl.BlockSpec(memory_space=pltpu.HBM)
    copies, sorted_tiles, pick, columns, same = pl.pallas_call(
        lambda *refs: prepare(months, *refs),
        out_shape=[
            jax.ShapeDtypeStruct((size, packed_rows, packed_width), rows.dtype),
            jax.ShapeDtypeStruct((block_count + block_count // 2, tile_height, cell_count), tiles.dtype),
            jax.ShapeDtypeStruct((SOURCES * height, size * packed_rows), jnp.bfloat16),
            jax.ShapeDtypeStruct((packed_width, tile_height), jnp.bfloat16),
            jax.ShapeDtypeStruct((SOURCES * height, tile_height), jnp.float32),
        ],
        in_specs=[hbm] * 3,
        out_specs=[vmem] * 5,
        scratch_shapes=[
            pltpu.VMEM(rows.shape, rows.dtype),
            pltpu.SMEM(blocks.shape, blocks.dtype),
            pltpu.VMEM(tiles.shape, tiles.dtype),
            pltpu.SemaphoreType.DMA((3,)),
        ],
        compiler_params=pltpu.CompilerParams(vmem_limit_bytes=24 * 1024 * 1024),
        cost_estimate=pl.CostEstimate(flops=0, bytes_accessed=tiles.size * 4, transcendentals=0),
    )(rows, blocks, tiles)

    inner = [device for device in range(1, size) if device != centre(size)]
    received = exchange(copies, [centre(size)] + inner + [0])

    coded = pl.pallas_call(
        tile_sums,
        out_shape=jax.ShapeDtypeStruct((size, own_blocks * height + SCALE_ROWS, cell_count), jnp.int16),
        in_specs=[vmem] * 5,
        out_specs=vmem,
        compiler_params=pltpu.CompilerParams(vmem_limit_bytes=20 * 1024 * 1024),
        cost_estimate=pl.CostEstimate(
            flops=2 * slot_count * height * tile_height * cell_count,
            bytes_accessed=propagator.size * 4,
            transcendentals=0,
        ),
    )(received, pick, columns, same, sorted_tiles)

    owned = pl.pallas_call(
        add_parts,
        out_shape=jax.ShapeDtypeStruct((own_blocks, height, cell_count), jnp.float32),
        in_specs=[vmem],
        out_specs=vmem,
        compiler_params=pltpu.CompilerParams(vmem_limit_bytes=16 * 1024 * 1024),
    )(exchange(coded, [sums_device(slot, size) for slot in range(size)]))
    return owned.reshape(own_blocks, tracer_count, months, cell_count)


def solution(mesh):
    in_specs = (
        P(("groups", "tm"), None, None, "cells"),
        P(("groups", "tm"), None),
        P("tm", None, None),
    )
    out_specs = P(("groups", "tm"), None, None, "cells")
    return jax.shard_map(shards, mesh=mesh, in_specs=in_specs, out_specs=out_specs, check_vma=False)
```

```python
import jax
import jax.numpy as jnp
from jax import lax
from jax.experimental import pallas as pl
from jax.experimental.pallas import tpu as pltpu
from jax.sharding import PartitionSpec as P

STEPS = 32700.0
LEVELS = 128
SMALLEST = 2.0**-126
SCALE_ROWS = 8
WRITTEN_OUT = 17
SOURCES = 2


def centre(size):
    return size * 5 // 8


def history_slot(device, size):
    after = device - (device > centre(size)).astype(jnp.int32)
    return jnp.where(device == centre(size), 0, jnp.where(device == 0, size - 1, after))


def sums_device(slot, size):
    if isinstance(slot, int):
        return centre(size) if slot == 0 else size - slot - (size - slot <= centre(size))
    after = size - slot - (size - slot <= centre(size)).astype(jnp.int32)
    return jnp.where(slot == 0, centre(size), after)


def exchange(value, order):
    return lax.all_to_all(value, "tm", 0, 0, axis_index_groups=[order], tiled=True)


def split(value, divisor):
    if divisor & (divisor - 1):
        return lax.div(value, jnp.full_like(value, divisor)), lax.rem(value, jnp.full_like(value, divisor))
    return value >> (divisor.bit_length() - 1), value & (divisor - 1)


def each(count, body):
    if count <= WRITTEN_OUT:
        for index in range(count):
            body(index)
    else:
        lax.fori_loop(0, count, lambda index, carry: (body(index), carry)[1], 0)


def arrange(
    size, months, source_width, load_blocks, load_tiles, blocks_ref, tiles_ref, sorted_ref, pick_ref, columns_ref
):
    slot_count = tiles_ref.shape[0]
    half_count = sorted_ref.shape[0] // 3
    block_count = half_count * 2
    own_blocks = block_count // size
    height = pick_ref.shape[0] // SOURCES
    packed_rows = pick_ref.shape[1] // size
    group = sorted_ref.shape[0] // size

    def clear(index):
        sorted_ref[pl.ds(index * group, group)] = jnp.zeros((group,) + tiles_ref.shape[1:], sorted_ref.dtype)

    each(size, clear)
    tracer = split(lax.broadcasted_iota(jnp.int32, (height, pick_ref.shape[1]), 0), months)[0]
    offset = lax.broadcasted_iota(jnp.int32, (height, pick_ref.shape[1]), 1) - tracer
    column_of = split(lax.broadcasted_iota(jnp.int32, columns_ref.shape[1:], 1), months)[0]
    shift = lax.broadcasted_iota(jnp.int32, columns_ref.shape[1:], 0) - column_of
    load_blocks.wait()
    lower = jnp.minimum(blocks_ref[0, 0], block_count - 1 - blocks_ref[0, 0])

    def place_of(slot):
        return blocks_ref[1, slot] + jnp.where(blocks_ref[0, slot] == lower, 0, half_count)

    places = [place_of(slot) for slot in range(slot_count)] if slot_count <= WRITTEN_OUT else None
    for which, source in enumerate((lower, block_count - 1 - lower)):
        owner, block = split(source, own_blocks)
        picked = offset == history_slot(owner, size) * packed_rows
        pick_ref[pl.ds(which * height, height)] = picked.astype(pick_ref.dtype)
        columns_ref[which] = (shift == block * source_width).astype(columns_ref.dtype)
    load_tiles.wait()

    def place(slot):
        sorted_ref[places[slot] if places else place_of(slot)] = tiles_ref[slot]

    each(slot_count, place)


def prepare(
    months,
    rows_in,
    blocks_in,
    tiles_in,
    copies_ref,
    sorted_ref,
    pick_ref,
    columns_ref,
    same_ref,
    rows_ref,
    padded_ref,
    blocks_ref,
    tiles_ref,
    semaphores,
):
    size, packed_rows, packed_width = copies_ref.shape
    used_rows, source_width = rows_ref.shape
    own_blocks = sorted_ref.shape[0] // 3 * 2 // size
    load_rows = pltpu.make_async_copy(rows_in, rows_ref, semaphores.at[0])
    load_blocks = pltpu.make_async_copy(blocks_in, blocks_ref, semaphores.at[1])
    load_tiles = pltpu.make_async_copy(tiles_in, tiles_ref, semaphores.at[2])
    for load in (load_rows, load_blocks, load_tiles):
        load.start()
    month_of_row = split(lax.broadcasted_iota(jnp.int32, same_ref.shape, 0), months)[1]
    month_of_column = split(lax.broadcasted_iota(jnp.int32, same_ref.shape, 1), months)[1]
    same_ref[...] = (month_of_row == month_of_column).astype(same_ref.dtype)
    padded_ref[...] = jnp.zeros(padded_ref.shape, padded_ref.dtype)
    taker = (packed_rows, padded_ref.shape[0])
    placer = (padded_ref.shape[1], packed_width)
    take = lax.broadcasted_iota(jnp.int32, taker, 1) - lax.broadcasted_iota(jnp.int32, taker, 0) * own_blocks
    put = lax.broadcasted_iota(jnp.int32, placer, 1) - lax.broadcasted_iota(jnp.int32, placer, 0)
    load_rows.wait()
    padded_ref[:used_rows, :source_width] = rows_ref[...]
    packed = jnp.zeros((packed_rows, packed_width), jnp.float32)
    for block in range(own_blocks):
        taken = jnp.dot((take == block).astype(padded_ref.dtype), padded_ref[...], preferred_element_type=jnp.float32)
        packed += jnp.dot(
            taken.astype(padded_ref.dtype),
            (put == block * source_width).astype(padded_ref.dtype),
            preferred_element_type=jnp.float32,
        )
    packed = packed.astype(copies_ref.dtype)

    def copy(owner):
        copies_ref[owner] = packed

    each(size, copy)
    arrange(
        size,
        months,
        source_width,
        load_blocks,
        load_tiles,
        blocks_ref,
        tiles_ref,
        sorted_ref,
        pick_ref,
        columns_ref,
    )


def tile_sums(histories_ref, pick_ref, columns_ref, same_ref, sorted_ref, coded_ref):
    size, packed_rows, packed_width = histories_ref.shape
    half_count = sorted_ref.shape[0] // 3
    own_blocks = half_count * 2 // size
    height = pick_ref.shape[0] // SOURCES
    cell_count = coded_ref.shape[2]
    coded_rows = own_blocks * height

    histories = histories_ref[...].reshape(size * packed_rows, packed_width)
    tall = jnp.dot(pick_ref[...], histories, preferred_element_type=jnp.float32)
    tall = tall.astype(jnp.bfloat16)
    wide = []
    for which in range(SOURCES):
        rows = tall[which * height : (which + 1) * height]
        widened = jnp.dot(rows, columns_ref[which], preferred_element_type=jnp.float32)
        wide.append((widened * same_ref[...]).astype(jnp.bfloat16))

    def product(which, start):
        tiles = jnp.concatenate([sorted_ref[start + block] for block in range(own_blocks)], axis=1)
        return jnp.dot(wide[which], tiles, preferred_element_type=jnp.float32)

    def code(slot):
        owner = sums_device(slot, size)
        start = owner * own_blocks
        total = product(0, start)
        if isinstance(slot, int):
            if owner >= size // 2:
                total += product(1, half_count + start)
        else:
            upper = product(1, half_count + jnp.maximum(start, half_count))
            total += jnp.where(owner >= size // 2, upper, 0.0)
        values = [total[:, block * cell_count : (block + 1) * cell_count] for block in range(own_blocks)]
        top = jnp.abs(values[0])
        for value in values[1:]:
            top = jnp.maximum(top, jnp.abs(value))
        top = jnp.max(top, axis=0, keepdims=True)
        level = jnp.ceil(jnp.log2(jnp.maximum(top, SMALLEST)) * LEVELS)
        half = jnp.exp2(level * (-0.5 / LEVELS))
        for block, value in enumerate(values):
            steps = jnp.round(value * half * (half * STEPS))
            coded_ref[slot, pl.ds(block * height, height)] = steps.astype(jnp.int32).astype(jnp.int16)
        spread = jnp.broadcast_to(level.astype(jnp.int32), (SCALE_ROWS, cell_count))
        coded_ref[slot, pl.ds(coded_rows, SCALE_ROWS)] = spread.astype(jnp.int16)

    each(size, code)


def add_parts(coded_ref, total_ref):
    size = coded_ref.shape[0]
    own_blocks, height, cell_count = total_ref.shape
    coded_rows = own_blocks * height
    total_ref[...] = jnp.zeros(total_ref.shape, total_ref.dtype)

    def add(slot):
        level = coded_ref[slot, pl.ds(coded_rows, SCALE_ROWS)].astype(jnp.int32).astype(jnp.float32)[:1]
        half = jnp.exp2(level * (0.5 / LEVELS))
        for block in range(own_blocks):
            steps = coded_ref[slot, pl.ds(block * height, height)].astype(jnp.int32)
            total_ref[block] += steps.astype(jnp.float32) * (half * (1.0 / STEPS)) * half

    each(size, add)


def shards(propagator, tile_blocks, histories):
    size = lax.axis_size("tm")
    own_blocks, tracer_count, source_width = histories.shape
    slot_count, source_width, months, cell_count = propagator.shape
    block_count = size * own_blocks
    height = tracer_count * months
    tile_height = source_width * months

    used_rows = tracer_count * own_blocks
    padded_shape = (used_rows + -used_rows % 16, source_width + -source_width % 128)
    packed_rows = tracer_count + -tracer_count % 16
    packed_width = own_blocks * source_width + -(own_blocks * source_width) % 128
    rows, blocks, tiles = (
        pltpu.with_memory_space_constraint(value, pltpu.HBM)
        for value in (
            jnp.swapaxes(histories, 0, 1).reshape(used_rows, source_width),
            tile_blocks.T,
            propagator.reshape(slot_count, tile_height, cell_count),
        )
    )
    vmem = pl.BlockSpec(memory_space=pltpu.VMEM)
    hbm = pl.BlockSpec(memory_space=pltpu.HBM)
    copies, sorted_tiles, pick, columns, same = pl.pallas_call(
        lambda *refs: prepare(months, *refs),
        out_shape=[
            jax.ShapeDtypeStruct((size, packed_rows, packed_width), rows.dtype),
            jax.ShapeDtypeStruct((block_count + block_count // 2, tile_height, cell_count), tiles.dtype),
            jax.ShapeDtypeStruct((SOURCES * height, size * packed_rows), jnp.bfloat16),
            jax.ShapeDtypeStruct((SOURCES, packed_width, tile_height), jnp.bfloat16),
            jax.ShapeDtypeStruct((height, tile_height), jnp.float32),
        ],
        in_specs=[hbm] * 3,
        out_specs=[vmem] * 5,
        scratch_shapes=[
            pltpu.VMEM(rows.shape, rows.dtype),
            pltpu.VMEM(padded_shape, rows.dtype),
            pltpu.SMEM(blocks.shape, blocks.dtype),
            pltpu.VMEM(tiles.shape, tiles.dtype),
            pltpu.SemaphoreType.DMA((3,)),
        ],
        compiler_params=pltpu.CompilerParams(vmem_limit_bytes=24 * 1024 * 1024),
        cost_estimate=pl.CostEstimate(flops=0, bytes_accessed=tiles.size * 4, transcendentals=0),
    )(rows, blocks, tiles)

    inner = [device for device in range(1, size) if device != centre(size)]
    received = exchange(copies, [centre(size)] + inner + [0])

    coded = pl.pallas_call(
        tile_sums,
        out_shape=jax.ShapeDtypeStruct((size, own_blocks * height + SCALE_ROWS, cell_count), jnp.int16),
        in_specs=[vmem] * 5,
        out_specs=vmem,
        compiler_params=pltpu.CompilerParams(vmem_limit_bytes=20 * 1024 * 1024),
        cost_estimate=pl.CostEstimate(
            flops=2 * slot_count * height * tile_height * cell_count,
            bytes_accessed=propagator.size * 4,
            transcendentals=0,
        ),
    )(received, pick, columns, same, sorted_tiles)

    owned = pl.pallas_call(
        add_parts,
        out_shape=jax.ShapeDtypeStruct((own_blocks, height, cell_count), jnp.float32),
        in_specs=[vmem],
        out_specs=vmem,
        compiler_params=pltpu.CompilerParams(vmem_limit_bytes=16 * 1024 * 1024),
    )(exchange(coded, [sums_device(slot, size) for slot in range(size)]))
    return owned.reshape(own_blocks, tracer_count, months, cell_count)


def solution(mesh):
    in_specs = (
        P(("groups", "tm"), None, None, "cells"),
        P(("groups", "tm"), None),
        P("tm", None, None),
    )
    out_specs = P(("groups", "tm"), None, None, "cells")
    return jax.shard_map(shards, mesh=mesh, in_specs=in_specs, out_specs=out_specs, check_vma=False)
```

```python
import jax
import jax.numpy as jnp
from jax import lax
from jax.experimental import pallas as pl
from jax.experimental.pallas import tpu as pltpu
from jax.sharding import PartitionSpec as P

STEPS = 32700.0
LEVELS = 128
SMALLEST = 2.0**-126
SCALE_ROWS = 8
WRITTEN_OUT = 17
SOURCES = 2


def centre(size):
    return size * 5 // 8


def history_slot(device, size):
    after = device - (device > centre(size)).astype(jnp.int32)
    return jnp.where(device == centre(size), 0, jnp.where(device == 0, size - 1, after))


def sums_device(slot, size):
    if isinstance(slot, int):
        return centre(size) if slot == 0 else size - slot - (size - slot <= centre(size))
    after = size - slot - (size - slot <= centre(size)).astype(jnp.int32)
    return jnp.where(slot == 0, centre(size), after)


def exchange(value, order):
    return lax.all_to_all(value, "tm", 0, 0, axis_index_groups=[order], tiled=True)


def split(value, divisor):
    if divisor & (divisor - 1):
        return lax.div(value, jnp.full_like(value, divisor)), lax.rem(value, jnp.full_like(value, divisor))
    return value >> (divisor.bit_length() - 1), value & (divisor - 1)


def each(count, body):
    if count <= WRITTEN_OUT:
        for index in range(count):
            body(index)
    else:
        lax.fori_loop(0, count, lambda index, carry: (body(index), carry)[1], 0)


def arrange(
    size, months, source_width, load_blocks, load_tiles, blocks_ref, tiles_ref, sorted_ref, pick_ref, columns_ref
):
    slot_count = tiles_ref.shape[0]
    half_count = sorted_ref.shape[0] // 3
    block_count = half_count * 2
    own_blocks = block_count // size
    height = pick_ref.shape[0] // SOURCES
    packed_rows = pick_ref.shape[1] // size
    group = sorted_ref.shape[0] // size

    def clear(index):
        sorted_ref[pl.ds(index * group, group)] = jnp.zeros((group,) + tiles_ref.shape[1:], sorted_ref.dtype)

    each(size, clear)
    tracer = split(lax.broadcasted_iota(jnp.int32, (height, pick_ref.shape[1]), 0), months)[0]
    offset = lax.broadcasted_iota(jnp.int32, (height, pick_ref.shape[1]), 1) - tracer
    column_of = split(lax.broadcasted_iota(jnp.int32, columns_ref.shape[1:], 1), months)[0]
    shift = lax.broadcasted_iota(jnp.int32, columns_ref.shape[1:], 0) - column_of
    load_blocks.wait()
    lower = jnp.minimum(blocks_ref[0, 0], block_count - 1 - blocks_ref[0, 0])

    def place_of(slot):
        return blocks_ref[1, slot] + jnp.where(blocks_ref[0, slot] == lower, 0, half_count)

    places = [place_of(slot) for slot in range(slot_count)] if slot_count <= WRITTEN_OUT else None
    for which, source in enumerate((lower, block_count - 1 - lower)):
        owner, block = split(source, own_blocks)
        picked = offset == history_slot(owner, size) * packed_rows
        pick_ref[pl.ds(which * height, height)] = picked.astype(pick_ref.dtype)
        columns_ref[which] = (shift == block * source_width).astype(columns_ref.dtype)
    load_tiles.wait()

    def place(slot):
        sorted_ref[places[slot] if places else place_of(slot)] = tiles_ref[slot]

    each(slot_count, place)


def prepare(
    months,
    rows_in,
    blocks_in,
    tiles_in,
    copies_ref,
    sorted_ref,
    pick_ref,
    columns_ref,
    same_ref,
    rows_ref,
    padded_ref,
    blocks_ref,
    tiles_ref,
    semaphores,
):
    size, packed_rows, packed_width = copies_ref.shape
    used_rows, source_width = rows_ref.shape
    own_blocks = sorted_ref.shape[0] // 3 * 2 // size
    load_rows = pltpu.make_async_copy(rows_in, rows_ref, semaphores.at[0])
    load_blocks = pltpu.make_async_copy(blocks_in, blocks_ref, semaphores.at[1])
    load_tiles = pltpu.make_async_copy(tiles_in, tiles_ref, semaphores.at[2])
    for load in (load_rows, load_blocks, load_tiles):
        load.start()
    month_of_row = split(lax.broadcasted_iota(jnp.int32, same_ref.shape, 0), months)[1]
    month_of_column = split(lax.broadcasted_iota(jnp.int32, same_ref.shape, 1), months)[1]
    same_ref[...] = (month_of_row == month_of_column).astype(same_ref.dtype)
    padded_ref[...] = jnp.zeros(padded_ref.shape, padded_ref.dtype)
    taker = (packed_rows, padded_ref.shape[0])
    placer = (padded_ref.shape[1], packed_width)
    take = lax.broadcasted_iota(jnp.int32, taker, 1) - lax.broadcasted_iota(jnp.int32, taker, 0) * own_blocks
    put = lax.broadcasted_iota(jnp.int32, placer, 1) - lax.broadcasted_iota(jnp.int32, placer, 0)
    load_rows.wait()
    padded_ref[:used_rows, :source_width] = rows_ref[...]
    packed = jnp.zeros((packed_rows, packed_width), jnp.float32)
    for block in range(own_blocks):
        taken = jnp.dot((take == block).astype(padded_ref.dtype), padded_ref[...], preferred_element_type=jnp.float32)
        packed += jnp.dot(
            taken.astype(padded_ref.dtype),
            (put == block * source_width).astype(padded_ref.dtype),
            preferred_element_type=jnp.float32,
        )
    packed = packed.astype(copies_ref.dtype)

    def copy(owner):
        copies_ref[owner] = packed

    each(size, copy)
    arrange(
        size,
        months,
        source_width,
        load_blocks,
        load_tiles,
        blocks_ref,
        tiles_ref,
        sorted_ref,
        pick_ref,
        columns_ref,
    )


def tile_sums(histories_ref, pick_ref, columns_ref, same_ref, sorted_ref, coded_ref):
    size, packed_rows, packed_width = histories_ref.shape
    half_count = sorted_ref.shape[0] // 3
    own_blocks = half_count * 2 // size
    height = pick_ref.shape[0] // SOURCES
    cell_count = coded_ref.shape[2]
    coded_rows = own_blocks * height

    histories = histories_ref[...].reshape(size * packed_rows, packed_width)
    tall = jnp.dot(pick_ref[...], histories, preferred_element_type=jnp.float32)
    tall = tall.astype(jnp.bfloat16)
    wide = []
    for which in range(SOURCES):
        rows = tall[which * height : (which + 1) * height]
        widened = jnp.dot(rows, columns_ref[which], preferred_element_type=jnp.float32)
        wide.append((widened * same_ref[...]).astype(jnp.bfloat16))

    def product(which, start):
        tiles = jnp.concatenate([sorted_ref[start + block] for block in range(own_blocks)], axis=1)
        return jnp.dot(wide[which], tiles, preferred_element_type=jnp.float32)

    def code(slot):
        owner = sums_device(slot, size)
        start = owner * own_blocks
        total = product(0, start)
        if isinstance(slot, int):
            if owner >= size // 2:
                total += product(1, half_count + start)
        else:
            upper = product(1, half_count + jnp.maximum(start, half_count))
            total += jnp.where(owner >= size // 2, upper, 0.0)
        values = [total[:, block * cell_count : (block + 1) * cell_count] for block in range(own_blocks)]
        top = jnp.abs(values[0])
        for value in values[1:]:
            top = jnp.maximum(top, jnp.abs(value))
        top = jnp.max(top, axis=0, keepdims=True)
        level = jnp.ceil(jnp.log2(jnp.maximum(top, SMALLEST)) * LEVELS)
        half = jnp.exp2(level * (-0.5 / LEVELS))
        for block, value in enumerate(values):
            steps = jnp.round(value * half * (half * STEPS))
            coded_ref[slot, pl.ds(block * height, height)] = steps.astype(jnp.int32).astype(jnp.int16)
        spread = jnp.broadcast_to(level.astype(jnp.int32), (SCALE_ROWS, cell_count))
        coded_ref[slot, pl.ds(coded_rows, SCALE_ROWS)] = spread.astype(jnp.int16)

    each(size, code)


def add_parts(coded_ref, total_out, total_ref, semaphores):
    size = coded_ref.shape[0]
    own_blocks, height, cell_count = total_ref.shape
    stores = []
    for block in range(own_blocks):

        def add(slot, total):
            level = coded_ref[slot, pl.ds(own_blocks * height, SCALE_ROWS)].astype(jnp.int32)
            half = jnp.exp2(level.astype(jnp.float32)[:1] * (0.5 / LEVELS))
            steps = coded_ref[slot, pl.ds(block * height, height)].astype(jnp.int32)
            return total + steps.astype(jnp.float32) * (half * (1.0 / STEPS)) * half

        total = jnp.zeros((height, cell_count), jnp.float32)
        if size <= WRITTEN_OUT:
            for slot in range(size):
                total = add(slot, total)
        else:
            total = lax.fori_loop(0, size, add, total)
        total_ref[block] = total
        stores.append(pltpu.make_async_copy(total_ref.at[block], total_out.at[block], semaphores.at[block]))
        stores[-1].start()
    for store in stores:
        store.wait()


def shards(propagator, tile_blocks, histories):
    size = lax.axis_size("tm")
    own_blocks, tracer_count, source_width = histories.shape
    slot_count, source_width, months, cell_count = propagator.shape
    block_count = size * own_blocks
    height = tracer_count * months
    tile_height = source_width * months

    used_rows = tracer_count * own_blocks
    padded_shape = (used_rows + -used_rows % 16, source_width + -source_width % 128)
    packed_rows = tracer_count + -tracer_count % 16
    packed_width = own_blocks * source_width + -(own_blocks * source_width) % 128
    rows, blocks, tiles = (
        pltpu.with_memory_space_constraint(value, pltpu.HBM)
        for value in (
            jnp.swapaxes(histories, 0, 1).reshape(used_rows, source_width),
            tile_blocks.T,
            propagator.reshape(slot_count, tile_height, cell_count),
        )
    )
    vmem = pl.BlockSpec(memory_space=pltpu.VMEM)
    hbm = pl.BlockSpec(memory_space=pltpu.HBM)
    copies, sorted_tiles, pick, columns, same = pl.pallas_call(
        lambda *refs: prepare(months, *refs),
        out_shape=[
            jax.ShapeDtypeStruct((size, packed_rows, packed_width), rows.dtype),
            jax.ShapeDtypeStruct((block_count + block_count // 2, tile_height, cell_count), tiles.dtype),
            jax.ShapeDtypeStruct((SOURCES * height, size * packed_rows), jnp.bfloat16),
            jax.ShapeDtypeStruct((SOURCES, packed_width, tile_height), jnp.bfloat16),
            jax.ShapeDtypeStruct((height, tile_height), jnp.float32),
        ],
        in_specs=[hbm] * 3,
        out_specs=[vmem] * 5,
        scratch_shapes=[
            pltpu.VMEM(rows.shape, rows.dtype),
            pltpu.VMEM(padded_shape, rows.dtype),
            pltpu.SMEM(blocks.shape, blocks.dtype),
            pltpu.VMEM(tiles.shape, tiles.dtype),
            pltpu.SemaphoreType.DMA((3,)),
        ],
        compiler_params=pltpu.CompilerParams(vmem_limit_bytes=24 * 1024 * 1024),
        cost_estimate=pl.CostEstimate(flops=0, bytes_accessed=tiles.size * 4, transcendentals=0),
    )(rows, blocks, tiles)

    inner = [device for device in range(1, size) if device != centre(size)]
    received = exchange(copies, [centre(size)] + inner + [0])

    coded = pl.pallas_call(
        tile_sums,
        out_shape=jax.ShapeDtypeStruct((size, own_blocks * height + SCALE_ROWS, cell_count), jnp.int16),
        in_specs=[vmem] * 5,
        out_specs=vmem,
        compiler_params=pltpu.CompilerParams(vmem_limit_bytes=20 * 1024 * 1024),
        cost_estimate=pl.CostEstimate(
            flops=2 * slot_count * height * tile_height * cell_count,
            bytes_accessed=propagator.size * 4,
            transcendentals=0,
        ),
    )(received, pick, columns, same, sorted_tiles)

    owned = pl.pallas_call(
        add_parts,
        out_shape=jax.ShapeDtypeStruct((own_blocks, height, cell_count), jnp.float32),
        in_specs=[vmem],
        out_specs=hbm,
        scratch_shapes=[
            pltpu.VMEM((own_blocks, height, cell_count), jnp.float32),
            pltpu.SemaphoreType.DMA((own_blocks,)),
        ],
        compiler_params=pltpu.CompilerParams(vmem_limit_bytes=16 * 1024 * 1024),
    )(exchange(coded, [sums_device(slot, size) for slot in range(size)]))
    return owned.reshape(own_blocks, tracer_count, months, cell_count)


def solution(mesh):
    in_specs = (
        P(("groups", "tm"), None, None, "cells"),
        P(("groups", "tm"), None),
        P("tm", None, None),
    )
    out_specs = P(("groups", "tm"), None, None, "cells")
    return jax.shard_map(shards, mesh=mesh, in_specs=in_specs, out_specs=out_specs, check_vma=False)
```

```python
import jax
import jax.numpy as jnp
from jax import lax
from jax.experimental import pallas as pl
from jax.experimental.pallas import tpu as pltpu
from jax.sharding import PartitionSpec as P

STEPS = 32700.0
LEVELS = 128
SMALLEST = 2.0**-126
SCALE_ROWS = 8
WRITTEN_OUT = 17
SOURCES = 2


def centre(size):
    return size * 5 // 8


def history_slot(device, size):
    after = device - (device > centre(size)).astype(jnp.int32)
    return jnp.where(device == centre(size), 0, jnp.where(device == 0, size - 1, after))


def sums_device(slot, size):
    after = slot - (slot > size // 2) * 1
    if isinstance(slot, int):
        return centre(size) if slot == 0 else 0 if slot == size // 2 else after + (after >= centre(size))
    after = after + (after >= centre(size)).astype(jnp.int32)
    return jnp.where(slot == 0, centre(size), jnp.where(slot == size // 2, 0, after))


def exchange(value, order):
    return lax.all_to_all(value, "tm", 0, 0, axis_index_groups=[order], tiled=True)


def split(value, divisor):
    if divisor & (divisor - 1):
        return lax.div(value, jnp.full_like(value, divisor)), lax.rem(value, jnp.full_like(value, divisor))
    return value >> (divisor.bit_length() - 1), value & (divisor - 1)


def each(count, body):
    if count <= WRITTEN_OUT:
        for index in range(count):
            body(index)
    else:
        lax.fori_loop(0, count, lambda index, carry: (body(index), carry)[1], 0)


def arrange(
    size, months, source_width, load_blocks, load_tiles, blocks_ref, tiles_ref, sorted_ref, pick_ref, columns_ref
):
    slot_count = tiles_ref.shape[0]
    half_count = sorted_ref.shape[0] // 3
    block_count = half_count * 2
    own_blocks = block_count // size
    height = pick_ref.shape[0] // SOURCES
    packed_rows = pick_ref.shape[1] // size
    group = sorted_ref.shape[0] // size

    def clear(index):
        sorted_ref[pl.ds(index * group, group)] = jnp.zeros((group,) + tiles_ref.shape[1:], sorted_ref.dtype)

    each(size, clear)
    tracer = split(lax.broadcasted_iota(jnp.int32, (height, pick_ref.shape[1]), 0), months)[0]
    offset = lax.broadcasted_iota(jnp.int32, (height, pick_ref.shape[1]), 1) - tracer
    column_of = split(lax.broadcasted_iota(jnp.int32, columns_ref.shape[1:], 1), months)[0]
    shift = lax.broadcasted_iota(jnp.int32, columns_ref.shape[1:], 0) - column_of
    load_blocks.wait()
    lower = jnp.minimum(blocks_ref[0, 0], block_count - 1 - blocks_ref[0, 0])

    def place_of(slot):
        return blocks_ref[1, slot] + jnp.where(blocks_ref[0, slot] == lower, 0, half_count)

    places = [place_of(slot) for slot in range(slot_count)] if slot_count <= WRITTEN_OUT else None
    for which, source in enumerate((lower, block_count - 1 - lower)):
        owner, block = split(source, own_blocks)
        picked = offset == history_slot(owner, size) * packed_rows
        pick_ref[pl.ds(which * height, height)] = picked.astype(pick_ref.dtype)
        columns_ref[which] = (shift == block * source_width).astype(columns_ref.dtype)
    load_tiles.wait()

    def place(slot):
        sorted_ref[places[slot] if places else place_of(slot)] = tiles_ref[slot]

    each(slot_count, place)


def prepare(
    months,
    rows_in,
    blocks_in,
    tiles_in,
    copies_ref,
    sorted_ref,
    pick_ref,
    columns_ref,
    same_ref,
    rows_ref,
    padded_ref,
    blocks_ref,
    tiles_ref,
    semaphores,
):
    size, packed_rows, packed_width = copies_ref.shape
    used_rows, source_width = rows_ref.shape
    own_blocks = sorted_ref.shape[0] // 3 * 2 // size
    load_rows = pltpu.make_async_copy(rows_in, rows_ref, semaphores.at[0])
    load_blocks = pltpu.make_async_copy(blocks_in, blocks_ref, semaphores.at[1])
    load_tiles = pltpu.make_async_copy(tiles_in, tiles_ref, semaphores.at[2])
    for load in (load_rows, load_blocks, load_tiles):
        load.start()
    month_of_row = split(lax.broadcasted_iota(jnp.int32, same_ref.shape, 0), months)[1]
    month_of_column = split(lax.broadcasted_iota(jnp.int32, same_ref.shape, 1), months)[1]
    same_ref[...] = (month_of_row == month_of_column).astype(same_ref.dtype)
    padded_ref[...] = jnp.zeros(padded_ref.shape, padded_ref.dtype)
    taker = (packed_rows, padded_ref.shape[0])
    placer = (padded_ref.shape[1], packed_width)
    take = lax.broadcasted_iota(jnp.int32, taker, 1) - lax.broadcasted_iota(jnp.int32, taker, 0) * own_blocks
    put = lax.broadcasted_iota(jnp.int32, placer, 1) - lax.broadcasted_iota(jnp.int32, placer, 0)
    load_rows.wait()
    padded_ref[:used_rows, :source_width] = rows_ref[...]
    packed = jnp.zeros((packed_rows, packed_width), jnp.float32)
    for block in range(own_blocks):
        taken = jnp.dot((take == block).astype(padded_ref.dtype), padded_ref[...], preferred_element_type=jnp.float32)
        packed += jnp.dot(
            taken.astype(padded_ref.dtype),
            (put == block * source_width).astype(padded_ref.dtype),
            preferred_element_type=jnp.float32,
        )
    packed = packed.astype(copies_ref.dtype)

    def copy(owner):
        copies_ref[owner] = packed

    each(size, copy)
    arrange(
        size,
        months,
        source_width,
        load_blocks,
        load_tiles,
        blocks_ref,
        tiles_ref,
        sorted_ref,
        pick_ref,
        columns_ref,
    )


def tile_sums(histories_ref, pick_ref, columns_ref, same_ref, sorted_ref, coded_ref):
    size, packed_rows, packed_width = histories_ref.shape
    half_count = sorted_ref.shape[0] // 3
    own_blocks = half_count * 2 // size
    height = pick_ref.shape[0] // SOURCES
    cell_count = coded_ref.shape[2]
    coded_rows = own_blocks * height

    histories = histories_ref[...].reshape(size * packed_rows, packed_width)
    tall = jnp.dot(pick_ref[...], histories, preferred_element_type=jnp.float32)
    tall = tall.astype(jnp.bfloat16)
    wide = []
    for which in range(SOURCES):
        rows = tall[which * height : (which + 1) * height]
        widened = jnp.dot(rows, columns_ref[which], preferred_element_type=jnp.float32)
        wide.append((widened * same_ref[...]).astype(jnp.bfloat16))

    def product(which, start):
        tiles = jnp.concatenate([sorted_ref[start + block] for block in range(own_blocks)], axis=1)
        return jnp.dot(wide[which], tiles, preferred_element_type=jnp.float32)

    def code(slot):
        owner = sums_device(slot, size)
        start = owner * own_blocks
        total = product(0, start)
        if isinstance(slot, int):
            if owner >= size // 2:
                total += product(1, half_count + start)
        else:
            upper = product(1, half_count + jnp.maximum(start, half_count))
            total += jnp.where(owner >= size // 2, upper, 0.0)
        values = [total[:, block * cell_count : (block + 1) * cell_count] for block in range(own_blocks)]
        top = jnp.abs(values[0])
        for value in values[1:]:
            top = jnp.maximum(top, jnp.abs(value))
        top = jnp.max(top, axis=0, keepdims=True)
        level = jnp.ceil(jnp.log2(jnp.maximum(top, SMALLEST)) * LEVELS)
        half = jnp.exp2(level * (-0.5 / LEVELS))
        for block, value in enumerate(values):
            steps = jnp.round(value * half * (half * STEPS))
            coded_ref[slot, pl.ds(block * height, height)] = steps.astype(jnp.int32).astype(jnp.int16)
        spread = jnp.broadcast_to(level.astype(jnp.int32), (SCALE_ROWS, cell_count))
        coded_ref[slot, pl.ds(coded_rows, SCALE_ROWS)] = spread.astype(jnp.int16)

    each(size, code)


def add_parts(coded_ref, total_out, total_ref, semaphores):
    size = coded_ref.shape[0]
    own_blocks, height, cell_count = total_ref.shape
    stores = []
    for block in range(own_blocks):

        def add(slot, total):
            level = coded_ref[slot, pl.ds(own_blocks * height, SCALE_ROWS)].astype(jnp.int32)
            half = jnp.exp2(level.astype(jnp.float32)[:1] * (0.5 / LEVELS))
            steps = coded_ref[slot, pl.ds(block * height, height)].astype(jnp.int32)
            return total + steps.astype(jnp.float32) * (half * (1.0 / STEPS)) * half

        total = jnp.zeros((height, cell_count), jnp.float32)
        if size <= WRITTEN_OUT:
            for slot in range(size):
                total = add(slot, total)
        else:
            total = lax.fori_loop(0, size, add, total)
        total_ref[block] = total
        stores.append(pltpu.make_async_copy(total_ref.at[block], total_out.at[block], semaphores.at[block]))
        stores[-1].start()
    for store in stores:
        store.wait()


def shards(propagator, tile_blocks, histories):
    size = lax.axis_size("tm")
    own_blocks, tracer_count, source_width = histories.shape
    slot_count, source_width, months, cell_count = propagator.shape
    block_count = size * own_blocks
    height = tracer_count * months
    tile_height = source_width * months

    used_rows = tracer_count * own_blocks
    padded_shape = (used_rows + -used_rows % 16, source_width + -source_width % 128)
    packed_rows = tracer_count + -tracer_count % 16
    packed_width = own_blocks * source_width + -(own_blocks * source_width) % 128
    rows, blocks, tiles = (
        pltpu.with_memory_space_constraint(value, pltpu.HBM)
        for value in (
            jnp.swapaxes(histories, 0, 1).reshape(used_rows, source_width),
            tile_blocks.T,
            propagator.reshape(slot_count, tile_height, cell_count),
        )
    )
    vmem = pl.BlockSpec(memory_space=pltpu.VMEM)
    hbm = pl.BlockSpec(memory_space=pltpu.HBM)
    copies, sorted_tiles, pick, columns, same = pl.pallas_call(
        lambda *refs: prepare(months, *refs),
        out_shape=[
            jax.ShapeDtypeStruct((size, packed_rows, packed_width), rows.dtype),
            jax.ShapeDtypeStruct((block_count + block_count // 2, tile_height, cell_count), tiles.dtype),
            jax.ShapeDtypeStruct((SOURCES * height, size * packed_rows), jnp.bfloat16),
            jax.ShapeDtypeStruct((SOURCES, packed_width, tile_height), jnp.bfloat16),
            jax.ShapeDtypeStruct((height, tile_height), jnp.float32),
        ],
        in_specs=[hbm] * 3,
        out_specs=[vmem] * 5,
        scratch_shapes=[
            pltpu.VMEM(rows.shape, rows.dtype),
            pltpu.VMEM(padded_shape, rows.dtype),
            pltpu.SMEM(blocks.shape, blocks.dtype),
            pltpu.VMEM(tiles.shape, tiles.dtype),
            pltpu.SemaphoreType.DMA((3,)),
        ],
        compiler_params=pltpu.CompilerParams(vmem_limit_bytes=24 * 1024 * 1024),
        cost_estimate=pl.CostEstimate(flops=0, bytes_accessed=tiles.size * 4, transcendentals=0),
    )(rows, blocks, tiles)

    inner = [device for device in range(1, size) if device != centre(size)]
    received = exchange(copies, [centre(size)] + inner + [0])

    coded = pl.pallas_call(
        tile_sums,
        out_shape=jax.ShapeDtypeStruct((size, own_blocks * height + SCALE_ROWS, cell_count), jnp.int16),
        in_specs=[vmem] * 5,
        out_specs=vmem,
        compiler_params=pltpu.CompilerParams(vmem_limit_bytes=20 * 1024 * 1024),
        cost_estimate=pl.CostEstimate(
            flops=2 * slot_count * height * tile_height * cell_count,
            bytes_accessed=propagator.size * 4,
            transcendentals=0,
        ),
    )(received, pick, columns, same, sorted_tiles)

    owned = pl.pallas_call(
        add_parts,
        out_shape=jax.ShapeDtypeStruct((own_blocks, height, cell_count), jnp.float32),
        in_specs=[vmem],
        out_specs=hbm,
        scratch_shapes=[
            pltpu.VMEM((own_blocks, height, cell_count), jnp.float32),
            pltpu.SemaphoreType.DMA((own_blocks,)),
        ],
        compiler_params=pltpu.CompilerParams(vmem_limit_bytes=16 * 1024 * 1024),
    )(exchange(coded, [sums_device(slot, size) for slot in range(size)]))
    return owned.reshape(own_blocks, tracer_count, months, cell_count)


def solution(mesh):
    in_specs = (
        P(("groups", "tm"), None, None, "cells"),
        P(("groups", "tm"), None),
        P("tm", None, None),
    )
    out_specs = P(("groups", "tm"), None, None, "cells")
    return jax.shard_map(shards, mesh=mesh, in_specs=in_specs, out_specs=out_specs, check_vma=False)
```

```python
import jax
import jax.numpy as jnp
from jax import lax
from jax.experimental import pallas as pl
from jax.experimental.pallas import tpu as pltpu
from jax.sharding import PartitionSpec as P

STEPS = 32700.0
LEVELS = 128
SMALLEST = 2.0**-126
SCALE_ROWS = 8
WRITTEN_OUT = 17
SOURCES = 2


def centre(size):
    return size * 5 // 8


def history_order(size):
    inner = [device for device in range(1, size) if device != centre(size)]
    return [centre(size)] + inner[: size // 2 - 1] + [0] + inner[size // 2 - 1 :]


def history_slot(device, size):
    after = device - (device > centre(size)).astype(jnp.int32)
    after = after + (after >= size // 2).astype(jnp.int32)
    return jnp.where(device == centre(size), 0, jnp.where(device == 0, size // 2, after))


def sums_device(slot, size):
    if isinstance(slot, int):
        return centre(size) if slot == 0 else size - slot - (size - slot <= centre(size))
    after = size - slot - (size - slot <= centre(size)).astype(jnp.int32)
    return jnp.where(slot == 0, centre(size), after)


def exchange(value, order):
    return lax.all_to_all(value, "tm", 0, 0, axis_index_groups=[order], tiled=True)


def split(value, divisor):
    if divisor & (divisor - 1):
        return lax.div(value, jnp.full_like(value, divisor)), lax.rem(value, jnp.full_like(value, divisor))
    return value >> (divisor.bit_length() - 1), value & (divisor - 1)


def each(count, body):
    if count <= WRITTEN_OUT:
        for index in range(count):
            body(index)
    else:
        lax.fori_loop(0, count, lambda index, carry: (body(index), carry)[1], 0)


def arrange(
    size, months, source_width, load_blocks, load_tiles, blocks_ref, tiles_ref, sorted_ref, pick_ref, columns_ref
):
    slot_count = tiles_ref.shape[0]
    half_count = sorted_ref.shape[0] // 3
    block_count = half_count * 2
    own_blocks = block_count // size
    height = pick_ref.shape[0] // SOURCES
    packed_rows = pick_ref.shape[1] // size
    group = sorted_ref.shape[0] // size

    def clear(index):
        sorted_ref[pl.ds(index * group, group)] = jnp.zeros((group,) + tiles_ref.shape[1:], sorted_ref.dtype)

    each(size, clear)
    tracer = split(lax.broadcasted_iota(jnp.int32, (height, pick_ref.shape[1]), 0), months)[0]
    offset = lax.broadcasted_iota(jnp.int32, (height, pick_ref.shape[1]), 1) - tracer
    column_of = split(lax.broadcasted_iota(jnp.int32, columns_ref.shape[1:], 1), months)[0]
    shift = lax.broadcasted_iota(jnp.int32, columns_ref.shape[1:], 0) - column_of
    load_blocks.wait()
    lower = jnp.minimum(blocks_ref[0, 0], block_count - 1 - blocks_ref[0, 0])

    def place_of(slot):
        return blocks_ref[1, slot] + jnp.where(blocks_ref[0, slot] == lower, 0, half_count)

    places = [place_of(slot) for slot in range(slot_count)] if slot_count <= WRITTEN_OUT else None
    for which, source in enumerate((lower, block_count - 1 - lower)):
        owner, block = split(source, own_blocks)
        picked = offset == history_slot(owner, size) * packed_rows
        pick_ref[pl.ds(which * height, height)] = picked.astype(pick_ref.dtype)
        columns_ref[which] = (shift == block * source_width).astype(columns_ref.dtype)
    load_tiles.wait()

    def place(slot):
        sorted_ref[places[slot] if places else place_of(slot)] = tiles_ref[slot]

    each(slot_count, place)


def prepare(
    months,
    rows_in,
    blocks_in,
    tiles_in,
    copies_ref,
    sorted_ref,
    pick_ref,
    columns_ref,
    same_ref,
    rows_ref,
    padded_ref,
    blocks_ref,
    tiles_ref,
    semaphores,
):
    size, packed_rows, packed_width = copies_ref.shape
    used_rows, source_width = rows_ref.shape
    own_blocks = sorted_ref.shape[0] // 3 * 2 // size
    load_rows = pltpu.make_async_copy(rows_in, rows_ref, semaphores.at[0])
    load_blocks = pltpu.make_async_copy(blocks_in, blocks_ref, semaphores.at[1])
    load_tiles = pltpu.make_async_copy(tiles_in, tiles_ref, semaphores.at[2])
    for load in (load_rows, load_blocks, load_tiles):
        load.start()
    month_of_row = split(lax.broadcasted_iota(jnp.int32, same_ref.shape, 0), months)[1]
    month_of_column = split(lax.broadcasted_iota(jnp.int32, same_ref.shape, 1), months)[1]
    same_ref[...] = (month_of_row == month_of_column).astype(same_ref.dtype)
    padded_ref[...] = jnp.zeros(padded_ref.shape, padded_ref.dtype)
    taker = (packed_rows, padded_ref.shape[0])
    placer = (padded_ref.shape[1], packed_width)
    take = lax.broadcasted_iota(jnp.int32, taker, 1) - lax.broadcasted_iota(jnp.int32, taker, 0) * own_blocks
    put = lax.broadcasted_iota(jnp.int32, placer, 1) - lax.broadcasted_iota(jnp.int32, placer, 0)
    load_rows.wait()
    padded_ref[:used_rows, :source_width] = rows_ref[...]
    packed = jnp.zeros((packed_rows, packed_width), jnp.float32)
    for block in range(own_blocks):
        taken = jnp.dot((take == block).astype(padded_ref.dtype), padded_ref[...], preferred_element_type=jnp.float32)
        packed += jnp.dot(
            taken.astype(padded_ref.dtype),
            (put == block * source_width).astype(padded_ref.dtype),
            preferred_element_type=jnp.float32,
        )
    packed = packed.astype(copies_ref.dtype)

    def copy(owner):
        copies_ref[owner] = packed

    each(size, copy)
    arrange(
        size,
        months,
        source_width,
        load_blocks,
        load_tiles,
        blocks_ref,
        tiles_ref,
        sorted_ref,
        pick_ref,
        columns_ref,
    )


def tile_sums(histories_ref, pick_ref, columns_ref, same_ref, sorted_ref, coded_ref):
    size, packed_rows, packed_width = histories_ref.shape
    half_count = sorted_ref.shape[0] // 3
    own_blocks = half_count * 2 // size
    height = pick_ref.shape[0] // SOURCES
    cell_count = coded_ref.shape[2]
    coded_rows = own_blocks * height

    histories = histories_ref[...].reshape(size * packed_rows, packed_width)
    tall = jnp.dot(pick_ref[...], histories, preferred_element_type=jnp.float32)
    tall = tall.astype(jnp.bfloat16)
    wide = []
    for which in range(SOURCES):
        rows = tall[which * height : (which + 1) * height]
        widened = jnp.dot(rows, columns_ref[which], preferred_element_type=jnp.float32)
        wide.append((widened * same_ref[...]).astype(jnp.bfloat16))

    def product(which, start):
        tiles = jnp.concatenate([sorted_ref[start + block] for block in range(own_blocks)], axis=1)
        return jnp.dot(wide[which], tiles, preferred_element_type=jnp.float32)

    def code(slot):
        owner = sums_device(slot, size)
        start = owner * own_blocks
        total = product(0, start)
        if isinstance(slot, int):
            if owner >= size // 2:
                total += product(1, half_count + start)
        else:
            upper = product(1, half_count + jnp.maximum(start, half_count))
            total += jnp.where(owner >= size // 2, upper, 0.0)
        values = [total[:, block * cell_count : (block + 1) * cell_count] for block in range(own_blocks)]
        top = jnp.abs(values[0])
        for value in values[1:]:
            top = jnp.maximum(top, jnp.abs(value))
        top = jnp.max(top, axis=0, keepdims=True)
        level = jnp.ceil(jnp.log2(jnp.maximum(top, SMALLEST)) * LEVELS)
        half = jnp.exp2(level * (-0.5 / LEVELS))
        for block, value in enumerate(values):
            steps = jnp.round(value * half * (half * STEPS))
            coded_ref[slot, pl.ds(block * height, height)] = steps.astype(jnp.int32).astype(jnp.int16)
        spread = jnp.broadcast_to(level.astype(jnp.int32), (SCALE_ROWS, cell_count))
        coded_ref[slot, pl.ds(coded_rows, SCALE_ROWS)] = spread.astype(jnp.int16)

    each(size, code)


def add_parts(coded_ref, total_out, total_ref, semaphores):
    size = coded_ref.shape[0]
    own_blocks, height, cell_count = total_ref.shape
    stores = []
    for block in range(own_blocks):

        def add(slot, total):
            level = coded_ref[slot, pl.ds(own_blocks * height, SCALE_ROWS)].astype(jnp.int32)
            half = jnp.exp2(level.astype(jnp.float32)[:1] * (0.5 / LEVELS))
            steps = coded_ref[slot, pl.ds(block * height, height)].astype(jnp.int32)
            return total + steps.astype(jnp.float32) * (half * (1.0 / STEPS)) * half

        total = jnp.zeros((height, cell_count), jnp.float32)
        if size <= WRITTEN_OUT:
            for slot in range(size):
                total = add(slot, total)
        else:
            total = lax.fori_loop(0, size, add, total)
        total_ref[block] = total
        stores.append(pltpu.make_async_copy(total_ref.at[block], total_out.at[block], semaphores.at[block]))
        stores[-1].start()
    for store in stores:
        store.wait()


def shards(propagator, tile_blocks, histories):
    size = lax.axis_size("tm")
    own_blocks, tracer_count, source_width = histories.shape
    slot_count, source_width, months, cell_count = propagator.shape
    block_count = size * own_blocks
    height = tracer_count * months
    tile_height = source_width * months

    used_rows = tracer_count * own_blocks
    padded_shape = (used_rows + -used_rows % 16, source_width + -source_width % 128)
    packed_rows = tracer_count + -tracer_count % 16
    packed_width = own_blocks * source_width + -(own_blocks * source_width) % 128
    rows, blocks, tiles = (
        pltpu.with_memory_space_constraint(value, pltpu.HBM)
        for value in (
            jnp.swapaxes(histories, 0, 1).reshape(used_rows, source_width),
            tile_blocks.T,
            propagator.reshape(slot_count, tile_height, cell_count),
        )
    )
    vmem = pl.BlockSpec(memory_space=pltpu.VMEM)
    hbm = pl.BlockSpec(memory_space=pltpu.HBM)
    copies, sorted_tiles, pick, columns, same = pl.pallas_call(
        lambda *refs: prepare(months, *refs),
        out_shape=[
            jax.ShapeDtypeStruct((size, packed_rows, packed_width), rows.dtype),
            jax.ShapeDtypeStruct((block_count + block_count // 2, tile_height, cell_count), tiles.dtype),
            jax.ShapeDtypeStruct((SOURCES * height, size * packed_rows), jnp.bfloat16),
            jax.ShapeDtypeStruct((SOURCES, packed_width, tile_height), jnp.bfloat16),
            jax.ShapeDtypeStruct((height, tile_height), jnp.float32),
        ],
        in_specs=[hbm] * 3,
        out_specs=[vmem] * 5,
        scratch_shapes=[
            pltpu.VMEM(rows.shape, rows.dtype),
            pltpu.VMEM(padded_shape, rows.dtype),
            pltpu.SMEM(blocks.shape, blocks.dtype),
            pltpu.VMEM(tiles.shape, tiles.dtype),
            pltpu.SemaphoreType.DMA((3,)),
        ],
        compiler_params=pltpu.CompilerParams(vmem_limit_bytes=24 * 1024 * 1024),
        cost_estimate=pl.CostEstimate(flops=0, bytes_accessed=tiles.size * 4, transcendentals=0),
    )(rows, blocks, tiles)

    received = exchange(copies, history_order(size))

    coded = pl.pallas_call(
        tile_sums,
        out_shape=jax.ShapeDtypeStruct((size, own_blocks * height + SCALE_ROWS, cell_count), jnp.int16),
        in_specs=[vmem] * 5,
        out_specs=vmem,
        compiler_params=pltpu.CompilerParams(vmem_limit_bytes=20 * 1024 * 1024),
        cost_estimate=pl.CostEstimate(
            flops=2 * slot_count * height * tile_height * cell_count,
            bytes_accessed=propagator.size * 4,
            transcendentals=0,
        ),
    )(received, pick, columns, same, sorted_tiles)

    owned = pl.pallas_call(
        add_parts,
        out_shape=jax.ShapeDtypeStruct((own_blocks, height, cell_count), jnp.float32),
        in_specs=[vmem],
        out_specs=hbm,
        scratch_shapes=[
            pltpu.VMEM((own_blocks, height, cell_count), jnp.float32),
            pltpu.SemaphoreType.DMA((own_blocks,)),
        ],
        compiler_params=pltpu.CompilerParams(vmem_limit_bytes=16 * 1024 * 1024),
    )(exchange(coded, [sums_device(slot, size) for slot in range(size)]))
    return owned.reshape(own_blocks, tracer_count, months, cell_count)


def solution(mesh):
    in_specs = (
        P(("groups", "tm"), None, None, "cells"),
        P(("groups", "tm"), None),
        P("tm", None, None),
    )
    out_specs = P(("groups", "tm"), None, None, "cells")
    return jax.shard_map(shards, mesh=mesh, in_specs=in_specs, out_specs=out_specs, check_vma=False)
```

```python
import functools

import jax
import jax.numpy as jnp
from jax import lax
from jax.experimental import pallas as pl
from jax.experimental.pallas import tpu as pltpu
from jax.sharding import PartitionSpec as P

STEPS = 32700.0
LEVELS = 128
SMALLEST = 2.0**-126
SCALE_ROWS = 8
WRITTEN_OUT = 17
SOURCES = 2


def centre(size):
    return size * 5 // 8


def history_order(size):
    inner = [device for device in range(1, size) if device != centre(size)]
    return [centre(size)] + inner[: size // 2 - 1] + [0] + inner[size // 2 - 1 :]


def history_slot(device, size):
    after = device - (device > centre(size)).astype(jnp.int32)
    after = after + (after >= size // 2).astype(jnp.int32)
    return jnp.where(device == centre(size), 0, jnp.where(device == 0, size // 2, after))


def sums_device(slot, size):
    if isinstance(slot, int):
        return centre(size) if slot == 0 else size - slot - (size - slot <= centre(size))
    after = size - slot - (size - slot <= centre(size)).astype(jnp.int32)
    return jnp.where(slot == 0, centre(size), after)


def exchange(value, order):
    return lax.all_to_all(value, "tm", 0, 0, axis_index_groups=[order], tiled=True)


def split(value, divisor):
    if divisor & (divisor - 1):
        return lax.div(value, jnp.full_like(value, divisor)), lax.rem(value, jnp.full_like(value, divisor))
    return value >> (divisor.bit_length() - 1), value & (divisor - 1)


def each(count, body):
    if count <= WRITTEN_OUT:
        for index in range(count):
            body(index)
    else:
        lax.fori_loop(0, count, lambda index, carry: (body(index), carry)[1], 0)


def arrange(
    size, months, source_width, load_blocks, load_tiles, blocks_ref, tiles_ref, sorted_ref, pick_ref, columns_ref
):
    slot_count = tiles_ref.shape[0]
    half_count = sorted_ref.shape[0] // 3
    block_count = half_count * 2
    own_blocks = block_count // size
    height = pick_ref.shape[0] // SOURCES
    packed_rows = pick_ref.shape[1] // size
    group = sorted_ref.shape[0] // size

    def clear(index):
        sorted_ref[pl.ds(index * group, group)] = jnp.zeros((group,) + tiles_ref.shape[1:], sorted_ref.dtype)

    each(size, clear)
    tracer = split(lax.broadcasted_iota(jnp.int32, (height, pick_ref.shape[1]), 0), months)[0]
    offset = lax.broadcasted_iota(jnp.int32, (height, pick_ref.shape[1]), 1) - tracer
    column_of = split(lax.broadcasted_iota(jnp.int32, columns_ref.shape[1:], 1), months)[0]
    shift = lax.broadcasted_iota(jnp.int32, columns_ref.shape[1:], 0) - column_of
    load_blocks.wait()
    lower = jnp.minimum(blocks_ref[0, 0], block_count - 1 - blocks_ref[0, 0])

    def place_of(slot):
        return blocks_ref[1, slot] + jnp.where(blocks_ref[0, slot] == lower, 0, half_count)

    places = [place_of(slot) for slot in range(slot_count)] if slot_count <= WRITTEN_OUT else None
    for which, source in enumerate((lower, block_count - 1 - lower)):
        owner, block = split(source, own_blocks)
        picked = offset == history_slot(owner, size) * packed_rows
        pick_ref[pl.ds(which * height, height)] = picked.astype(pick_ref.dtype)
        columns_ref[which] = (shift == block * source_width).astype(columns_ref.dtype)
    load_tiles.wait()

    def place(slot):
        sorted_ref[places[slot] if places else place_of(slot)] = tiles_ref[slot]

    each(slot_count, place)


def prepare(
    months,
    rows_in,
    blocks_in,
    tiles_in,
    copies_ref,
    sorted_ref,
    pick_ref,
    columns_ref,
    same_ref,
    rows_ref,
    padded_ref,
    blocks_ref,
    tiles_ref,
    semaphores,
):
    size, packed_rows, packed_width = copies_ref.shape
    used_rows, source_width = rows_ref.shape
    own_blocks = sorted_ref.shape[0] // 3 * 2 // size
    load_rows = pltpu.make_async_copy(rows_in, rows_ref, semaphores.at[0])
    load_blocks = pltpu.make_async_copy(blocks_in, blocks_ref, semaphores.at[1])
    load_tiles = pltpu.make_async_copy(tiles_in, tiles_ref, semaphores.at[2])
    for load in (load_rows, load_blocks, load_tiles):
        load.start()
    month_of_row = split(lax.broadcasted_iota(jnp.int32, same_ref.shape, 0), months)[1]
    month_of_column = split(lax.broadcasted_iota(jnp.int32, same_ref.shape, 1), months)[1]
    same_ref[...] = (month_of_row == month_of_column).astype(same_ref.dtype)
    padded_ref[...] = jnp.zeros(padded_ref.shape, padded_ref.dtype)
    taker = (packed_rows, padded_ref.shape[0])
    placer = (padded_ref.shape[1], packed_width)
    take = lax.broadcasted_iota(jnp.int32, taker, 1) - lax.broadcasted_iota(jnp.int32, taker, 0) * own_blocks
    put = lax.broadcasted_iota(jnp.int32, placer, 1) - lax.broadcasted_iota(jnp.int32, placer, 0)
    load_rows.wait()
    padded_ref[:used_rows, :source_width] = rows_ref[...]
    packed = jnp.zeros((packed_rows, packed_width), jnp.float32)
    for block in range(own_blocks):
        taken = jnp.dot((take == block).astype(padded_ref.dtype), padded_ref[...], preferred_element_type=jnp.float32)
        packed += jnp.dot(
            taken.astype(padded_ref.dtype),
            (put == block * source_width).astype(padded_ref.dtype),
            preferred_element_type=jnp.float32,
        )
    packed = packed.astype(copies_ref.dtype)

    def copy(owner):
        copies_ref[owner] = packed

    each(size, copy)
    arrange(
        size,
        months,
        source_width,
        load_blocks,
        load_tiles,
        blocks_ref,
        tiles_ref,
        sorted_ref,
        pick_ref,
        columns_ref,
    )


def tile_sums(
    histories_ref, pick_ref, columns_ref, same_ref, sorted_ref, coded_ref, sums_ref, top_ref, level_ref, half_ref
):
    size, packed_rows, packed_width = histories_ref.shape
    half_count = sorted_ref.shape[0] // 3
    own_blocks = half_count * 2 // size
    height = pick_ref.shape[0] // SOURCES
    cell_count = coded_ref.shape[2]
    coded_rows = own_blocks * height

    histories = histories_ref[...].reshape(size * packed_rows, packed_width)
    tall = jnp.dot(pick_ref[...], histories, preferred_element_type=jnp.float32)
    tall = tall.astype(jnp.bfloat16)
    wide = []
    for which in range(SOURCES):
        rows = tall[which * height : (which + 1) * height]
        widened = jnp.dot(rows, columns_ref[which], preferred_element_type=jnp.float32)
        wide.append((widened * same_ref[...]).astype(jnp.bfloat16))

    def product(which, start):
        tiles = jnp.concatenate([sorted_ref[start + block] for block in range(own_blocks)], axis=1)
        return jnp.dot(wide[which], tiles, preferred_element_type=jnp.float32)

    def add_up(slot):
        owner = sums_device(slot, size)
        start = owner * own_blocks
        total = product(0, start)
        if isinstance(slot, int):
            if owner >= size // 2:
                total += product(1, half_count + start)
        else:
            upper = product(1, half_count + jnp.maximum(start, half_count))
            total += jnp.where(owner >= size // 2, upper, 0.0)
        sums_ref[slot] = total
        top = jnp.max(jnp.abs(total), axis=0, keepdims=True)
        tops = [top[:, block * cell_count : (block + 1) * cell_count] for block in range(own_blocks)]
        top_ref[pl.ds(slot, 1)] = functools.reduce(jnp.maximum, tops)

    def code(slot):
        half = half_ref[pl.ds(slot, 1)]
        for block in range(own_blocks):
            value = sums_ref[slot, :, pl.ds(block * cell_count, cell_count)]
            steps = jnp.round(value * half * (half * STEPS))
            coded_ref[slot, pl.ds(block * height, height)] = steps.astype(jnp.int32).astype(jnp.int16)
        spread = jnp.broadcast_to(level_ref[pl.ds(slot, 1)], (SCALE_ROWS, cell_count))
        coded_ref[slot, pl.ds(coded_rows, SCALE_ROWS)] = spread.astype(jnp.int16)

    each(size, add_up)
    level = jnp.ceil(jnp.log2(jnp.maximum(top_ref[...], SMALLEST)) * LEVELS)
    level_ref[...] = level.astype(jnp.int32)
    half_ref[...] = jnp.exp2(level * (-0.5 / LEVELS))
    each(size, code)


def add_parts(coded_ref, total_out, total_ref, semaphores):
    size = coded_ref.shape[0]
    own_blocks, height, cell_count = total_ref.shape
    stores = []
    for block in range(own_blocks):

        def add(slot, total):
            level = coded_ref[slot, pl.ds(own_blocks * height, SCALE_ROWS)].astype(jnp.int32)
            half = jnp.exp2(level.astype(jnp.float32)[:1] * (0.5 / LEVELS))
            steps = coded_ref[slot, pl.ds(block * height, height)].astype(jnp.int32)
            return total + steps.astype(jnp.float32) * (half * (1.0 / STEPS)) * half

        total = jnp.zeros((height, cell_count), jnp.float32)
        if size <= WRITTEN_OUT:
            for slot in range(size):
                total = add(slot, total)
        else:
            total = lax.fori_loop(0, size, add, total)
        total_ref[block] = total
        stores.append(pltpu.make_async_copy(total_ref.at[block], total_out.at[block], semaphores.at[block]))
        stores[-1].start()
    for store in stores:
        store.wait()


def shards(propagator, tile_blocks, histories):
    size = lax.axis_size("tm")
    own_blocks, tracer_count, source_width = histories.shape
    slot_count, source_width, months, cell_count = propagator.shape
    block_count = size * own_blocks
    height = tracer_count * months
    tile_height = source_width * months

    used_rows = tracer_count * own_blocks
    padded_shape = (used_rows + -used_rows % 16, source_width + -source_width % 128)
    packed_rows = tracer_count + -tracer_count % 16
    packed_width = own_blocks * source_width + -(own_blocks * source_width) % 128
    rows, blocks, tiles = (
        pltpu.with_memory_space_constraint(value, pltpu.HBM)
        for value in (
            jnp.swapaxes(histories, 0, 1).reshape(used_rows, source_width),
            tile_blocks.T,
            propagator.reshape(slot_count, tile_height, cell_count),
        )
    )
    vmem = pl.BlockSpec(memory_space=pltpu.VMEM)
    hbm = pl.BlockSpec(memory_space=pltpu.HBM)
    copies, sorted_tiles, pick, columns, same = pl.pallas_call(
        lambda *refs: prepare(months, *refs),
        out_shape=[
            jax.ShapeDtypeStruct((size, packed_rows, packed_width), rows.dtype),
            jax.ShapeDtypeStruct((block_count + block_count // 2, tile_height, cell_count), tiles.dtype),
            jax.ShapeDtypeStruct((SOURCES * height, size * packed_rows), jnp.bfloat16),
            jax.ShapeDtypeStruct((SOURCES, packed_width, tile_height), jnp.bfloat16),
            jax.ShapeDtypeStruct((height, tile_height), jnp.float32),
        ],
        in_specs=[hbm] * 3,
        out_specs=[vmem] * 5,
        scratch_shapes=[
            pltpu.VMEM(rows.shape, rows.dtype),
            pltpu.VMEM(padded_shape, rows.dtype),
            pltpu.SMEM(blocks.shape, blocks.dtype),
            pltpu.VMEM(tiles.shape, tiles.dtype),
            pltpu.SemaphoreType.DMA((3,)),
        ],
        compiler_params=pltpu.CompilerParams(vmem_limit_bytes=24 * 1024 * 1024),
        cost_estimate=pl.CostEstimate(flops=0, bytes_accessed=tiles.size * 4, transcendentals=0),
    )(rows, blocks, tiles)

    received = exchange(copies, history_order(size))

    coded = pl.pallas_call(
        tile_sums,
        out_shape=jax.ShapeDtypeStruct((size, own_blocks * height + SCALE_ROWS, cell_count), jnp.int16),
        in_specs=[vmem] * 5,
        out_specs=vmem,
        scratch_shapes=[
            pltpu.VMEM((size, height, own_blocks * cell_count), jnp.float32),
            pltpu.VMEM((size, cell_count), jnp.float32),
            pltpu.VMEM((size, cell_count), jnp.int32),
            pltpu.VMEM((size, cell_count), jnp.float32),
        ],
        compiler_params=pltpu.CompilerParams(vmem_limit_bytes=20 * 1024 * 1024),
        cost_estimate=pl.CostEstimate(
            flops=2 * slot_count * height * tile_height * cell_count,
            bytes_accessed=propagator.size * 4,
            transcendentals=0,
        ),
    )(received, pick, columns, same, sorted_tiles)

    owned = pl.pallas_call(
        add_parts,
        out_shape=jax.ShapeDtypeStruct((own_blocks, height, cell_count), jnp.float32),
        in_specs=[vmem],
        out_specs=hbm,
        scratch_shapes=[
            pltpu.VMEM((own_blocks, height, cell_count), jnp.float32),
            pltpu.SemaphoreType.DMA((own_blocks,)),
        ],
        compiler_params=pltpu.CompilerParams(vmem_limit_bytes=16 * 1024 * 1024),
    )(exchange(coded, [sums_device(slot, size) for slot in range(size)]))
    return owned.reshape(own_blocks, tracer_count, months, cell_count)


def solution(mesh):
    in_specs = (
        P(("groups", "tm"), None, None, "cells"),
        P(("groups", "tm"), None),
        P("tm", None, None),
    )
    out_specs = P(("groups", "tm"), None, None, "cells")
    return jax.shard_map(shards, mesh=mesh, in_specs=in_specs, out_specs=out_specs, check_vma=False)
```

```python
import jax
import jax.numpy as jnp
from jax import lax
from jax.experimental import pallas as pl
from jax.experimental.pallas import tpu as pltpu
from jax.sharding import PartitionSpec as P

STEPS = 32700.0
LEVELS = 128
SMALLEST = 2.0**-126
SCALE_ROWS = 8
WRITTEN_OUT = 17
SOURCES = 2


def centre(size):
    return size * 5 // 8


def history_order(size):
    inner = [device for device in range(1, size) if device != centre(size)]
    return [centre(size)] + inner[: size // 2 - 1] + [0] + inner[size // 2 - 1 :]


def history_slot(device, size):
    after = device - (device > centre(size)).astype(jnp.int32)
    after = after + (after >= size // 2).astype(jnp.int32)
    return jnp.where(device == centre(size), 0, jnp.where(device == 0, size // 2, after))


def sums_device(slot, size):
    if isinstance(slot, int):
        return centre(size) if slot == 0 else size - slot - (size - slot <= centre(size))
    after = size - slot - (size - slot <= centre(size)).astype(jnp.int32)
    return jnp.where(slot == 0, centre(size), after)


def exchange(value, order):
    return lax.all_to_all(value, "tm", 0, 0, axis_index_groups=[order], tiled=True)


def split(value, divisor):
    if divisor & (divisor - 1):
        return lax.div(value, jnp.full_like(value, divisor)), lax.rem(value, jnp.full_like(value, divisor))
    return value >> (divisor.bit_length() - 1), value & (divisor - 1)


def each(count, body):
    if count <= WRITTEN_OUT:
        for index in range(count):
            body(index)
    else:
        lax.fori_loop(0, count, lambda index, carry: (body(index), carry)[1], 0)


def arrange(
    size, months, source_width, load_blocks, load_tiles, blocks_ref, tiles_ref, sorted_ref, pick_ref, columns_ref
):
    slot_count = tiles_ref.shape[0]
    half_count = sorted_ref.shape[0] // 3
    block_count = half_count * 2
    own_blocks = block_count // size
    height = pick_ref.shape[0] // SOURCES
    packed_rows = pick_ref.shape[1] // size
    tracer = split(lax.broadcasted_iota(jnp.int32, (height, pick_ref.shape[1]), 0), months)[0]
    offset = lax.broadcasted_iota(jnp.int32, (height, pick_ref.shape[1]), 1) - tracer
    column_of = split(lax.broadcasted_iota(jnp.int32, columns_ref.shape[1:], 1), months)[0]
    shift = lax.broadcasted_iota(jnp.int32, columns_ref.shape[1:], 0) - column_of
    load_blocks.wait()
    lower = jnp.minimum(blocks_ref[0, 0], block_count - 1 - blocks_ref[0, 0])

    def place_of(slot):
        return blocks_ref[1, slot] + jnp.where(blocks_ref[0, slot] == lower, 0, half_count)

    places = [place_of(slot) for slot in range(slot_count)] if slot_count <= WRITTEN_OUT else None
    for which, source in enumerate((lower, block_count - 1 - lower)):
        owner, block = split(source, own_blocks)
        picked = offset == history_slot(owner, size) * packed_rows
        pick_ref[pl.ds(which * height, height)] = picked.astype(pick_ref.dtype)
        columns_ref[which] = (shift == block * source_width).astype(columns_ref.dtype)
    load_tiles.wait()

    def place(slot):
        sorted_ref[places[slot] if places else place_of(slot)] = tiles_ref[slot]

    each(slot_count, place)


def prepare(
    months,
    rows_in,
    blocks_in,
    tiles_in,
    copies_ref,
    sorted_ref,
    pick_ref,
    columns_ref,
    same_ref,
    rows_ref,
    padded_ref,
    blocks_ref,
    tiles_ref,
    semaphores,
):
    size, packed_rows, packed_width = copies_ref.shape
    used_rows, source_width = rows_ref.shape
    own_blocks = sorted_ref.shape[0] // 3 * 2 // size
    load_rows = pltpu.make_async_copy(rows_in, rows_ref, semaphores.at[0])
    load_blocks = pltpu.make_async_copy(blocks_in, blocks_ref, semaphores.at[1])
    load_tiles = pltpu.make_async_copy(tiles_in, tiles_ref, semaphores.at[2])
    for load in (load_rows, load_blocks, load_tiles):
        load.start()
    month_of_row = split(lax.broadcasted_iota(jnp.int32, same_ref.shape, 0), months)[1]
    month_of_column = split(lax.broadcasted_iota(jnp.int32, same_ref.shape, 1), months)[1]
    same_ref[...] = (month_of_row == month_of_column).astype(same_ref.dtype)
    padded_ref[...] = jnp.zeros(padded_ref.shape, padded_ref.dtype)
    group = sorted_ref.shape[0] // size

    def clear(index):
        sorted_ref[pl.ds(index * group, group)] = jnp.zeros((group,) + sorted_ref.shape[1:], sorted_ref.dtype)

    each(size, clear)
    taker = (packed_rows, padded_ref.shape[0])
    placer = (padded_ref.shape[1], packed_width)
    take = lax.broadcasted_iota(jnp.int32, taker, 1) - lax.broadcasted_iota(jnp.int32, taker, 0) * own_blocks
    put = lax.broadcasted_iota(jnp.int32, placer, 1) - lax.broadcasted_iota(jnp.int32, placer, 0)
    load_rows.wait()
    padded_ref[:used_rows, :source_width] = rows_ref[...]
    packed = jnp.zeros((packed_rows, packed_width), jnp.float32)
    for block in range(own_blocks):
        taken = jnp.dot((take == block).astype(padded_ref.dtype), padded_ref[...], preferred_element_type=jnp.float32)
        packed += jnp.dot(
            taken.astype(padded_ref.dtype),
            (put == block * source_width).astype(padded_ref.dtype),
            preferred_element_type=jnp.float32,
        )
    packed = packed.astype(copies_ref.dtype)

    def copy(owner):
        copies_ref[owner] = packed

    each(size, copy)
    arrange(
        size,
        months,
        source_width,
        load_blocks,
        load_tiles,
        blocks_ref,
        tiles_ref,
        sorted_ref,
        pick_ref,
        columns_ref,
    )


def tile_sums(histories_ref, pick_ref, columns_ref, same_ref, sorted_ref, coded_ref):
    size, packed_rows, packed_width = histories_ref.shape
    half_count = sorted_ref.shape[0] // 3
    own_blocks = half_count * 2 // size
    height = pick_ref.shape[0] // SOURCES
    cell_count = coded_ref.shape[2]
    coded_rows = own_blocks * height

    histories = histories_ref[...].reshape(size * packed_rows, packed_width)
    tall = jnp.dot(pick_ref[...], histories, preferred_element_type=jnp.float32)
    tall = tall.astype(jnp.bfloat16)
    wide = []
    for which in range(SOURCES):
        rows = tall[which * height : (which + 1) * height]
        widened = jnp.dot(rows, columns_ref[which], preferred_element_type=jnp.float32)
        wide.append((widened * same_ref[...]).astype(jnp.bfloat16))

    def product(which, start):
        tiles = jnp.concatenate([sorted_ref[start + block] for block in range(own_blocks)], axis=1)
        return jnp.dot(wide[which], tiles, preferred_element_type=jnp.float32)

    def code(slot):
        owner = sums_device(slot, size)
        start = owner * own_blocks
        total = product(0, start)
        if isinstance(slot, int):
            if owner >= size // 2:
                total += product(1, half_count + start)
        else:
            upper = product(1, half_count + jnp.maximum(start, half_count))
            total += jnp.where(owner >= size // 2, upper, 0.0)
        values = [total[:, block * cell_count : (block + 1) * cell_count] for block in range(own_blocks)]
        top = jnp.abs(values[0])
        for value in values[1:]:
            top = jnp.maximum(top, jnp.abs(value))
        top = jnp.max(top, axis=0, keepdims=True)
        level = jnp.ceil(jnp.log2(jnp.maximum(top, SMALLEST)) * LEVELS)
        half = jnp.exp2(level * (-0.5 / LEVELS))
        for block, value in enumerate(values):
            steps = jnp.round(value * half * (half * STEPS))
            coded_ref[slot, pl.ds(block * height, height)] = steps.astype(jnp.int32).astype(jnp.int16)
        spread = jnp.broadcast_to(level.astype(jnp.int32), (SCALE_ROWS, cell_count))
        coded_ref[slot, pl.ds(coded_rows, SCALE_ROWS)] = spread.astype(jnp.int16)

    each(size, code)


def add_parts(coded_ref, total_out, total_ref, semaphores):
    size = coded_ref.shape[0]
    own_blocks, height, cell_count = total_ref.shape
    stores = []
    for block in range(own_blocks):

        def add(slot, total):
            level = coded_ref[slot, pl.ds(own_blocks * height, SCALE_ROWS)].astype(jnp.int32)
            half = jnp.exp2(level.astype(jnp.float32)[:1] * (0.5 / LEVELS))
            steps = coded_ref[slot, pl.ds(block * height, height)].astype(jnp.int32)
            return total + steps.astype(jnp.float32) * (half * (1.0 / STEPS)) * half

        total = jnp.zeros((height, cell_count), jnp.float32)
        if size <= WRITTEN_OUT:
            for slot in range(size):
                total = add(slot, total)
        else:
            total = lax.fori_loop(0, size, add, total)
        total_ref[block] = total
        stores.append(pltpu.make_async_copy(total_ref.at[block], total_out.at[block], semaphores.at[block]))
        stores[-1].start()
    for store in stores:
        store.wait()


def shards(propagator, tile_blocks, histories):
    size = lax.axis_size("tm")
    own_blocks, tracer_count, source_width = histories.shape
    slot_count, source_width, months, cell_count = propagator.shape
    block_count = size * own_blocks
    height = tracer_count * months
    tile_height = source_width * months

    used_rows = tracer_count * own_blocks
    padded_shape = (used_rows + -used_rows % 16, source_width + -source_width % 128)
    packed_rows = tracer_count + -tracer_count % 16
    packed_width = own_blocks * source_width + -(own_blocks * source_width) % 128
    rows, blocks, tiles = (
        pltpu.with_memory_space_constraint(value, pltpu.HBM)
        for value in (
            jnp.swapaxes(histories, 0, 1).reshape(used_rows, source_width),
            tile_blocks.T,
            propagator.reshape(slot_count, tile_height, cell_count),
        )
    )
    vmem = pl.BlockSpec(memory_space=pltpu.VMEM)
    hbm = pl.BlockSpec(memory_space=pltpu.HBM)
    copies, sorted_tiles, pick, columns, same = pl.pallas_call(
        lambda *refs: prepare(months, *refs),
        out_shape=[
            jax.ShapeDtypeStruct((size, packed_rows, packed_width), rows.dtype),
            jax.ShapeDtypeStruct((block_count + block_count // 2, tile_height, cell_count), tiles.dtype),
            jax.ShapeDtypeStruct((SOURCES * height, size * packed_rows), jnp.bfloat16),
            jax.ShapeDtypeStruct((SOURCES, packed_width, tile_height), jnp.bfloat16),
            jax.ShapeDtypeStruct((height, tile_height), jnp.float32),
        ],
        in_specs=[hbm] * 3,
        out_specs=[vmem] * 5,
        scratch_shapes=[
            pltpu.VMEM(rows.shape, rows.dtype),
            pltpu.VMEM(padded_shape, rows.dtype),
            pltpu.SMEM(blocks.shape, blocks.dtype),
            pltpu.VMEM(tiles.shape, tiles.dtype),
            pltpu.SemaphoreType.DMA((3,)),
        ],
        compiler_params=pltpu.CompilerParams(vmem_limit_bytes=24 * 1024 * 1024),
        cost_estimate=pl.CostEstimate(flops=0, bytes_accessed=tiles.size * 4, transcendentals=0),
    )(rows, blocks, tiles)

    received = exchange(copies, history_order(size))

    coded = pl.pallas_call(
        tile_sums,
        out_shape=jax.ShapeDtypeStruct((size, own_blocks * height + SCALE_ROWS, cell_count), jnp.int16),
        in_specs=[vmem] * 5,
        out_specs=vmem,
        compiler_params=pltpu.CompilerParams(vmem_limit_bytes=20 * 1024 * 1024),
        cost_estimate=pl.CostEstimate(
            flops=2 * slot_count * height * tile_height * cell_count,
            bytes_accessed=propagator.size * 4,
            transcendentals=0,
        ),
    )(received, pick, columns, same, sorted_tiles)

    owned = pl.pallas_call(
        add_parts,
        out_shape=jax.ShapeDtypeStruct((own_blocks, height, cell_count), jnp.float32),
        in_specs=[vmem],
        out_specs=hbm,
        scratch_shapes=[
            pltpu.VMEM((own_blocks, height, cell_count), jnp.float32),
            pltpu.SemaphoreType.DMA((own_blocks,)),
        ],
        compiler_params=pltpu.CompilerParams(vmem_limit_bytes=16 * 1024 * 1024),
    )(exchange(coded, [sums_device(slot, size) for slot in range(size)]))
    return owned.reshape(own_blocks, tracer_count, months, cell_count)


def solution(mesh):
    in_specs = (
        P(("groups", "tm"), None, None, "cells"),
        P(("groups", "tm"), None),
        P("tm", None, None),
    )
    out_specs = P(("groups", "tm"), None, None, "cells")
    return jax.shard_map(shards, mesh=mesh, in_specs=in_specs, out_specs=out_specs, check_vma=False)
```

```python
import jax
import jax.numpy as jnp
from jax import lax
from jax.experimental import pallas as pl
from jax.experimental.pallas import tpu as pltpu
from jax.sharding import PartitionSpec as P

STEPS = 32700.0
LEVELS = 128
SMALLEST = 2.0**-126
SCALE_ROWS = 8
WRITTEN_OUT = 17
SOURCES = 2


def centre(size):
    return size * 5 // 8


def history_order(size):
    inner = [device for device in range(1, size) if device != centre(size)]
    order = [centre(size)] + inner[: size // 2 - 1] + [0] + inner[size // 2 - 1 :]
    changed = {0: size * 3 // 4, size * 3 // 4: 0}
    return [changed.get(device, device) for device in order]


def history_slot(device, size):
    far = size * 3 // 4
    device = jnp.where(device == 0, far, jnp.where(device == far, 0, device))
    after = device - (device > centre(size)).astype(jnp.int32)
    after = after + (after >= size // 2).astype(jnp.int32)
    return jnp.where(device == centre(size), 0, jnp.where(device == 0, size // 2, after))


def sums_device(slot, size):
    if isinstance(slot, int):
        return centre(size) if slot == 0 else size - slot - (size - slot <= centre(size))
    after = size - slot - (size - slot <= centre(size)).astype(jnp.int32)
    return jnp.where(slot == 0, centre(size), after)


def exchange(value, order):
    return lax.all_to_all(value, "tm", 0, 0, axis_index_groups=[order], tiled=True)


def split(value, divisor):
    if divisor & (divisor - 1):
        return lax.div(value, jnp.full_like(value, divisor)), lax.rem(value, jnp.full_like(value, divisor))
    return value >> (divisor.bit_length() - 1), value & (divisor - 1)


def each(count, body):
    if count <= WRITTEN_OUT:
        for index in range(count):
            body(index)
    else:
        lax.fori_loop(0, count, lambda index, carry: (body(index), carry)[1], 0)


def arrange(
    size, months, source_width, load_blocks, load_tiles, blocks_ref, tiles_ref, sorted_ref, pick_ref, columns_ref
):
    slot_count = tiles_ref.shape[0]
    half_count = sorted_ref.shape[0] // 3
    block_count = half_count * 2
    own_blocks = block_count // size
    height = pick_ref.shape[0] // SOURCES
    packed_rows = pick_ref.shape[1] // size
    tracer = split(lax.broadcasted_iota(jnp.int32, (height, pick_ref.shape[1]), 0), months)[0]
    offset = lax.broadcasted_iota(jnp.int32, (height, pick_ref.shape[1]), 1) - tracer
    column_of = split(lax.broadcasted_iota(jnp.int32, columns_ref.shape[1:], 1), months)[0]
    shift = lax.broadcasted_iota(jnp.int32, columns_ref.shape[1:], 0) - column_of
    load_blocks.wait()
    lower = jnp.minimum(blocks_ref[0, 0], block_count - 1 - blocks_ref[0, 0])

    def place_of(slot):
        return blocks_ref[1, slot] + jnp.where(blocks_ref[0, slot] == lower, 0, half_count)

    places = [place_of(slot) for slot in range(slot_count)] if slot_count <= WRITTEN_OUT else None
    for which, source in enumerate((lower, block_count - 1 - lower)):
        owner, block = split(source, own_blocks)
        picked = offset == history_slot(owner, size) * packed_rows
        pick_ref[pl.ds(which * height, height)] = picked.astype(pick_ref.dtype)
        columns_ref[which] = (shift == block * source_width).astype(columns_ref.dtype)
    load_tiles.wait()

    def place(slot):
        sorted_ref[places[slot] if places else place_of(slot)] = tiles_ref[slot]

    each(slot_count, place)


def prepare(
    months,
    rows_in,
    blocks_in,
    tiles_in,
    copies_ref,
    sorted_ref,
    pick_ref,
    columns_ref,
    same_ref,
    rows_ref,
    padded_ref,
    blocks_ref,
    tiles_ref,
    semaphores,
):
    size, packed_rows, packed_width = copies_ref.shape
    used_rows, source_width = rows_ref.shape
    own_blocks = sorted_ref.shape[0] // 3 * 2 // size
    load_rows = pltpu.make_async_copy(rows_in, rows_ref, semaphores.at[0])
    load_blocks = pltpu.make_async_copy(blocks_in, blocks_ref, semaphores.at[1])
    load_tiles = pltpu.make_async_copy(tiles_in, tiles_ref, semaphores.at[2])
    for load in (load_rows, load_blocks, load_tiles):
        load.start()
    month_of_row = split(lax.broadcasted_iota(jnp.int32, same_ref.shape, 0), months)[1]
    month_of_column = split(lax.broadcasted_iota(jnp.int32, same_ref.shape, 1), months)[1]
    same_ref[...] = (month_of_row == month_of_column).astype(same_ref.dtype)
    padded_ref[...] = jnp.zeros(padded_ref.shape, padded_ref.dtype)
    group = sorted_ref.shape[0] // size

    def clear(index):
        sorted_ref[pl.ds(index * group, group)] = jnp.zeros((group,) + sorted_ref.shape[1:], sorted_ref.dtype)

    each(size, clear)
    taker = (packed_rows, padded_ref.shape[0])
    placer = (padded_ref.shape[1], packed_width)
    take = lax.broadcasted_iota(jnp.int32, taker, 1) - lax.broadcasted_iota(jnp.int32, taker, 0) * own_blocks
    put = lax.broadcasted_iota(jnp.int32, placer, 1) - lax.broadcasted_iota(jnp.int32, placer, 0)
    load_rows.wait()
    padded_ref[:used_rows, :source_width] = rows_ref[...]
    packed = jnp.zeros((packed_rows, packed_width), jnp.float32)
    for block in range(own_blocks):
        taken = jnp.dot((take == block).astype(padded_ref.dtype), padded_ref[...], preferred_element_type=jnp.float32)
        packed += jnp.dot(
            taken.astype(padded_ref.dtype),
            (put == block * source_width).astype(padded_ref.dtype),
            preferred_element_type=jnp.float32,
        )
    packed = packed.astype(copies_ref.dtype)

    def copy(owner):
        copies_ref[owner] = packed

    each(size, copy)
    arrange(
        size,
        months,
        source_width,
        load_blocks,
        load_tiles,
        blocks_ref,
        tiles_ref,
        sorted_ref,
        pick_ref,
        columns_ref,
    )


def tile_sums(histories_ref, pick_ref, columns_ref, same_ref, sorted_ref, coded_ref):
    size, packed_rows, packed_width = histories_ref.shape
    half_count = sorted_ref.shape[0] // 3
    own_blocks = half_count * 2 // size
    height = pick_ref.shape[0] // SOURCES
    cell_count = coded_ref.shape[2]
    coded_rows = own_blocks * height

    histories = histories_ref[...].reshape(size * packed_rows, packed_width)
    tall = jnp.dot(pick_ref[...], histories, preferred_element_type=jnp.float32)
    tall = tall.astype(jnp.bfloat16)
    wide = []
    for which in range(SOURCES):
        rows = tall[which * height : (which + 1) * height]
        widened = jnp.dot(rows, columns_ref[which], preferred_element_type=jnp.float32)
        wide.append((widened * same_ref[...]).astype(jnp.bfloat16))

    def product(which, start):
        tiles = jnp.concatenate([sorted_ref[start + block] for block in range(own_blocks)], axis=1)
        return jnp.dot(wide[which], tiles, preferred_element_type=jnp.float32)

    def code(slot):
        owner = sums_device(slot, size)
        start = owner * own_blocks
        total = product(0, start)
        if isinstance(slot, int):
            if owner >= size // 2:
                total += product(1, half_count + start)
        else:
            upper = product(1, half_count + jnp.maximum(start, half_count))
            total += jnp.where(owner >= size // 2, upper, 0.0)
        values = [total[:, block * cell_count : (block + 1) * cell_count] for block in range(own_blocks)]
        top = jnp.abs(values[0])
        for value in values[1:]:
            top = jnp.maximum(top, jnp.abs(value))
        top = jnp.max(top, axis=0, keepdims=True)
        level = jnp.ceil(jnp.log2(jnp.maximum(top, SMALLEST)) * LEVELS)
        half = jnp.exp2(level * (-0.5 / LEVELS))
        for block, value in enumerate(values):
            steps = jnp.round(value * half * (half * STEPS))
            coded_ref[slot, pl.ds(block * height, height)] = steps.astype(jnp.int32).astype(jnp.int16)
        spread = jnp.broadcast_to(level.astype(jnp.int32), (SCALE_ROWS, cell_count))
        coded_ref[slot, pl.ds(coded_rows, SCALE_ROWS)] = spread.astype(jnp.int16)

    each(size, code)


def add_parts(coded_ref, total_out, total_ref, semaphores):
    size = coded_ref.shape[0]
    own_blocks, height, cell_count = total_ref.shape
    stores = []
    for block in range(own_blocks):

        def add(slot, total):
            level = coded_ref[slot, pl.ds(own_blocks * height, SCALE_ROWS)].astype(jnp.int32)
            half = jnp.exp2(level.astype(jnp.float32)[:1] * (0.5 / LEVELS))
            steps = coded_ref[slot, pl.ds(block * height, height)].astype(jnp.int32)
            return total + steps.astype(jnp.float32) * (half * (1.0 / STEPS)) * half

        total = jnp.zeros((height, cell_count), jnp.float32)
        if size <= WRITTEN_OUT:
            for slot in range(size):
                total = add(slot, total)
        else:
            total = lax.fori_loop(0, size, add, total)
        total_ref[block] = total
        stores.append(pltpu.make_async_copy(total_ref.at[block], total_out.at[block], semaphores.at[block]))
        stores[-1].start()
    for store in stores:
        store.wait()


def shards(propagator, tile_blocks, histories):
    size = lax.axis_size("tm")
    own_blocks, tracer_count, source_width = histories.shape
    slot_count, source_width, months, cell_count = propagator.shape
    block_count = size * own_blocks
    height = tracer_count * months
    tile_height = source_width * months

    used_rows = tracer_count * own_blocks
    padded_shape = (used_rows + -used_rows % 16, source_width + -source_width % 128)
    packed_rows = tracer_count + -tracer_count % 16
    packed_width = own_blocks * source_width + -(own_blocks * source_width) % 128
    rows, blocks, tiles = (
        pltpu.with_memory_space_constraint(value, pltpu.HBM)
        for value in (
            jnp.swapaxes(histories, 0, 1).reshape(used_rows, source_width),
            tile_blocks.T,
            propagator.reshape(slot_count, tile_height, cell_count),
        )
    )
    vmem = pl.BlockSpec(memory_space=pltpu.VMEM)
    hbm = pl.BlockSpec(memory_space=pltpu.HBM)
    copies, sorted_tiles, pick, columns, same = pl.pallas_call(
        lambda *refs: prepare(months, *refs),
        out_shape=[
            jax.ShapeDtypeStruct((size, packed_rows, packed_width), rows.dtype),
            jax.ShapeDtypeStruct((block_count + block_count // 2, tile_height, cell_count), tiles.dtype),
            jax.ShapeDtypeStruct((SOURCES * height, size * packed_rows), jnp.bfloat16),
            jax.ShapeDtypeStruct((SOURCES, packed_width, tile_height), jnp.bfloat16),
            jax.ShapeDtypeStruct((height, tile_height), jnp.float32),
        ],
        in_specs=[hbm] * 3,
        out_specs=[vmem] * 5,
        scratch_shapes=[
            pltpu.VMEM(rows.shape, rows.dtype),
            pltpu.VMEM(padded_shape, rows.dtype),
            pltpu.SMEM(blocks.shape, blocks.dtype),
            pltpu.VMEM(tiles.shape, tiles.dtype),
            pltpu.SemaphoreType.DMA((3,)),
        ],
        compiler_params=pltpu.CompilerParams(vmem_limit_bytes=24 * 1024 * 1024),
        cost_estimate=pl.CostEstimate(flops=0, bytes_accessed=tiles.size * 4, transcendentals=0),
    )(rows, blocks, tiles)

    received = exchange(copies, history_order(size))

    coded = pl.pallas_call(
        tile_sums,
        out_shape=jax.ShapeDtypeStruct((size, own_blocks * height + SCALE_ROWS, cell_count), jnp.int16),
        in_specs=[vmem] * 5,
        out_specs=vmem,
        compiler_params=pltpu.CompilerParams(vmem_limit_bytes=20 * 1024 * 1024),
        cost_estimate=pl.CostEstimate(
            flops=2 * slot_count * height * tile_height * cell_count,
            bytes_accessed=propagator.size * 4,
            transcendentals=0,
        ),
    )(received, pick, columns, same, sorted_tiles)

    owned = pl.pallas_call(
        add_parts,
        out_shape=jax.ShapeDtypeStruct((own_blocks, height, cell_count), jnp.float32),
        in_specs=[vmem],
        out_specs=hbm,
        scratch_shapes=[
            pltpu.VMEM((own_blocks, height, cell_count), jnp.float32),
            pltpu.SemaphoreType.DMA((own_blocks,)),
        ],
        compiler_params=pltpu.CompilerParams(vmem_limit_bytes=16 * 1024 * 1024),
    )(exchange(coded, [sums_device(slot, size) for slot in range(size)]))
    return owned.reshape(own_blocks, tracer_count, months, cell_count)


def solution(mesh):
    in_specs = (
        P(("groups", "tm"), None, None, "cells"),
        P(("groups", "tm"), None),
        P("tm", None, None),
    )
    out_specs = P(("groups", "tm"), None, None, "cells")
    return jax.shard_map(shards, mesh=mesh, in_specs=in_specs, out_specs=out_specs, check_vma=False)
```

```python
import jax
import jax.numpy as jnp
from jax import lax
from jax.experimental import pallas as pl
from jax.experimental.pallas import tpu as pltpu
from jax.sharding import PartitionSpec as P

STEPS = 32700.0
LEVELS = 128
SMALLEST = 2.0**-126
SCALE_ROWS = 8
WRITTEN_OUT = 17
SOURCES = 2


def centre(size):
    return size * 5 // 8


def history_order(size):
    inner = [device for device in range(1, size) if device != centre(size)]
    return [centre(size)] + inner[: size // 2 - 1] + [0] + inner[size // 2 - 1 :]


def history_slot(device, size):
    after = device - (device > centre(size)).astype(jnp.int32)
    after = after + (after >= size // 2).astype(jnp.int32)
    return jnp.where(device == centre(size), 0, jnp.where(device == 0, size // 2, after))


def sums_device(slot, size):
    if isinstance(slot, int):
        return centre(size) if slot == 0 else size - slot - (size - slot <= centre(size))
    after = size - slot - (size - slot <= centre(size)).astype(jnp.int32)
    return jnp.where(slot == 0, centre(size), after)


def exchange(value, order):
    return lax.all_to_all(value, "tm", 0, 0, axis_index_groups=[order], tiled=True)


def split(value, divisor):
    if divisor & (divisor - 1):
        return lax.div(value, jnp.full_like(value, divisor)), lax.rem(value, jnp.full_like(value, divisor))
    return value >> (divisor.bit_length() - 1), value & (divisor - 1)


def each(count, body):
    if count <= WRITTEN_OUT:
        for index in range(count):
            body(index)
    else:
        lax.fori_loop(0, count, lambda index, carry: (body(index), carry)[1], 0)


def arrange(
    size, months, source_width, load_blocks, load_tiles, blocks_ref, tiles_ref, sorted_ref, pick_ref, columns_ref
):
    slot_count = tiles_ref.shape[0]
    half_count = sorted_ref.shape[0] // 3
    block_count = half_count * 2
    own_blocks = block_count // size
    height = pick_ref.shape[0] // SOURCES
    packed_rows = pick_ref.shape[1] // size
    tracer = split(lax.broadcasted_iota(jnp.int32, (height, pick_ref.shape[1]), 0), months)[0]
    offset = lax.broadcasted_iota(jnp.int32, (height, pick_ref.shape[1]), 1) - tracer
    column_of = split(lax.broadcasted_iota(jnp.int32, columns_ref.shape[1:], 1), months)[0]
    shift = lax.broadcasted_iota(jnp.int32, columns_ref.shape[1:], 0) - column_of
    load_blocks.wait()
    lower = jnp.minimum(blocks_ref[0, 0], block_count - 1 - blocks_ref[0, 0])

    def place_of(slot):
        return blocks_ref[1, slot] + jnp.where(blocks_ref[0, slot] == lower, 0, half_count)

    places = [place_of(slot) for slot in range(slot_count)] if slot_count <= WRITTEN_OUT else None
    for which, source in enumerate((lower, block_count - 1 - lower)):
        owner, block = split(source, own_blocks)
        picked = offset == history_slot(owner, size) * packed_rows
        pick_ref[pl.ds(which * height, height)] = picked.astype(pick_ref.dtype)
        columns_ref[which] = (shift == block * source_width).astype(columns_ref.dtype)
    load_tiles.wait()

    def place(slot):
        sorted_ref[places[slot] if places else place_of(slot)] = tiles_ref[slot]

    each(slot_count, place)


def prepare(
    months,
    rows_in,
    blocks_in,
    tiles_in,
    copies_ref,
    sorted_ref,
    pick_ref,
    columns_ref,
    same_ref,
    rows_ref,
    padded_ref,
    blocks_ref,
    tiles_ref,
    semaphores,
):
    size, packed_rows, packed_width = copies_ref.shape
    used_rows, source_width = rows_ref.shape
    own_blocks = sorted_ref.shape[0] // 3 * 2 // size
    load_rows = pltpu.make_async_copy(rows_in, rows_ref, semaphores.at[0])
    load_blocks = pltpu.make_async_copy(blocks_in, blocks_ref, semaphores.at[1])
    load_tiles = pltpu.make_async_copy(tiles_in, tiles_ref, semaphores.at[2])
    for load in (load_tiles, load_rows, load_blocks):
        load.start()
    month_of_row = split(lax.broadcasted_iota(jnp.int32, same_ref.shape, 0), months)[1]
    month_of_column = split(lax.broadcasted_iota(jnp.int32, same_ref.shape, 1), months)[1]
    same_ref[...] = (month_of_row == month_of_column).astype(same_ref.dtype)
    padded_ref[...] = jnp.zeros(padded_ref.shape, padded_ref.dtype)
    group = sorted_ref.shape[0] // size

    def clear(index):
        sorted_ref[pl.ds(index * group, group)] = jnp.zeros((group,) + sorted_ref.shape[1:], sorted_ref.dtype)

    each(size, clear)
    taker = (packed_rows, padded_ref.shape[0])
    placer = (padded_ref.shape[1], packed_width)
    take = lax.broadcasted_iota(jnp.int32, taker, 1) - lax.broadcasted_iota(jnp.int32, taker, 0) * own_blocks
    put = lax.broadcasted_iota(jnp.int32, placer, 1) - lax.broadcasted_iota(jnp.int32, placer, 0)
    load_rows.wait()
    padded_ref[:used_rows, :source_width] = rows_ref[...]
    packed = jnp.zeros((packed_rows, packed_width), jnp.float32)
    for block in range(own_blocks):
        taken = jnp.dot((take == block).astype(padded_ref.dtype), padded_ref[...], preferred_element_type=jnp.float32)
        packed += jnp.dot(
            taken.astype(padded_ref.dtype),
            (put == block * source_width).astype(padded_ref.dtype),
            preferred_element_type=jnp.float32,
        )
    packed = packed.astype(copies_ref.dtype)

    def copy(owner):
        copies_ref[owner] = packed

    each(size, copy)
    arrange(
        size,
        months,
        source_width,
        load_blocks,
        load_tiles,
        blocks_ref,
        tiles_ref,
        sorted_ref,
        pick_ref,
        columns_ref,
    )


def tile_sums(histories_ref, pick_ref, columns_ref, same_ref, sorted_ref, coded_ref):
    size, packed_rows, packed_width = histories_ref.shape
    half_count = sorted_ref.shape[0] // 3
    own_blocks = half_count * 2 // size
    height = pick_ref.shape[0] // SOURCES
    cell_count = coded_ref.shape[2]
    coded_rows = own_blocks * height

    histories = histories_ref[...].reshape(size * packed_rows, packed_width)
    tall = jnp.dot(pick_ref[...], histories, preferred_element_type=jnp.float32)
    tall = tall.astype(jnp.bfloat16)
    wide = []
    for which in range(SOURCES):
        rows = tall[which * height : (which + 1) * height]
        widened = jnp.dot(rows, columns_ref[which], preferred_element_type=jnp.float32)
        wide.append((widened * same_ref[...]).astype(jnp.bfloat16))

    both = jnp.concatenate(wide, axis=1)

    def side_by_side(start):
        return jnp.concatenate([sorted_ref[start + block] for block in range(own_blocks)], axis=1)

    def code(slot):
        owner = sums_device(slot, size)
        start = owner * own_blocks
        tiles = side_by_side(start)
        if isinstance(slot, int) and owner < size // 2:
            total = jnp.dot(wide[0], tiles, preferred_element_type=jnp.float32)
        else:
            upper = side_by_side(half_count + (start if isinstance(slot, int) else jnp.maximum(start, half_count)))
            if not isinstance(slot, int):
                upper = jnp.where(owner >= size // 2, upper, jnp.zeros_like(upper))
            stacked = jnp.concatenate([tiles, upper], axis=0)
            total = jnp.dot(both, stacked, preferred_element_type=jnp.float32)
        values = [total[:, block * cell_count : (block + 1) * cell_count] for block in range(own_blocks)]
        top = jnp.abs(values[0])
        for value in values[1:]:
            top = jnp.maximum(top, jnp.abs(value))
        top = jnp.max(top, axis=0, keepdims=True)
        level = jnp.ceil(jnp.log2(jnp.maximum(top, SMALLEST)) * LEVELS)
        half = jnp.exp2(level * (-0.5 / LEVELS))
        for block, value in enumerate(values):
            steps = jnp.round(value * half * (half * STEPS))
            coded_ref[slot, pl.ds(block * height, height)] = steps.astype(jnp.int32).astype(jnp.int16)
        spread = jnp.broadcast_to(level.astype(jnp.int32), (SCALE_ROWS, cell_count))
        coded_ref[slot, pl.ds(coded_rows, SCALE_ROWS)] = spread.astype(jnp.int16)

    each(size, code)


def add_parts(coded_ref, total_out, total_ref, semaphores):
    size = coded_ref.shape[0]
    own_blocks, height, cell_count = total_ref.shape
    stores = []
    for block in range(own_blocks):

        def add(slot, total):
            level = coded_ref[slot, pl.ds(own_blocks * height, SCALE_ROWS)].astype(jnp.int32)
            half = jnp.exp2(level.astype(jnp.float32)[:1] * (0.5 / LEVELS))
            steps = coded_ref[slot, pl.ds(block * height, height)].astype(jnp.int32)
            return total + steps.astype(jnp.float32) * (half * (1.0 / STEPS)) * half

        total = jnp.zeros((height, cell_count), jnp.float32)
        if size <= WRITTEN_OUT:
            for slot in range(size):
                total = add(slot, total)
        else:
            total = lax.fori_loop(0, size, add, total)
        total_ref[block] = total
        stores.append(pltpu.make_async_copy(total_ref.at[block], total_out.at[block], semaphores.at[block]))
        stores[-1].start()
    for store in stores:
        store.wait()


def shards(propagator, tile_blocks, histories):
    size = lax.axis_size("tm")
    own_blocks, tracer_count, source_width = histories.shape
    slot_count, source_width, months, cell_count = propagator.shape
    block_count = size * own_blocks
    height = tracer_count * months
    tile_height = source_width * months

    used_rows = tracer_count * own_blocks
    padded_shape = (used_rows + -used_rows % 16, source_width + -source_width % 128)
    packed_rows = tracer_count + -tracer_count % 16
    packed_width = own_blocks * source_width + -(own_blocks * source_width) % 128
    rows, blocks, tiles = (
        pltpu.with_memory_space_constraint(value, pltpu.HBM)
        for value in (
            jnp.swapaxes(histories, 0, 1).reshape(used_rows, source_width),
            tile_blocks.T,
            propagator.reshape(slot_count, tile_height, cell_count),
        )
    )
    vmem = pl.BlockSpec(memory_space=pltpu.VMEM)
    hbm = pl.BlockSpec(memory_space=pltpu.HBM)
    copies, sorted_tiles, pick, columns, same = pl.pallas_call(
        lambda *refs: prepare(months, *refs),
        out_shape=[
            jax.ShapeDtypeStruct((size, packed_rows, packed_width), rows.dtype),
            jax.ShapeDtypeStruct((block_count + block_count // 2, tile_height, cell_count), tiles.dtype),
            jax.ShapeDtypeStruct((SOURCES * height, size * packed_rows), jnp.bfloat16),
            jax.ShapeDtypeStruct((SOURCES, packed_width, tile_height), jnp.bfloat16),
            jax.ShapeDtypeStruct((height, tile_height), jnp.float32),
        ],
        in_specs=[hbm] * 3,
        out_specs=[vmem] * 5,
        scratch_shapes=[
            pltpu.VMEM(rows.shape, rows.dtype),
            pltpu.VMEM(padded_shape, rows.dtype),
            pltpu.SMEM(blocks.shape, blocks.dtype),
            pltpu.VMEM(tiles.shape, tiles.dtype),
            pltpu.SemaphoreType.DMA((3,)),
        ],
        compiler_params=pltpu.CompilerParams(vmem_limit_bytes=24 * 1024 * 1024),
        cost_estimate=pl.CostEstimate(flops=0, bytes_accessed=tiles.size * 4, transcendentals=0),
    )(rows, blocks, tiles)

    received = exchange(copies, history_order(size))

    coded = pl.pallas_call(
        tile_sums,
        out_shape=jax.ShapeDtypeStruct((size, own_blocks * height + SCALE_ROWS, cell_count), jnp.int16),
        in_specs=[vmem] * 5,
        out_specs=vmem,
        compiler_params=pltpu.CompilerParams(vmem_limit_bytes=20 * 1024 * 1024),
        cost_estimate=pl.CostEstimate(
            flops=2 * slot_count * height * tile_height * cell_count,
            bytes_accessed=propagator.size * 4,
            transcendentals=0,
        ),
    )(received, pick, columns, same, sorted_tiles)

    owned = pl.pallas_call(
        add_parts,
        out_shape=jax.ShapeDtypeStruct((own_blocks, height, cell_count), jnp.float32),
        in_specs=[vmem],
        out_specs=hbm,
        scratch_shapes=[
            pltpu.VMEM((own_blocks, height, cell_count), jnp.float32),
            pltpu.SemaphoreType.DMA((own_blocks,)),
        ],
        compiler_params=pltpu.CompilerParams(vmem_limit_bytes=16 * 1024 * 1024),
    )(exchange(coded, [sums_device(slot, size) for slot in range(size)]))
    return owned.reshape(own_blocks, tracer_count, months, cell_count)


def solution(mesh):
    in_specs = (
        P(("groups", "tm"), None, None, "cells"),
        P(("groups", "tm"), None),
        P("tm", None, None),
    )
    out_specs = P(("groups", "tm"), None, None, "cells")
    return jax.shard_map(shards, mesh=mesh, in_specs=in_specs, out_specs=out_specs, check_vma=False)
```

```python
import jax
import jax.numpy as jnp
from jax import lax
from jax.experimental import pallas as pl
from jax.experimental.pallas import tpu as pltpu
from jax.sharding import PartitionSpec as P

STEPS = 32700.0
LEVELS = 128
SMALLEST = 2.0**-126
SCALE_ROWS = 8
WRITTEN_OUT = 17
SOURCES = 2


def centre(size):
    return size * 5 // 8


def history_order(size):
    inner = [device for device in range(1, size) if device != centre(size)]
    return [centre(size)] + inner[: size // 2 - 1] + [0] + inner[size // 2 - 1 :]


def history_slot(device, size):
    after = device - (device > centre(size)).astype(jnp.int32)
    after = after + (after >= size // 2).astype(jnp.int32)
    return jnp.where(device == centre(size), 0, jnp.where(device == 0, size // 2, after))


def sums_device(slot, size):
    if isinstance(slot, int):
        return centre(size) if slot == 0 else size - slot - (size - slot <= centre(size))
    after = size - slot - (size - slot <= centre(size)).astype(jnp.int32)
    return jnp.where(slot == 0, centre(size), after)


def exchange(value, order):
    return lax.all_to_all(value, "tm", 0, 0, axis_index_groups=[order], tiled=True)


def split(value, divisor):
    if divisor & (divisor - 1):
        return lax.div(value, jnp.full_like(value, divisor)), lax.rem(value, jnp.full_like(value, divisor))
    return value >> (divisor.bit_length() - 1), value & (divisor - 1)


def each(count, body):
    if count <= WRITTEN_OUT:
        for index in range(count):
            body(index)
    else:
        lax.fori_loop(0, count, lambda index, carry: (body(index), carry)[1], 0)


def arrange(
    size, months, source_width, load_blocks, load_tiles, blocks_ref, tiles_ref, sorted_ref, pick_ref, columns_ref
):
    slot_count = tiles_ref.shape[0]
    half_count = sorted_ref.shape[0] // 3
    block_count = half_count * 2
    own_blocks = block_count // size
    height = pick_ref.shape[0] // SOURCES
    packed_rows = pick_ref.shape[1] // size
    tracer = split(lax.broadcasted_iota(jnp.int32, (height, pick_ref.shape[1]), 0), months)[0]
    offset = lax.broadcasted_iota(jnp.int32, (height, pick_ref.shape[1]), 1) - tracer
    column_of = split(lax.broadcasted_iota(jnp.int32, columns_ref.shape[1:], 1), months)[0]
    shift = lax.broadcasted_iota(jnp.int32, columns_ref.shape[1:], 0) - column_of
    load_blocks.wait()
    lower = jnp.minimum(blocks_ref[0, 0], block_count - 1 - blocks_ref[0, 0])

    def place_of(slot):
        return blocks_ref[1, slot] + jnp.where(blocks_ref[0, slot] == lower, 0, half_count)

    places = [place_of(slot) for slot in range(slot_count)] if slot_count <= WRITTEN_OUT else None
    for which, source in enumerate((lower, block_count - 1 - lower)):
        owner, block = split(source, own_blocks)
        picked = offset == history_slot(owner, size) * packed_rows
        pick_ref[pl.ds(which * height, height)] = picked.astype(pick_ref.dtype)
        columns_ref[which] = (shift == block * source_width).astype(columns_ref.dtype)
    load_tiles.wait()

    def place(slot):
        sorted_ref[places[slot] if places else place_of(slot)] = tiles_ref[slot]

    each(slot_count, place)


def prepare(
    months,
    rows_in,
    blocks_in,
    tiles_in,
    copies_ref,
    sorted_ref,
    pick_ref,
    columns_ref,
    same_ref,
    rows_ref,
    padded_ref,
    blocks_ref,
    tiles_ref,
    semaphores,
):
    size, packed_rows, packed_width = copies_ref.shape
    used_rows, source_width = rows_ref.shape
    own_blocks = sorted_ref.shape[0] // 3 * 2 // size
    load_rows = pltpu.make_async_copy(rows_in, rows_ref, semaphores.at[0])
    load_blocks = pltpu.make_async_copy(blocks_in, blocks_ref, semaphores.at[1])
    load_tiles = pltpu.make_async_copy(tiles_in, tiles_ref, semaphores.at[2])
    load_blocks.start()
    load_rows.start()
    load_tiles.start(priority=1)
    month_of_row = split(lax.broadcasted_iota(jnp.int32, same_ref.shape, 0), months)[1]
    month_of_column = split(lax.broadcasted_iota(jnp.int32, same_ref.shape, 1), months)[1]
    same_ref[...] = (month_of_row == month_of_column).astype(same_ref.dtype)
    padded_ref[...] = jnp.zeros(padded_ref.shape, padded_ref.dtype)
    group = sorted_ref.shape[0] // size

    def clear(index):
        sorted_ref[pl.ds(index * group, group)] = jnp.zeros((group,) + sorted_ref.shape[1:], sorted_ref.dtype)

    each(size, clear)
    taker = (packed_rows, padded_ref.shape[0])
    placer = (padded_ref.shape[1], packed_width)
    take = lax.broadcasted_iota(jnp.int32, taker, 1) - lax.broadcasted_iota(jnp.int32, taker, 0) * own_blocks
    put = lax.broadcasted_iota(jnp.int32, placer, 1) - lax.broadcasted_iota(jnp.int32, placer, 0)
    load_rows.wait()
    padded_ref[:used_rows, :source_width] = rows_ref[...]
    packed = jnp.zeros((packed_rows, packed_width), jnp.float32)
    for block in range(own_blocks):
        taken = jnp.dot((take == block).astype(padded_ref.dtype), padded_ref[...], preferred_element_type=jnp.float32)
        packed += jnp.dot(
            taken.astype(padded_ref.dtype),
            (put == block * source_width).astype(padded_ref.dtype),
            preferred_element_type=jnp.float32,
        )
    packed = packed.astype(copies_ref.dtype)

    def copy(owner):
        copies_ref[owner] = packed

    each(size, copy)
    arrange(
        size,
        months,
        source_width,
        load_blocks,
        load_tiles,
        blocks_ref,
        tiles_ref,
        sorted_ref,
        pick_ref,
        columns_ref,
    )


def tile_sums(histories_ref, pick_ref, columns_ref, same_ref, sorted_ref, coded_ref):
    size, packed_rows, packed_width = histories_ref.shape
    half_count = sorted_ref.shape[0] // 3
    own_blocks = half_count * 2 // size
    height = pick_ref.shape[0] // SOURCES
    cell_count = coded_ref.shape[2]
    coded_rows = own_blocks * height

    histories = histories_ref[...].reshape(size * packed_rows, packed_width)
    tall = jnp.dot(pick_ref[...], histories, preferred_element_type=jnp.float32)
    tall = tall.astype(jnp.bfloat16)
    wide = []
    for which in range(SOURCES):
        rows = tall[which * height : (which + 1) * height]
        widened = jnp.dot(rows, columns_ref[which], preferred_element_type=jnp.float32)
        wide.append((widened * same_ref[...]).astype(jnp.bfloat16))

    def product(which, start):
        tiles = jnp.concatenate([sorted_ref[start + block] for block in range(own_blocks)], axis=1)
        return jnp.dot(wide[which], tiles, preferred_element_type=jnp.float32)

    def code(slot):
        owner = sums_device(slot, size)
        start = owner * own_blocks
        total = product(0, start)
        if isinstance(slot, int):
            if owner >= size // 2:
                total += product(1, half_count + start)
        else:
            upper = product(1, half_count + jnp.maximum(start, half_count))
            total += jnp.where(owner >= size // 2, upper, 0.0)
        values = [total[:, block * cell_count : (block + 1) * cell_count] for block in range(own_blocks)]
        top = jnp.abs(values[0])
        for value in values[1:]:
            top = jnp.maximum(top, jnp.abs(value))
        top = jnp.max(top, axis=0, keepdims=True)
        level = jnp.ceil(jnp.log2(jnp.maximum(top, SMALLEST)) * LEVELS)
        half = jnp.exp2(level * (-0.5 / LEVELS))
        for block, value in enumerate(values):
            steps = jnp.round(value * half * (half * STEPS))
            coded_ref[slot, pl.ds(block * height, height)] = steps.astype(jnp.int32).astype(jnp.int16)
        spread = jnp.broadcast_to(level.astype(jnp.int32), (SCALE_ROWS, cell_count))
        coded_ref[slot, pl.ds(coded_rows, SCALE_ROWS)] = spread.astype(jnp.int16)

    each(size, code)


def add_parts(coded_ref, total_out, total_ref, semaphores):
    size = coded_ref.shape[0]
    own_blocks, height, cell_count = total_ref.shape
    stores = []
    for block in range(own_blocks):

        def add(slot, total):
            level = coded_ref[slot, pl.ds(own_blocks * height, SCALE_ROWS)].astype(jnp.int32)
            half = jnp.exp2(level.astype(jnp.float32)[:1] * (0.5 / LEVELS))
            steps = coded_ref[slot, pl.ds(block * height, height)].astype(jnp.int32)
            return total + steps.astype(jnp.float32) * (half * (1.0 / STEPS)) * half

        total = jnp.zeros((height, cell_count), jnp.float32)
        if size <= WRITTEN_OUT:
            for slot in range(size):
                total = add(slot, total)
        else:
            total = lax.fori_loop(0, size, add, total)
        total_ref[block] = total
        stores.append(pltpu.make_async_copy(total_ref.at[block], total_out.at[block], semaphores.at[block]))
        stores[-1].start()
    for store in stores:
        store.wait()


def shards(propagator, tile_blocks, histories):
    size = lax.axis_size("tm")
    own_blocks, tracer_count, source_width = histories.shape
    slot_count, source_width, months, cell_count = propagator.shape
    block_count = size * own_blocks
    height = tracer_count * months
    tile_height = source_width * months

    used_rows = tracer_count * own_blocks
    padded_shape = (used_rows + -used_rows % 16, source_width + -source_width % 128)
    packed_rows = tracer_count + -tracer_count % 16
    packed_width = own_blocks * source_width + -(own_blocks * source_width) % 128
    rows, blocks, tiles = (
        pltpu.with_memory_space_constraint(value, pltpu.HBM)
        for value in (
            jnp.swapaxes(histories, 0, 1).reshape(used_rows, source_width),
            tile_blocks.T,
            propagator.reshape(slot_count, tile_height, cell_count),
        )
    )
    vmem = pl.BlockSpec(memory_space=pltpu.VMEM)
    hbm = pl.BlockSpec(memory_space=pltpu.HBM)
    copies, sorted_tiles, pick, columns, same = pl.pallas_call(
        lambda *refs: prepare(months, *refs),
        out_shape=[
            jax.ShapeDtypeStruct((size, packed_rows, packed_width), rows.dtype),
            jax.ShapeDtypeStruct((block_count + block_count // 2, tile_height, cell_count), tiles.dtype),
            jax.ShapeDtypeStruct((SOURCES * height, size * packed_rows), jnp.bfloat16),
            jax.ShapeDtypeStruct((SOURCES, packed_width, tile_height), jnp.bfloat16),
            jax.ShapeDtypeStruct((height, tile_height), jnp.float32),
        ],
        in_specs=[hbm] * 3,
        out_specs=[vmem] * 5,
        scratch_shapes=[
            pltpu.VMEM(rows.shape, rows.dtype),
            pltpu.VMEM(padded_shape, rows.dtype),
            pltpu.SMEM(blocks.shape, blocks.dtype),
            pltpu.VMEM(tiles.shape, tiles.dtype),
            pltpu.SemaphoreType.DMA((3,)),
        ],
        compiler_params=pltpu.CompilerParams(vmem_limit_bytes=24 * 1024 * 1024),
        cost_estimate=pl.CostEstimate(flops=0, bytes_accessed=tiles.size * 4, transcendentals=0),
    )(rows, blocks, tiles)

    received = exchange(copies, history_order(size))

    coded = pl.pallas_call(
        tile_sums,
        out_shape=jax.ShapeDtypeStruct((size, own_blocks * height + SCALE_ROWS, cell_count), jnp.int16),
        in_specs=[vmem] * 5,
        out_specs=vmem,
        compiler_params=pltpu.CompilerParams(vmem_limit_bytes=20 * 1024 * 1024),
        cost_estimate=pl.CostEstimate(
            flops=2 * slot_count * height * tile_height * cell_count,
            bytes_accessed=propagator.size * 4,
            transcendentals=0,
        ),
    )(received, pick, columns, same, sorted_tiles)

    owned = pl.pallas_call(
        add_parts,
        out_shape=jax.ShapeDtypeStruct((own_blocks, height, cell_count), jnp.float32),
        in_specs=[vmem],
        out_specs=hbm,
        scratch_shapes=[
            pltpu.VMEM((own_blocks, height, cell_count), jnp.float32),
            pltpu.SemaphoreType.DMA((own_blocks,)),
        ],
        compiler_params=pltpu.CompilerParams(vmem_limit_bytes=16 * 1024 * 1024),
    )(exchange(coded, [sums_device(slot, size) for slot in range(size)]))
    return owned.reshape(own_blocks, tracer_count, months, cell_count)


def solution(mesh):
    in_specs = (
        P(("groups", "tm"), None, None, "cells"),
        P(("groups", "tm"), None),
        P("tm", None, None),
    )
    out_specs = P(("groups", "tm"), None, None, "cells")
    return jax.shard_map(shards, mesh=mesh, in_specs=in_specs, out_specs=out_specs, check_vma=False)
```

```python
import jax
import jax.numpy as jnp
from jax import lax
from jax.experimental import pallas as pl
from jax.experimental.pallas import tpu as pltpu
from jax.sharding import PartitionSpec as P

STEPS = 32700.0
LEVELS = 128
SMALLEST = 2.0**-126
SCALE_ROWS = 8
WRITTEN_OUT = 17
SOURCES = 2


def centre(size):
    return size * 5 // 8


def history_order(size):
    inner = [device for device in range(1, size) if device != centre(size)]
    return [centre(size)] + inner[: size // 2 - 1] + [0] + inner[size // 2 - 1 :]


def history_slot(device, size):
    after = device - (device > centre(size)).astype(jnp.int32)
    after = after + (after >= size // 2).astype(jnp.int32)
    return jnp.where(device == centre(size), 0, jnp.where(device == 0, size // 2, after))


def sums_device(slot, size):
    if isinstance(slot, int):
        return centre(size) if slot == 0 else size - slot - (size - slot <= centre(size))
    after = size - slot - (size - slot <= centre(size)).astype(jnp.int32)
    return jnp.where(slot == 0, centre(size), after)


def exchange(value, order):
    return lax.all_to_all(value, "tm", 0, 0, axis_index_groups=[order], tiled=True)


def split(value, divisor):
    if divisor & (divisor - 1):
        return lax.div(value, jnp.full_like(value, divisor)), lax.rem(value, jnp.full_like(value, divisor))
    return value >> (divisor.bit_length() - 1), value & (divisor - 1)


def each(count, body):
    if count <= WRITTEN_OUT:
        for index in range(count):
            body(index)
    else:
        lax.fori_loop(0, count, lambda index, carry: (body(index), carry)[1], 0)


def arrange(
    size, months, source_width, load_blocks, load_tiles, blocks_ref, tiles_ref, sorted_ref, pick_ref, columns_ref
):
    slot_count = tiles_ref.shape[0]
    half_count = sorted_ref.shape[0] // 3
    block_count = half_count * 2
    own_blocks = block_count // size
    height = pick_ref.shape[0] // SOURCES
    packed_rows = pick_ref.shape[1] // size
    tracer = split(lax.broadcasted_iota(jnp.int32, (height, pick_ref.shape[1]), 0), months)[0]
    offset = lax.broadcasted_iota(jnp.int32, (height, pick_ref.shape[1]), 1) - tracer
    column_of = split(lax.broadcasted_iota(jnp.int32, columns_ref.shape[1:], 1), months)[0]
    shift = lax.broadcasted_iota(jnp.int32, columns_ref.shape[1:], 0) - column_of
    load_blocks.wait()
    lower = jnp.minimum(blocks_ref[0, 0], block_count - 1 - blocks_ref[0, 0])

    def place_of(slot):
        return blocks_ref[1, slot] + jnp.where(blocks_ref[0, slot] == lower, 0, half_count)

    places = [place_of(slot) for slot in range(slot_count)] if slot_count <= WRITTEN_OUT else None
    for which, source in enumerate((lower, block_count - 1 - lower)):
        owner, block = split(source, own_blocks)
        picked = offset == history_slot(owner, size) * packed_rows
        pick_ref[pl.ds(which * height, height)] = picked.astype(pick_ref.dtype)
        columns_ref[which] = (shift == block * source_width).astype(columns_ref.dtype)

    def place(slot):
        sorted_ref[places[slot] if places else place_of(slot)] = tiles_ref[slot]

    middle = slot_count // 2
    load_tiles[0].wait()
    each(middle, place)
    load_tiles[1].wait()
    each(slot_count - middle, lambda slot: place(middle + slot))


def prepare(
    months,
    rows_in,
    blocks_in,
    tiles_in,
    copies_ref,
    sorted_ref,
    pick_ref,
    columns_ref,
    same_ref,
    rows_ref,
    padded_ref,
    blocks_ref,
    tiles_ref,
    semaphores,
):
    size, packed_rows, packed_width = copies_ref.shape
    used_rows, source_width = rows_ref.shape
    own_blocks = sorted_ref.shape[0] // 3 * 2 // size
    load_rows = pltpu.make_async_copy(rows_in, rows_ref, semaphores.at[0])
    load_blocks = pltpu.make_async_copy(blocks_in, blocks_ref, semaphores.at[1])
    middle = tiles_ref.shape[0] // 2
    load_tiles = [
        pltpu.make_async_copy(
            tiles_in.at[pl.ds(start, count)], tiles_ref.at[pl.ds(start, count)], semaphores.at[2 + half]
        )
        for half, (start, count) in enumerate([(0, middle), (middle, tiles_ref.shape[0] - middle)])
    ]
    for load in (load_rows, load_blocks, *load_tiles):
        load.start()
    month_of_row = split(lax.broadcasted_iota(jnp.int32, same_ref.shape, 0), months)[1]
    month_of_column = split(lax.broadcasted_iota(jnp.int32, same_ref.shape, 1), months)[1]
    same_ref[...] = (month_of_row == month_of_column).astype(same_ref.dtype)
    padded_ref[...] = jnp.zeros(padded_ref.shape, padded_ref.dtype)
    group = sorted_ref.shape[0] // size

    def clear(index):
        sorted_ref[pl.ds(index * group, group)] = jnp.zeros((group,) + sorted_ref.shape[1:], sorted_ref.dtype)

    each(size, clear)
    taker = (packed_rows, padded_ref.shape[0])
    placer = (padded_ref.shape[1], packed_width)
    take = lax.broadcasted_iota(jnp.int32, taker, 1) - lax.broadcasted_iota(jnp.int32, taker, 0) * own_blocks
    put = lax.broadcasted_iota(jnp.int32, placer, 1) - lax.broadcasted_iota(jnp.int32, placer, 0)
    load_rows.wait()
    padded_ref[:used_rows, :source_width] = rows_ref[...]
    packed = jnp.zeros((packed_rows, packed_width), jnp.float32)
    for block in range(own_blocks):
        taken = jnp.dot((take == block).astype(padded_ref.dtype), padded_ref[...], preferred_element_type=jnp.float32)
        packed += jnp.dot(
            taken.astype(padded_ref.dtype),
            (put == block * source_width).astype(padded_ref.dtype),
            preferred_element_type=jnp.float32,
        )
    packed = packed.astype(copies_ref.dtype)

    def copy(owner):
        copies_ref[owner] = packed

    each(size, copy)
    arrange(
        size,
        months,
        source_width,
        load_blocks,
        load_tiles,
        blocks_ref,
        tiles_ref,
        sorted_ref,
        pick_ref,
        columns_ref,
    )


def tile_sums(histories_ref, pick_ref, columns_ref, same_ref, sorted_ref, coded_ref):
    size, packed_rows, packed_width = histories_ref.shape
    half_count = sorted_ref.shape[0] // 3
    own_blocks = half_count * 2 // size
    height = pick_ref.shape[0] // SOURCES
    cell_count = coded_ref.shape[2]
    coded_rows = own_blocks * height

    histories = histories_ref[...].reshape(size * packed_rows, packed_width)
    tall = jnp.dot(pick_ref[...], histories, preferred_element_type=jnp.float32)
    tall = tall.astype(jnp.bfloat16)
    wide = []
    for which in range(SOURCES):
        rows = tall[which * height : (which + 1) * height]
        widened = jnp.dot(rows, columns_ref[which], preferred_element_type=jnp.float32)
        wide.append((widened * same_ref[...]).astype(jnp.bfloat16))

    def product(which, start):
        tiles = jnp.concatenate([sorted_ref[start + block] for block in range(own_blocks)], axis=1)
        return jnp.dot(wide[which], tiles, preferred_element_type=jnp.float32)

    def code(slot):
        owner = sums_device(slot, size)
        start = owner * own_blocks
        total = product(0, start)
        if isinstance(slot, int):
            if owner >= size // 2:
                total += product(1, half_count + start)
        else:
            upper = product(1, half_count + jnp.maximum(start, half_count))
            total += jnp.where(owner >= size // 2, upper, 0.0)
        values = [total[:, block * cell_count : (block + 1) * cell_count] for block in range(own_blocks)]
        top = jnp.abs(values[0])
        for value in values[1:]:
            top = jnp.maximum(top, jnp.abs(value))
        top = jnp.max(top, axis=0, keepdims=True)
        level = jnp.ceil(jnp.log2(jnp.maximum(top, SMALLEST)) * LEVELS)
        half = jnp.exp2(level * (-0.5 / LEVELS))
        for block, value in enumerate(values):
            steps = jnp.round(value * half * (half * STEPS))
            coded_ref[slot, pl.ds(block * height, height)] = steps.astype(jnp.int32).astype(jnp.int16)
        spread = jnp.broadcast_to(level.astype(jnp.int32), (SCALE_ROWS, cell_count))
        coded_ref[slot, pl.ds(coded_rows, SCALE_ROWS)] = spread.astype(jnp.int16)

    each(size, code)


def add_parts(coded_ref, total_out, total_ref, semaphores):
    size = coded_ref.shape[0]
    own_blocks, height, cell_count = total_ref.shape
    stores = []
    for block in range(own_blocks):

        def add(slot, total):
            level = coded_ref[slot, pl.ds(own_blocks * height, SCALE_ROWS)].astype(jnp.int32)
            half = jnp.exp2(level.astype(jnp.float32)[:1] * (0.5 / LEVELS))
            steps = coded_ref[slot, pl.ds(block * height, height)].astype(jnp.int32)
            return total + steps.astype(jnp.float32) * (half * (1.0 / STEPS)) * half

        total = jnp.zeros((height, cell_count), jnp.float32)
        if size <= WRITTEN_OUT:
            for slot in range(size):
                total = add(slot, total)
        else:
            total = lax.fori_loop(0, size, add, total)
        total_ref[block] = total
        stores.append(pltpu.make_async_copy(total_ref.at[block], total_out.at[block], semaphores.at[block]))
        stores[-1].start()
    for store in stores:
        store.wait()


def shards(propagator, tile_blocks, histories):
    size = lax.axis_size("tm")
    own_blocks, tracer_count, source_width = histories.shape
    slot_count, source_width, months, cell_count = propagator.shape
    block_count = size * own_blocks
    height = tracer_count * months
    tile_height = source_width * months

    used_rows = tracer_count * own_blocks
    padded_shape = (used_rows + -used_rows % 16, source_width + -source_width % 128)
    packed_rows = tracer_count + -tracer_count % 16
    packed_width = own_blocks * source_width + -(own_blocks * source_width) % 128
    rows, blocks, tiles = (
        pltpu.with_memory_space_constraint(value, pltpu.HBM)
        for value in (
            jnp.swapaxes(histories, 0, 1).reshape(used_rows, source_width),
            tile_blocks.T,
            propagator.reshape(slot_count, tile_height, cell_count),
        )
    )
    vmem = pl.BlockSpec(memory_space=pltpu.VMEM)
    hbm = pl.BlockSpec(memory_space=pltpu.HBM)
    copies, sorted_tiles, pick, columns, same = pl.pallas_call(
        lambda *refs: prepare(months, *refs),
        out_shape=[
            jax.ShapeDtypeStruct((size, packed_rows, packed_width), rows.dtype),
            jax.ShapeDtypeStruct((block_count + block_count // 2, tile_height, cell_count), tiles.dtype),
            jax.ShapeDtypeStruct((SOURCES * height, size * packed_rows), jnp.bfloat16),
            jax.ShapeDtypeStruct((SOURCES, packed_width, tile_height), jnp.bfloat16),
            jax.ShapeDtypeStruct((height, tile_height), jnp.float32),
        ],
        in_specs=[hbm] * 3,
        out_specs=[vmem] * 5,
        scratch_shapes=[
            pltpu.VMEM(rows.shape, rows.dtype),
            pltpu.VMEM(padded_shape, rows.dtype),
            pltpu.SMEM(blocks.shape, blocks.dtype),
            pltpu.VMEM(tiles.shape, tiles.dtype),
            pltpu.SemaphoreType.DMA((4,)),
        ],
        compiler_params=pltpu.CompilerParams(vmem_limit_bytes=24 * 1024 * 1024),
        cost_estimate=pl.CostEstimate(flops=0, bytes_accessed=tiles.size * 4, transcendentals=0),
    )(rows, blocks, tiles)

    received = exchange(copies, history_order(size))

    coded = pl.pallas_call(
        tile_sums,
        out_shape=jax.ShapeDtypeStruct((size, own_blocks * height + SCALE_ROWS, cell_count), jnp.int16),
        in_specs=[vmem] * 5,
        out_specs=vmem,
        compiler_params=pltpu.CompilerParams(vmem_limit_bytes=20 * 1024 * 1024),
        cost_estimate=pl.CostEstimate(
            flops=2 * slot_count * height * tile_height * cell_count,
            bytes_accessed=propagator.size * 4,
            transcendentals=0,
        ),
    )(received, pick, columns, same, sorted_tiles)

    owned = pl.pallas_call(
        add_parts,
        out_shape=jax.ShapeDtypeStruct((own_blocks, height, cell_count), jnp.float32),
        in_specs=[vmem],
        out_specs=hbm,
        scratch_shapes=[
            pltpu.VMEM((own_blocks, height, cell_count), jnp.float32),
            pltpu.SemaphoreType.DMA((own_blocks,)),
        ],
        compiler_params=pltpu.CompilerParams(vmem_limit_bytes=16 * 1024 * 1024),
    )(exchange(coded, [sums_device(slot, size) for slot in range(size)]))
    return owned.reshape(own_blocks, tracer_count, months, cell_count)


def solution(mesh):
    in_specs = (
        P(("groups", "tm"), None, None, "cells"),
        P(("groups", "tm"), None),
        P("tm", None, None),
    )
    out_specs = P(("groups", "tm"), None, None, "cells")
    return jax.shard_map(shards, mesh=mesh, in_specs=in_specs, out_specs=out_specs, check_vma=False)
```

```python
import jax
import jax.numpy as jnp
from jax import lax
from jax.experimental import pallas as pl
from jax.experimental.pallas import tpu as pltpu
from jax.sharding import PartitionSpec as P

STEPS = 32700.0
LEVELS = 128
SMALLEST = 2.0**-126
SCALE_ROWS = 8
PARTS = 4
WRITTEN_OUT = 17
SOURCES = 2


def centre(size):
    return size * 5 // 8


def history_order(size):
    inner = [device for device in range(1, size) if device != centre(size)]
    return [centre(size)] + inner[: size // 2 - 1] + [0] + inner[size // 2 - 1 :]


def history_slot(device, size):
    after = device - (device > centre(size)).astype(jnp.int32)
    after = after + (after >= size // 2).astype(jnp.int32)
    return jnp.where(device == centre(size), 0, jnp.where(device == 0, size // 2, after))


def sums_device(slot, size):
    if isinstance(slot, int):
        return centre(size) if slot == 0 else size - slot - (size - slot <= centre(size))
    after = size - slot - (size - slot <= centre(size)).astype(jnp.int32)
    return jnp.where(slot == 0, centre(size), after)


def exchange(value, order):
    return lax.all_to_all(value, "tm", 0, 0, axis_index_groups=[order], tiled=True)


def split(value, divisor):
    if divisor & (divisor - 1):
        return lax.div(value, jnp.full_like(value, divisor)), lax.rem(value, jnp.full_like(value, divisor))
    return value >> (divisor.bit_length() - 1), value & (divisor - 1)


def each(count, body):
    if count <= WRITTEN_OUT:
        for index in range(count):
            body(index)
    else:
        lax.fori_loop(0, count, lambda index, carry: (body(index), carry)[1], 0)


def parts_of(count):
    return [range(count * part // PARTS, count * (part + 1) // PARTS) for part in range(PARTS)]


def arrange(
    size, months, source_width, load_blocks, load_tiles, blocks_ref, tiles_ref, sorted_ref, pick_ref, columns_ref
):
    slot_count = tiles_ref.shape[0]
    half_count = sorted_ref.shape[0] // 3
    block_count = half_count * 2
    own_blocks = block_count // size
    height = pick_ref.shape[0] // SOURCES
    packed_rows = pick_ref.shape[1] // size
    tracer = split(lax.broadcasted_iota(jnp.int32, (height, pick_ref.shape[1]), 0), months)[0]
    offset = lax.broadcasted_iota(jnp.int32, (height, pick_ref.shape[1]), 1) - tracer
    column_of = split(lax.broadcasted_iota(jnp.int32, columns_ref.shape[1:], 1), months)[0]
    shift = lax.broadcasted_iota(jnp.int32, columns_ref.shape[1:], 0) - column_of
    load_blocks.wait()
    lower = jnp.minimum(blocks_ref[0, 0], block_count - 1 - blocks_ref[0, 0])

    def place_of(slot):
        return blocks_ref[1, slot] + jnp.where(blocks_ref[0, slot] == lower, 0, half_count)

    places = [place_of(slot) for slot in range(slot_count)] if slot_count <= WRITTEN_OUT else None
    for which, source in enumerate((lower, block_count - 1 - lower)):
        owner, block = split(source, own_blocks)
        picked = offset == history_slot(owner, size) * packed_rows
        pick_ref[pl.ds(which * height, height)] = picked.astype(pick_ref.dtype)
        columns_ref[which] = (shift == block * source_width).astype(columns_ref.dtype)

    def place(slot):
        sorted_ref[places[slot] if places else place_of(slot)] = tiles_ref[slot]

    for load, part in zip(load_tiles, parts_of(slot_count)):
        load.wait()
        each(len(part), lambda slot, part=part: place(part.start + slot))


def prepare(
    months,
    rows_in,
    blocks_in,
    tiles_in,
    copies_ref,
    sorted_ref,
    pick_ref,
    columns_ref,
    same_ref,
    rows_ref,
    padded_ref,
    blocks_ref,
    tiles_ref,
    semaphores,
):
    size, packed_rows, packed_width = copies_ref.shape
    used_rows, source_width = rows_ref.shape
    own_blocks = sorted_ref.shape[0] // 3 * 2 // size
    load_rows = pltpu.make_async_copy(rows_in, rows_ref, semaphores.at[0])
    load_blocks = pltpu.make_async_copy(blocks_in, blocks_ref, semaphores.at[1])
    load_tiles = [
        pltpu.make_async_copy(
            tiles_in.at[pl.ds(part.start, len(part))],
            tiles_ref.at[pl.ds(part.start, len(part))],
            semaphores.at[2 + index],
        )
        for index, part in enumerate(parts_of(tiles_ref.shape[0]))
    ]
    for load in (load_rows, load_blocks, *load_tiles):
        load.start()
    month_of_row = split(lax.broadcasted_iota(jnp.int32, same_ref.shape, 0), months)[1]
    month_of_column = split(lax.broadcasted_iota(jnp.int32, same_ref.shape, 1), months)[1]
    same_ref[...] = (month_of_row == month_of_column).astype(same_ref.dtype)
    padded_ref[...] = jnp.zeros(padded_ref.shape, padded_ref.dtype)
    group = sorted_ref.shape[0] // size

    def clear(index):
        sorted_ref[pl.ds(index * group, group)] = jnp.zeros((group,) + sorted_ref.shape[1:], sorted_ref.dtype)

    each(size, clear)
    taker = (packed_rows, padded_ref.shape[0])
    placer = (padded_ref.shape[1], packed_width)
    take = lax.broadcasted_iota(jnp.int32, taker, 1) - lax.broadcasted_iota(jnp.int32, taker, 0) * own_blocks
    put = lax.broadcasted_iota(jnp.int32, placer, 1) - lax.broadcasted_iota(jnp.int32, placer, 0)
    load_rows.wait()
    padded_ref[:used_rows, :source_width] = rows_ref[...]
    packed = jnp.zeros((packed_rows, packed_width), jnp.float32)
    for block in range(own_blocks):
        taken = jnp.dot((take == block).astype(padded_ref.dtype), padded_ref[...], preferred_element_type=jnp.float32)
        packed += jnp.dot(
            taken.astype(padded_ref.dtype),
            (put == block * source_width).astype(padded_ref.dtype),
            preferred_element_type=jnp.float32,
        )
    packed = packed.astype(copies_ref.dtype)

    def copy(owner):
        copies_ref[owner] = packed

    each(size, copy)
    arrange(
        size,
        months,
        source_width,
        load_blocks,
        load_tiles,
        blocks_ref,
        tiles_ref,
        sorted_ref,
        pick_ref,
        columns_ref,
    )


def tile_sums(histories_ref, pick_ref, columns_ref, same_ref, sorted_ref, coded_ref):
    size, packed_rows, packed_width = histories_ref.shape
    half_count = sorted_ref.shape[0] // 3
    own_blocks = half_count * 2 // size
    height = pick_ref.shape[0] // SOURCES
    cell_count = coded_ref.shape[2]
    coded_rows = own_blocks * height

    histories = histories_ref[...].reshape(size * packed_rows, packed_width)
    tall = jnp.dot(pick_ref[...], histories, preferred_element_type=jnp.float32)
    tall = tall.astype(jnp.bfloat16)
    wide = []
    for which in range(SOURCES):
        rows = tall[which * height : (which + 1) * height]
        widened = jnp.dot(rows, columns_ref[which], preferred_element_type=jnp.float32)
        wide.append((widened * same_ref[...]).astype(jnp.bfloat16))

    def product(which, start):
        tiles = jnp.concatenate([sorted_ref[start + block] for block in range(own_blocks)], axis=1)
        return jnp.dot(wide[which], tiles, preferred_element_type=jnp.float32)

    def code(slot):
        owner = sums_device(slot, size)
        start = owner * own_blocks
        total = product(0, start)
        if isinstance(slot, int):
            if owner >= size // 2:
                total += product(1, half_count + start)
        else:
            upper = product(1, half_count + jnp.maximum(start, half_count))
            total += jnp.where(owner >= size // 2, upper, 0.0)
        values = [total[:, block * cell_count : (block + 1) * cell_count] for block in range(own_blocks)]
        top = jnp.abs(values[0])
        for value in values[1:]:
            top = jnp.maximum(top, jnp.abs(value))
        top = jnp.max(top, axis=0, keepdims=True)
        level = jnp.ceil(jnp.log2(jnp.maximum(top, SMALLEST)) * LEVELS)
        half = jnp.exp2(level * (-0.5 / LEVELS))
        for block, value in enumerate(values):
            steps = jnp.round(value * half * (half * STEPS))
            coded_ref[slot, pl.ds(block * height, height)] = steps.astype(jnp.int32).astype(jnp.int16)
        spread = jnp.broadcast_to(level.astype(jnp.int32), (SCALE_ROWS, cell_count))
        coded_ref[slot, pl.ds(coded_rows, SCALE_ROWS)] = spread.astype(jnp.int16)

    each(size, code)


def add_parts(coded_ref, total_out, total_ref, semaphores):
    size = coded_ref.shape[0]
    own_blocks, height, cell_count = total_ref.shape
    stores = []
    for block in range(own_blocks):

        def add(slot, total):
            level = coded_ref[slot, pl.ds(own_blocks * height, SCALE_ROWS)].astype(jnp.int32)
            half = jnp.exp2(level.astype(jnp.float32)[:1] * (0.5 / LEVELS))
            steps = coded_ref[slot, pl.ds(block * height, height)].astype(jnp.int32)
            return total + steps.astype(jnp.float32) * (half * (1.0 / STEPS)) * half

        total = jnp.zeros((height, cell_count), jnp.float32)
        if size <= WRITTEN_OUT:
            for slot in range(size):
                total = add(slot, total)
        else:
            total = lax.fori_loop(0, size, add, total)
        total_ref[block] = total
        stores.append(pltpu.make_async_copy(total_ref.at[block], total_out.at[block], semaphores.at[block]))
        stores[-1].start()
    for store in stores:
        store.wait()


def shards(propagator, tile_blocks, histories):
    size = lax.axis_size("tm")
    own_blocks, tracer_count, source_width = histories.shape
    slot_count, source_width, months, cell_count = propagator.shape
    block_count = size * own_blocks
    height = tracer_count * months
    tile_height = source_width * months

    used_rows = tracer_count * own_blocks
    padded_shape = (used_rows + -used_rows % 16, source_width + -source_width % 128)
    packed_rows = tracer_count + -tracer_count % 16
    packed_width = own_blocks * source_width + -(own_blocks * source_width) % 128
    rows, blocks, tiles = (
        pltpu.with_memory_space_constraint(value, pltpu.HBM)
        for value in (
            jnp.swapaxes(histories, 0, 1).reshape(used_rows, source_width),
            tile_blocks.T,
            propagator.reshape(slot_count, tile_height, cell_count),
        )
    )
    vmem = pl.BlockSpec(memory_space=pltpu.VMEM)
    hbm = pl.BlockSpec(memory_space=pltpu.HBM)
    copies, sorted_tiles, pick, columns, same = pl.pallas_call(
        lambda *refs: prepare(months, *refs),
        out_shape=[
            jax.ShapeDtypeStruct((size, packed_rows, packed_width), rows.dtype),
            jax.ShapeDtypeStruct((block_count + block_count // 2, tile_height, cell_count), tiles.dtype),
            jax.ShapeDtypeStruct((SOURCES * height, size * packed_rows), jnp.bfloat16),
            jax.ShapeDtypeStruct((SOURCES, packed_width, tile_height), jnp.bfloat16),
            jax.ShapeDtypeStruct((height, tile_height), jnp.float32),
        ],
        in_specs=[hbm] * 3,
        out_specs=[vmem] * 5,
        scratch_shapes=[
            pltpu.VMEM(rows.shape, rows.dtype),
            pltpu.VMEM(padded_shape, rows.dtype),
            pltpu.SMEM(blocks.shape, blocks.dtype),
            pltpu.VMEM(tiles.shape, tiles.dtype),
            pltpu.SemaphoreType.DMA((2 + PARTS,)),
        ],
        compiler_params=pltpu.CompilerParams(vmem_limit_bytes=24 * 1024 * 1024),
        cost_estimate=pl.CostEstimate(flops=0, bytes_accessed=tiles.size * 4, transcendentals=0),
    )(rows, blocks, tiles)

    received = exchange(copies, history_order(size))

    coded = pl.pallas_call(
        tile_sums,
        out_shape=jax.ShapeDtypeStruct((size, own_blocks * height + SCALE_ROWS, cell_count), jnp.int16),
        in_specs=[vmem] * 5,
        out_specs=vmem,
        compiler_params=pltpu.CompilerParams(vmem_limit_bytes=20 * 1024 * 1024),
        cost_estimate=pl.CostEstimate(
            flops=2 * slot_count * height * tile_height * cell_count,
            bytes_accessed=propagator.size * 4,
            transcendentals=0,
        ),
    )(received, pick, columns, same, sorted_tiles)

    owned = pl.pallas_call(
        add_parts,
        out_shape=jax.ShapeDtypeStruct((own_blocks, height, cell_count), jnp.float32),
        in_specs=[vmem],
        out_specs=hbm,
        scratch_shapes=[
            pltpu.VMEM((own_blocks, height, cell_count), jnp.float32),
            pltpu.SemaphoreType.DMA((own_blocks,)),
        ],
        compiler_params=pltpu.CompilerParams(vmem_limit_bytes=16 * 1024 * 1024),
    )(exchange(coded, [sums_device(slot, size) for slot in range(size)]))
    return owned.reshape(own_blocks, tracer_count, months, cell_count)


def solution(mesh):
    in_specs = (
        P(("groups", "tm"), None, None, "cells"),
        P(("groups", "tm"), None),
        P("tm", None, None),
    )
    out_specs = P(("groups", "tm"), None, None, "cells")
    return jax.shard_map(shards, mesh=mesh, in_specs=in_specs, out_specs=out_specs, check_vma=False)
```

```python
import jax
import jax.numpy as jnp
from jax import lax
from jax.experimental import pallas as pl
from jax.experimental.pallas import tpu as pltpu
from jax.sharding import PartitionSpec as P

STEPS = 32700.0
LEVELS = 128
SMALLEST = 2.0**-126
SCALE_ROWS = 8
WRITTEN_OUT = 17
SOURCES = 2


def centre(size):
    return size * 5 // 8


def history_order(size):
    inner = [device for device in range(1, size) if device != centre(size)]
    return [centre(size)] + inner[: size // 2 - 1] + [0] + inner[size // 2 - 1 :]


def history_slot(device, size):
    after = device - (device > centre(size)).astype(jnp.int32)
    after = after + (after >= size // 2).astype(jnp.int32)
    return jnp.where(device == centre(size), 0, jnp.where(device == 0, size // 2, after))


def sums_device(slot, size):
    if isinstance(slot, int):
        return centre(size) if slot == 0 else size - slot - (size - slot <= centre(size))
    after = size - slot - (size - slot <= centre(size)).astype(jnp.int32)
    return jnp.where(slot == 0, centre(size), after)


def exchange(value, order):
    return lax.all_to_all(value, "tm", 0, 0, axis_index_groups=[order], tiled=True)


def split(value, divisor):
    if divisor & (divisor - 1):
        return lax.div(value, jnp.full_like(value, divisor)), lax.rem(value, jnp.full_like(value, divisor))
    return value >> (divisor.bit_length() - 1), value & (divisor - 1)


def each(count, body):
    if count <= WRITTEN_OUT:
        for index in range(count):
            body(index)
    else:
        lax.fori_loop(0, count, lambda index, carry: (body(index), carry)[1], 0)


def arrange(
    size, months, source_width, load_blocks, load_tiles, blocks_ref, tiles_ref, sorted_ref, pick_ref, columns_ref
):
    slot_count = tiles_ref.shape[0]
    half_count = sorted_ref.shape[0] // 3
    block_count = half_count * 2
    own_blocks = block_count // size
    height = pick_ref.shape[0] // SOURCES
    packed_rows = pick_ref.shape[1] // size
    tracer = split(lax.broadcasted_iota(jnp.int32, (height, pick_ref.shape[1]), 0), months)[0]
    offset = lax.broadcasted_iota(jnp.int32, (height, pick_ref.shape[1]), 1) - tracer
    column_of = split(lax.broadcasted_iota(jnp.int32, columns_ref.shape[1:], 1), months)[0]
    shift = lax.broadcasted_iota(jnp.int32, columns_ref.shape[1:], 0) - column_of
    load_blocks.wait()
    lower = jnp.minimum(blocks_ref[0, 0], block_count - 1 - blocks_ref[0, 0])

    def place_of(slot):
        return blocks_ref[1, slot] + jnp.where(blocks_ref[0, slot] == lower, 0, half_count)

    places = [place_of(slot) for slot in range(slot_count)] if slot_count <= WRITTEN_OUT else None
    for which, source in enumerate((lower, block_count - 1 - lower)):
        owner, block = split(source, own_blocks)
        picked = offset == history_slot(owner, size) * packed_rows
        pick_ref[pl.ds(which * height, height)] = picked.astype(pick_ref.dtype)
        columns_ref[which] = (shift == block * source_width).astype(columns_ref.dtype)

    def place(slot):
        sorted_ref[places[slot] if places else place_of(slot)] = tiles_ref[slot]

    middle = slot_count * 2 // 3
    load_tiles[0].wait()
    each(middle, place)
    load_tiles[1].wait()
    each(slot_count - middle, lambda slot: place(middle + slot))


def prepare(
    months,
    rows_in,
    blocks_in,
    tiles_in,
    copies_ref,
    sorted_ref,
    pick_ref,
    columns_ref,
    same_ref,
    rows_ref,
    padded_ref,
    blocks_ref,
    tiles_ref,
    semaphores,
):
    size, packed_rows, packed_width = copies_ref.shape
    used_rows, source_width = rows_ref.shape
    own_blocks = sorted_ref.shape[0] // 3 * 2 // size
    load_rows = pltpu.make_async_copy(rows_in, rows_ref, semaphores.at[0])
    load_blocks = pltpu.make_async_copy(blocks_in, blocks_ref, semaphores.at[1])
    middle = tiles_ref.shape[0] * 2 // 3
    load_tiles = [
        pltpu.make_async_copy(
            tiles_in.at[pl.ds(start, count)], tiles_ref.at[pl.ds(start, count)], semaphores.at[2 + half]
        )
        for half, (start, count) in enumerate([(0, middle), (middle, tiles_ref.shape[0] - middle)])
    ]
    for load in (load_rows, load_blocks, *load_tiles):
        load.start()
    month_of_row = split(lax.broadcasted_iota(jnp.int32, same_ref.shape, 0), months)[1]
    month_of_column = split(lax.broadcasted_iota(jnp.int32, same_ref.shape, 1), months)[1]
    same_ref[...] = (month_of_row == month_of_column).astype(same_ref.dtype)
    padded_ref[...] = jnp.zeros(padded_ref.shape, padded_ref.dtype)
    group = sorted_ref.shape[0] // size

    def clear(index):
        sorted_ref[pl.ds(index * group, group)] = jnp.zeros((group,) + sorted_ref.shape[1:], sorted_ref.dtype)

    each(size, clear)
    taker = (packed_rows, padded_ref.shape[0])
    placer = (padded_ref.shape[1], packed_width)
    take = lax.broadcasted_iota(jnp.int32, taker, 1) - lax.broadcasted_iota(jnp.int32, taker, 0) * own_blocks
    put = lax.broadcasted_iota(jnp.int32, placer, 1) - lax.broadcasted_iota(jnp.int32, placer, 0)
    load_rows.wait()
    padded_ref[:used_rows, :source_width] = rows_ref[...]
    packed = jnp.zeros((packed_rows, packed_width), jnp.float32)
    for block in range(own_blocks):
        taken = jnp.dot((take == block).astype(padded_ref.dtype), padded_ref[...], preferred_element_type=jnp.float32)
        packed += jnp.dot(
            taken.astype(padded_ref.dtype),
            (put == block * source_width).astype(padded_ref.dtype),
            preferred_element_type=jnp.float32,
        )
    packed = packed.astype(copies_ref.dtype)

    def copy(owner):
        copies_ref[owner] = packed

    each(size, copy)
    arrange(
        size,
        months,
        source_width,
        load_blocks,
        load_tiles,
        blocks_ref,
        tiles_ref,
        sorted_ref,
        pick_ref,
        columns_ref,
    )


def tile_sums(histories_ref, pick_ref, columns_ref, same_ref, sorted_ref, coded_ref):
    size, packed_rows, packed_width = histories_ref.shape
    half_count = sorted_ref.shape[0] // 3
    own_blocks = half_count * 2 // size
    height = pick_ref.shape[0] // SOURCES
    cell_count = coded_ref.shape[2]
    coded_rows = own_blocks * height

    histories = histories_ref[...].reshape(size * packed_rows, packed_width)
    tall = jnp.dot(pick_ref[...], histories, preferred_element_type=jnp.float32)
    tall = tall.astype(jnp.bfloat16)
    wide = []
    for which in range(SOURCES):
        rows = tall[which * height : (which + 1) * height]
        widened = jnp.dot(rows, columns_ref[which], preferred_element_type=jnp.float32)
        wide.append((widened * same_ref[...]).astype(jnp.bfloat16))

    def product(which, start):
        tiles = jnp.concatenate([sorted_ref[start + block] for block in range(own_blocks)], axis=1)
        return jnp.dot(wide[which], tiles, preferred_element_type=jnp.float32)

    def code(slot):
        owner = sums_device(slot, size)
        start = owner * own_blocks
        total = product(0, start)
        if isinstance(slot, int):
            if owner >= size // 2:
                total += product(1, half_count + start)
        else:
            upper = product(1, half_count + jnp.maximum(start, half_count))
            total += jnp.where(owner >= size // 2, upper, 0.0)
        values = [total[:, block * cell_count : (block + 1) * cell_count] for block in range(own_blocks)]
        top = jnp.abs(values[0])
        for value in values[1:]:
            top = jnp.maximum(top, jnp.abs(value))
        top = jnp.max(top, axis=0, keepdims=True)
        level = jnp.ceil(jnp.log2(jnp.maximum(top, SMALLEST)) * LEVELS)
        half = jnp.exp2(level * (-0.5 / LEVELS))
        for block, value in enumerate(values):
            steps = jnp.round(value * half * (half * STEPS))
            coded_ref[slot, pl.ds(block * height, height)] = steps.astype(jnp.int32).astype(jnp.int16)
        spread = jnp.broadcast_to(level.astype(jnp.int32), (SCALE_ROWS, cell_count))
        coded_ref[slot, pl.ds(coded_rows, SCALE_ROWS)] = spread.astype(jnp.int16)

    each(size, code)


def add_parts(coded_ref, total_out, total_ref, semaphores):
    size = coded_ref.shape[0]
    own_blocks, height, cell_count = total_ref.shape
    stores = []
    for block in range(own_blocks):

        def add(slot, total):
            level = coded_ref[slot, pl.ds(own_blocks * height, SCALE_ROWS)].astype(jnp.int32)
            half = jnp.exp2(level.astype(jnp.float32)[:1] * (0.5 / LEVELS))
            steps = coded_ref[slot, pl.ds(block * height, height)].astype(jnp.int32)
            return total + steps.astype(jnp.float32) * (half * (1.0 / STEPS)) * half

        total = jnp.zeros((height, cell_count), jnp.float32)
        if size <= WRITTEN_OUT:
            for slot in range(size):
                total = add(slot, total)
        else:
            total = lax.fori_loop(0, size, add, total)
        total_ref[block] = total
        stores.append(pltpu.make_async_copy(total_ref.at[block], total_out.at[block], semaphores.at[block]))
        stores[-1].start()
    for store in stores:
        store.wait()


def shards(propagator, tile_blocks, histories):
    size = lax.axis_size("tm")
    own_blocks, tracer_count, source_width = histories.shape
    slot_count, source_width, months, cell_count = propagator.shape
    block_count = size * own_blocks
    height = tracer_count * months
    tile_height = source_width * months

    used_rows = tracer_count * own_blocks
    padded_shape = (used_rows + -used_rows % 16, source_width + -source_width % 128)
    packed_rows = tracer_count + -tracer_count % 16
    packed_width = own_blocks * source_width + -(own_blocks * source_width) % 128
    rows, blocks, tiles = (
        pltpu.with_memory_space_constraint(value, pltpu.HBM)
        for value in (
            jnp.swapaxes(histories, 0, 1).reshape(used_rows, source_width),
            tile_blocks.T,
            propagator.reshape(slot_count, tile_height, cell_count),
        )
    )
    vmem = pl.BlockSpec(memory_space=pltpu.VMEM)
    hbm = pl.BlockSpec(memory_space=pltpu.HBM)
    copies, sorted_tiles, pick, columns, same = pl.pallas_call(
        lambda *refs: prepare(months, *refs),
        out_shape=[
            jax.ShapeDtypeStruct((size, packed_rows, packed_width), rows.dtype),
            jax.ShapeDtypeStruct((block_count + block_count // 2, tile_height, cell_count), tiles.dtype),
            jax.ShapeDtypeStruct((SOURCES * height, size * packed_rows), jnp.bfloat16),
            jax.ShapeDtypeStruct((SOURCES, packed_width, tile_height), jnp.bfloat16),
            jax.ShapeDtypeStruct((height, tile_height), jnp.float32),
        ],
        in_specs=[hbm] * 3,
        out_specs=[vmem] * 5,
        scratch_shapes=[
            pltpu.VMEM(rows.shape, rows.dtype),
            pltpu.VMEM(padded_shape, rows.dtype),
            pltpu.SMEM(blocks.shape, blocks.dtype),
            pltpu.VMEM(tiles.shape, tiles.dtype),
            pltpu.SemaphoreType.DMA((4,)),
        ],
        compiler_params=pltpu.CompilerParams(vmem_limit_bytes=24 * 1024 * 1024),
        cost_estimate=pl.CostEstimate(flops=0, bytes_accessed=tiles.size * 4, transcendentals=0),
    )(rows, blocks, tiles)

    received = exchange(copies, history_order(size))

    coded = pl.pallas_call(
        tile_sums,
        out_shape=jax.ShapeDtypeStruct((size, own_blocks * height + SCALE_ROWS, cell_count), jnp.int16),
        in_specs=[vmem] * 5,
        out_specs=vmem,
        compiler_params=pltpu.CompilerParams(vmem_limit_bytes=20 * 1024 * 1024),
        cost_estimate=pl.CostEstimate(
            flops=2 * slot_count * height * tile_height * cell_count,
            bytes_accessed=propagator.size * 4,
            transcendentals=0,
        ),
    )(received, pick, columns, same, sorted_tiles)

    owned = pl.pallas_call(
        add_parts,
        out_shape=jax.ShapeDtypeStruct((own_blocks, height, cell_count), jnp.float32),
        in_specs=[vmem],
        out_specs=hbm,
        scratch_shapes=[
            pltpu.VMEM((own_blocks, height, cell_count), jnp.float32),
            pltpu.SemaphoreType.DMA((own_blocks,)),
        ],
        compiler_params=pltpu.CompilerParams(vmem_limit_bytes=16 * 1024 * 1024),
    )(exchange(coded, [sums_device(slot, size) for slot in range(size)]))
    return owned.reshape(own_blocks, tracer_count, months, cell_count)


def solution(mesh):
    in_specs = (
        P(("groups", "tm"), None, None, "cells"),
        P(("groups", "tm"), None),
        P("tm", None, None),
    )
    out_specs = P(("groups", "tm"), None, None, "cells")
    return jax.shard_map(shards, mesh=mesh, in_specs=in_specs, out_specs=out_specs, check_vma=False)
```
